32 devices in a mesh: seq: 2 (over x), exp: 8 (over z, y), dp: 2 (over core).
Axes of the slice: x: 2, y: 2, z: 4, core: 2. Of those that a mesh axis runs over, the one named last changes fastest.
Arguments:
- tokens: bfloat16 [2, 16, 768, 768], P(None, ('exp', 'dp'), 'seq'), may hold values from -6 to 6
- first_gain: bfloat16 [768], P('dp'), may hold values from 0.5 to 1.5
- first_shift: bfloat16 [768], P('dp'), may hold values from -1.5 to 1.5
- attention_in: bfloat16 [768, 2304], P('dp'), may hold values from -0.21875 to 0.21875
- attention_out: bfloat16 [768, 768], P('dp'), may hold values from -1.75 to 1.75
- second_gain: bfloat16 [768], P('dp'), may hold values from 0.5 to 1.5
- second_shift: bfloat16 [768], P('dp'), may hold values from -1.5 to 1.5
- router_weight: bfloat16 [768, 8], P('dp'), may hold values from -0.15625 to 0.15625
- up_weight: bfloat16 [8, 768, 3072], P('exp', 'dp'), may hold values from -0.21875 to 0.21875
- down_weight: bfloat16 [8, 3072, 768], P('exp', 'dp'), may hold values from -0.15625 to 0.15625
- routes: int32 [2, 16, 768, 2], P(None, ('exp', 'dp'), 'seq'), may hold values from 0 to 7, all different within a row
- priority: int32 [2, 16, 768], P(None, ('exp', 'dp'), 'seq'), may hold values from 0 to 1048575
- lengths: int32 [2, 16, 4], P(None, ('exp', 'dp')), may hold values from 0 to 576, as said below
- out_cotangent: bfloat16 [2, 16, 768, 768], P(None, ('exp', 'dp'), 'seq'), may hold values from -6 to 6
Outputs:
- mixed: bfloat16 [2, 16, 768, 768], P(None, ('exp', 'dp'), 'seq')
- tokens_grad: bfloat16 [2, 16, 768, 768], P(None, ('exp', 'dp'), 'seq')
- first_gain_grad: float32 [768], P('dp')
- first_shift_grad: float32 [768], P('dp')
- attention_in_grad: float32 [768, 2304], P('dp')
- attention_out_grad: float32 [768, 768], P('dp')
- second_gain_grad: float32 [768], P('dp')
- second_shift_grad: float32 [768], P('dp')
- router_weight_grad: float32 [768, 8], P('dp')
- up_weight_grad: float32 [8, 768, 3072], P('exp', 'dp')
- down_weight_grad: float32 [8, 3072, 768], P('exp', 'dp')
The draws below stay inside these ranges and needn't reach their ends.
Inputs may be any that keep to these rules, and one draw needn't show every extreme that they name: `routes`: each patch names two different experts. Each sequence is grouped by resolution: either one image of 576 patches followed by a padding document of 192 patches and two empty entries, or three images of 196 patches followed by a padding document of 180 patches; padding rows form a document of their own; the 4 lengths of one sequence sum to 768.
All inputs are finite; a program needn't handle non-finite values.
Results may differ from the reference program's by a relative error of at most 0.015.
Values may be sent and summed in bfloat16 or wider, within the bound.
A program may use at most 256 MiB of HBM per device.

```python
import jax
import jax.numpy as jnp
from jax import lax

D = 768
HEADS = 12
HEAD_DIM = 64
FF = 3072
TOK_DEV = 384
MB = 2
SEQLEN = 768
MOST = 576
SHORT = 196
GROUPS = 16
EXPERTS = 8
CAP = 101
N_SEQ = 2


def draw_lengths(key, part):
    key = jax.random.fold_in(key, 5)
    ticket = jax.random.randint(key, (MB, GROUPS), 0, 81)
    first_group = jnp.arange(GROUPS, dtype=jnp.int32)[None, :] == 0
    larger = (ticket < 32) | first_group
    long_row = jnp.array([MOST, SEQLEN - MOST, 0, 0], dtype=jnp.int32)
    short_row = jnp.array([SHORT, SHORT, SHORT, SEQLEN - 3 * SHORT], dtype=jnp.int32)
    return jnp.where(larger[..., None], long_row[None, None, :], short_row[None, None, :]).astype(jnp.int32)


def place_ends(result, stream_key, low, high):
    spot = [jax.random.randint(jax.random.fold_in(stream_key, axis), (), 0, length) for axis, length in enumerate(result.shape)]
    longest = result.shape.index(max(result.shape))
    next_to = spot[:longest] + [(spot[longest] + 1) % result.shape[longest]] + spot[longest + 1:]
    return result.at[tuple(spot)].set(low).at[tuple(next_to)].set(high)


def block_scale(stream_key, dims, shards, low, largest):
    factor_of = 1.0
    for dim, shards_of in shards:
        draws = jax.random.uniform(jax.random.fold_in(jax.random.fold_in(stream_key, 6), dim), (shards_of,), jnp.float32, low / len(shards), largest / len(shards))
        factor_of = factor_of * jnp.repeat(jnp.exp(draws), dims[dim] // shards_of).reshape((-1,) + (1,) * (len(dims) - 1 - dim))
    return factor_of


def picks_of(key, rows, amount, top, lift):
    order = jax.random.permutation(jax.random.fold_in(key, 1), amount)
    boost = order
    for power in range(3):
        boost = boost * boost // amount
    boost = boost * lift // amount
    tickets = jax.random.randint(jax.random.fold_in(key, 2), (rows, amount), 0, 4096) + boost
    fixed_rows = jax.random.permutation(jax.random.fold_in(key, 3), rows)[jnp.arange(amount) % rows]
    tickets = jnp.where(jnp.arange(rows)[:, None] == fixed_rows[None, :], 1 << 14, tickets)
    score = tickets * amount + jnp.arange(amount)
    return lax.top_k(score.astype(jnp.int32), top)[1].astype(jnp.int32)


def gaussian(key, shape, deviation, limit, split=(), kind=jnp.bfloat16):
    entries = jax.random.normal(key, shape, jnp.float32) * deviation
    if len(split) > 0:
        entries = block_scale(key, shape, split, -0.22, 0.18) * entries
    return jnp.clip(entries, min=-limit, max=limit).astype(kind)


def setup_inputs(seed: int = 0) -> dict:
    splits = jax.random.split(jax.random.key(seed), 15)
    return {
        "tokens": gaussian(splits[0], (MB, GROUPS, SEQLEN, D), 1.0, 6.0, ((1, 16), (2, 2))),
        "first_gain": jnp.clip(1.0 + 0.1 * jax.random.normal(splits[1], (D,), jnp.float32), 0.5, 1.5).astype(jnp.bfloat16),
        "first_shift": gaussian(splits[2], (D,), 0.3, 1.5, ((0, 2),)),
        "attention_in": gaussian(splits[3], (D, 3 * D), D ** -0.5, 0.21875, ((0, 2),)),
        "attention_out": gaussian(splits[4], (D, D), (D // 64) ** -0.5, 1.75, ((0, 2),)),
        "second_gain": jnp.clip(1.0 + 0.1 * jax.random.normal(splits[5], (D,), jnp.float32), 0.5, 1.5).astype(jnp.bfloat16),
        "second_shift": gaussian(splits[6], (D,), 0.3, 1.5, ((0, 2),)),
        "router_weight": gaussian(splits[7], (D, EXPERTS), (2 * D) ** -0.5, 0.15625, ((0, 2),)),
        "up_weight": gaussian(splits[8], (EXPERTS, D, FF), D ** -0.5, 0.21875, ((0, 8), (1, 2))),
        "down_weight": gaussian(splits[9], (EXPERTS, FF, D), (FF // 2) ** -0.5, 0.15625, ((0, 8), (1, 2))),
        "routes": picks_of(splits[10], MB * GROUPS * SEQLEN, EXPERTS, 2, 2048).reshape((MB, GROUPS, SEQLEN, 2)),
        "priority": place_ends(jax.random.randint(splits[11], (MB, GROUPS, SEQLEN), 0, 1048576), jax.random.fold_in(splits[11], 1), 0, 1048575).astype(jnp.int32),
        "lengths": draw_lengths(jax.random.fold_in(splits[14], 71), 0),
        "out_cotangent": gaussian(splits[13], (MB, GROUPS, SEQLEN, D), 1.0, 6.0, ((1, 16), (2, 2))),
    }


@jax.custom_vjp
def low(v):
    return lax.optimization_barrier(v.astype(jnp.bfloat16)).astype(jnp.float32)

@jax.custom_vjp
def low_back(v):
    return v

def low_keep(v):
    return (low(v), None)

def low_pass(kept, grad):
    return (grad,)

def back_keep(v):
    return (v, None)

def back_low(kept, grad):
    return (low(grad),)
low.defvjp(low_keep, low_pass)
low_back.defvjp(back_keep, back_low)
EPSILON = 1e-06
HIGHEST = lax.Precision.HIGHEST

def layer_norm(values, gain, shift):
    centre = values - lax.optimization_barrier(jnp.mean(values, axis=-1, keepdims=True))
    spread = lax.optimization_barrier(jnp.mean(centre * centre, axis=-1, keepdims=True))
    return centre * lax.rsqrt(spread + EPSILON) * gain + shift

def doc_ids(length_row, total):
    bounds = jnp.cumsum(length_row).astype(jnp.int32)
    places = jnp.arange(total, dtype=jnp.int32)
    return lax.optimization_barrier(jnp.sum((places[:, None] >= bounds[None, :]).astype(jnp.int32), axis=1)).astype(jnp.int32)

def assign(route_block, level_block, experts, capacity):
    count = route_block.shape[0] * 2
    wanted = route_block.reshape(-1).astype(jnp.int32)
    places = jnp.arange(count, dtype=jnp.int32)
    order_k = places % 2
    owner = places // 2
    level = jnp.repeat(level_block, 2)
    ahead = (order_k[None, :] < order_k[:, None]) | (order_k[None, :] == order_k[:, None]) & ((level[None, :] > level[:, None]) | (level[None, :] == level[:, None]) & (owner[None, :] < owner[:, None]))
    queue = lax.optimization_barrier(jnp.sum((ahead & (wanted[None, :] == wanted[:, None])).astype(jnp.int32), axis=1)).astype(jnp.int32)
    kept = queue < capacity
    slot = jnp.where(kept, wanted * capacity + queue, 0).astype(jnp.int32)
    cells = jnp.arange(experts * capacity, dtype=jnp.int32)
    match = (slot[None, :] == cells[:, None]) & kept[None, :]
    source = lax.optimization_barrier(jnp.sum(jnp.where(match, owner[None, :], 0), axis=1)).astype(jnp.int32)
    picked = lax.optimization_barrier(jnp.sum(jnp.where(match, places[None, :], 0), axis=1)).astype(jnp.int32)
    filled = jnp.any(match, axis=1)
    return (slot, kept, source, picked, filled)

def attend(packed, documents):
    length = packed.shape[0]
    query = packed[:, :D].reshape(length, HEADS, HEAD_DIM)
    keys = packed[:, D:2 * D].reshape(length, HEADS, HEAD_DIM)
    values = packed[:, 2 * D:].reshape(length, HEADS, HEAD_DIM)
    scores = jnp.einsum('qhd,khd->hqk', query, keys, precision=HIGHEST) * HEAD_DIM ** (-0.5)
    scores = low_back(scores)
    visible = documents[:, None] == documents[None, :]
    scores = jnp.where(visible[None], scores, -1e+30)
    weighting = jax.nn.softmax(scores, axis=-1)
    return jnp.einsum('hqk,khd->qhd', low(weighting), values, precision=HIGHEST).reshape(length, D)

def attend_couple(couple):
    return jax.checkpoint(attend)(couple[0], couple[1])

def expert(rows_in, up_matrix, down_matrix):
    hidden = low_back(jnp.dot(rows_in, up_matrix, precision=HIGHEST))
    active = low(jax.nn.gelu(hidden, approximate=False))
    return jnp.dot(active, down_matrix, precision=HIGHEST)

def expert_triple(triple):
    return jax.checkpoint(expert)(triple[0], triple[1], triple[2])

def take_rows(table, where_from):
    return jnp.take(table, where_from, axis=0)

def forward(inputs, first_gain, first_shift, attention_in, attention_out, second_gain, second_shift, router_weight, up_weight, down_weight, routes, priority, lengths):
    groups = inputs.shape[0]
    blocks = groups * N_SEQ
    first_norm = low(layer_norm(inputs, first_gain, first_shift))
    packed = low(low_back(jnp.einsum('gsd,de->gse', first_norm, attention_in, precision=HIGHEST)))
    documents = jax.vmap(lambda length_row: doc_ids(length_row, SEQLEN))(lengths)
    attended = lax.map(attend_couple, (packed, documents))
    attended = low(low_back(attended))
    residual = inputs + low_back(jnp.einsum('gsd,de->gse', attended, attention_out, precision=HIGHEST))
    moe_input = low(layer_norm(residual, second_gain, second_shift)).reshape(blocks, TOK_DEV, D)
    logits = jnp.einsum('btd,de->bte', moe_input, router_weight, precision=HIGHEST)
    route_blocks = routes.reshape(blocks, TOK_DEV, 2)
    picks = (route_blocks[..., None] == jnp.arange(EXPERTS, dtype=jnp.int32)).astype(jnp.float32)
    chosen = lax.optimization_barrier(jnp.sum(picks * logits[:, :, None, :], axis=-1))
    gate = jax.nn.softmax(chosen, axis=-1)
    slot, kept, source, picked, filled = jax.vmap(lambda route_rows, level_rows: assign(route_rows, level_rows, EXPERTS, CAP))(route_blocks, priority.reshape(blocks, TOK_DEV))
    outgoing = jax.vmap(take_rows)(moe_input, source)
    outgoing = low_back(jnp.where(filled[..., None], outgoing, 0.0))
    per_expert = outgoing.reshape(blocks, EXPERTS, CAP, D).transpose(1, 0, 2, 3).reshape(EXPERTS, blocks * CAP, D)
    produced = lax.map(expert_triple, (per_expert, up_weight, down_weight))
    produced = produced.reshape(EXPERTS, blocks, CAP, D).transpose(1, 0, 2, 3).reshape(blocks, EXPERTS * CAP, D)
    produced = low(low_back(produced))
    gathered = jax.vmap(take_rows)(produced, slot)
    gathered = jnp.where(kept[..., None], gathered, 0.0).reshape(blocks, TOK_DEV, 2, D)
    mixed = residual.reshape(blocks, TOK_DEV, D) + lax.optimization_barrier(jnp.sum(gate[..., None] * gathered, axis=2))
    return mixed.reshape(groups, SEQLEN, D)

def reference(tokens, first_gain, first_shift, attention_in, attention_out, second_gain, second_shift, router_weight, up_weight, down_weight, routes, priority, lengths, out_cotangent):
    params = tuple((item.astype(jnp.float32) for item in (first_gain, first_shift, attention_in, attention_out, second_gain, second_shift, router_weight, up_weight, down_weight)))
    totals = [jnp.zeros(item.shape, jnp.float32) for item in params]
    mixed_parts = []
    grad_parts = []
    for micro in range(MB):

        def local_forward(inputs, *weights):
            return forward(inputs, *weights, routes[micro], priority[micro], lengths[micro])
        mixed_one, pull = jax.vjp(local_forward, tokens[micro].astype(jnp.float32), *params)
        pulled = pull(out_cotangent[micro].astype(jnp.float32))
        mixed_parts.append(mixed_one.astype(jnp.bfloat16))
        grad_parts.append(pulled[0].astype(jnp.bfloat16))
        totals = [total + item for total, item in zip(totals, pulled[1:])]
    return (jnp.stack(mixed_parts), jnp.stack(grad_parts), totals[0], totals[1], totals[2], totals[3], totals[4], totals[5], totals[6], totals[7], totals[8])
```

```python
from functools import partial

import jax
import jax.numpy as jnp
from jax import lax
from jax.experimental import pallas as pl
from jax.experimental.pallas import tpu as pltpu
from jax.sharding import PartitionSpec as P

HEADS = 12
EPSILON = 1e-06
F32 = jnp.float32
BF16 = jnp.bfloat16
VMEM = pl.BlockSpec(memory_space=pltpu.VMEM)
SMEM = pl.BlockSpec(memory_space=pltpu.SMEM)
ROUTER_ROW = 8


def mm(a, b):
    return lax.dot_general(a, b, (((1,), (0,)), ((), ())), preferred_element_type=F32)


def mm_nt(a, b):
    return lax.dot_general(a, b, (((1,), (1,)), ((), ())), preferred_element_type=F32)


def mm_tn(a, b):
    return lax.dot_general(a, b, (((0,), (0,)), ((), ())), preferred_element_type=F32)


def iota(shape, dim):
    return lax.broadcasted_iota(jnp.int32, shape, dim)


def row_of(column, size):
    return jnp.sum(jnp.where(iota((size, size), 0) == iota((size, size), 1), column, 0.0), axis=0, keepdims=True)


def column_of(row, size):
    return jnp.sum(jnp.where(iota((size, size), 0) == iota((size, size), 1), row, 0.0), axis=1, keepdims=True)


def normalise(values):
    centre = values - jnp.mean(values, axis=-1, keepdims=True)
    spread = jnp.mean(centre * centre, axis=-1, keepdims=True)
    scale = lax.rsqrt(spread + EPSILON)
    return centre * scale, scale


def norm_backward(grad, gain, xhat, scale):
    scaled = grad * gain
    along = jnp.mean(scaled * xhat, axis=-1, keepdims=True)
    return scale * (scaled - jnp.mean(scaled, axis=-1, keepdims=True) - xhat * along)


def assign_stage(routes, level, capacity, padded):
    rows = routes.shape[0]
    level_row = level.astype(F32)
    level_column = column_of(level_row, rows)
    me, other = iota((rows, rows), 0), iota((rows, rows), 1)
    ahead = (level_row > level_column) | ((level_row == level_column) & (other < me))
    lane = iota((rows, 128), 1)
    first, second = routes[:, 0:1], routes[:, 1:2]
    wants = jnp.where((lane == first) | (lane == second + 64), 1.0, 0.0)
    count = mm(jnp.where(ahead, 1.0, 0.0).astype(BF16), wants.astype(BF16))
    total = jnp.sum(wants, axis=0, keepdims=True)
    rank_one = jnp.sum(jnp.where(lane == first, count, 0.0), axis=1, keepdims=True)
    rank_two = jnp.sum(
        jnp.where(lane == second + 64, count, 0.0) + jnp.where(lane == second, total, 0.0),
        axis=1,
        keepdims=True,
    )
    slot_one = jnp.where(rank_one < capacity, first.astype(F32) * padded + rank_one, -1.0)
    slot_two = jnp.where(rank_two < capacity, second.astype(F32) * padded + rank_two, -1.0)
    return slot_one, slot_two


def batch_of(experts, padded):
    best = 1
    for count in range(1, experts + 1):
        if experts % count == 0 and count * padded <= 256 and (count * padded) % 16 == 0:
            best = count
    return best


def spread_stage(values, slot_one, slot_two, experts, padded, store, extra=None):
    rows, width = values.shape
    one, two = row_of(slot_one, rows).astype(jnp.int32), row_of(slot_two, rows).astype(jnp.int32)
    batch = batch_of(experts, padded)
    place = iota((batch * padded, rows), 0)
    for start in range(0, experts, batch):
        here = place + start * padded
        pick = jnp.where((here == one) | (here == two), 1.0, 0.0).astype(BF16)
        block = mm(pick, values).reshape(batch, padded, width)
        if extra is not None:
            parts = []
            for inner in range(batch):
                parts.append(extra(start + inner, block[inner]))
            block = jnp.stack(parts)
        store(start, batch, block.astype(BF16))


def with_rows(block, first_row, rows):
    place = iota(block.shape, 0)
    for step, row in enumerate(rows):
        wide = jnp.concatenate([row, jnp.zeros((1, block.shape[1] - row.shape[1]), F32)], axis=1)
        block = jnp.where(place == first_row + step, wide, block)
    return block


def pieces(value, count):
    parts = []
    for _ in range(count):
        part = value.astype(BF16).astype(F32)
        parts.append(part)
        value = value - part
    return parts


def dispatch_kernel(capacity, padded, routes_ref, level_ref, cot_ref, slots_ref, sent_ref):
    slot_one, slot_two = assign_stage(routes_ref[...], level_ref[...], capacity, padded)
    lane = iota(slots_ref.shape, 1)
    slots_ref[...] = jnp.where(lane == 0, slot_one, slot_two).astype(jnp.int32)

    def store(start, batch, block):
        sent_ref[start : start + batch] = block

    spread_stage(cot_ref[...], slot_one, slot_two, sent_ref.shape[0], padded, store)


def first_kernel(tokens_ref, pack_ref, weight_ref, query_ref, pairs_ref):
    width = tokens_ref.shape[1]
    pack = pack_ref[...].astype(F32)
    xhat, _ = normalise(tokens_ref[...].astype(F32))
    low = (xhat * pack[0:1] + pack[1:2]).astype(BF16)
    query_ref[...] = mm(low, weight_ref[:, 0:width]).astype(BF16)
    for part in range(2):
        pairs_ref[:, part * width : (part + 1) * width] = mm(
            low, weight_ref[:, (part + 1) * width : (part + 2) * width]
        ).astype(BF16)


def bias_stage(lengths_ref, rows, store):
    own_start = lax.axis_index("seq") * rows
    span = lax.axis_size("seq") * rows
    ends = []
    total = 0
    for step in range(lengths_ref.shape[0]):
        total = total + lengths_ref[step]
        ends.append(total)

    def documents(place):
        found = jnp.zeros(place.shape, jnp.int32)
        for end in ends:
            found = found + jnp.where(place >= end, 1, 0)
        return found

    asked = documents(iota((1, rows), 1) + own_start)
    for half in range(2):
        start = own_start if half == 0 else span - rows - own_start
        held = documents(iota((rows, 1), 0) + start)
        store(half, jnp.where(held == asked, 0.0, -1e30))


def attend_stage(query_ref, pair_refs, bias_ref, attended_ref, stats_ref):
    rows, width = query_ref.shape
    head_dim = width // HEADS
    couple = 2 * head_dim
    low_lane = iota((1, couple), 1) < head_dim

    def step(index, _):
        lanes = pl.ds(pl.multiple_of(index * couple, couple), couple)
        value_lanes = pl.ds(pl.multiple_of(width + index * couple, couple), couple)
        query = query_ref[:, lanes].astype(F32) * head_dim**-0.5
        keys = [ref[:, lanes] for ref in pair_refs]
        values = [ref[:, value_lanes].astype(F32).T.astype(BF16) for ref in pair_refs]
        outs = []
        for head in range(2):
            mine = jnp.where(low_lane == (head == 0), query, 0.0).astype(BF16)
            scores = [mm_nt(keys[half], mine) + bias_ref[half] for half in range(2)]
            peak = jnp.maximum(*[jnp.max(part, axis=0, keepdims=True) for part in scores])
            raised = [jnp.exp(part - peak) for part in scores]
            total = sum(jnp.sum(part, axis=0, keepdims=True) for part in raised)
            here = slice(head * head_dim, (head + 1) * head_dim)
            summed = sum(mm(values[half][here], raised[half].astype(BF16)) for half in range(2))
            outs.append(summed / total)
            stats_ref[pl.ds(index * 2 + head, 1), :] = peak + jnp.log(total)
        attended_ref[:, lanes] = jnp.concatenate(outs, axis=0).T.astype(BF16)
        return 0

    lax.fori_loop(0, HEADS // 2, step, 0)


def gates_of(logits, routes):
    lane = iota(logits.shape, 1)
    chosen = [
        jnp.sum(jnp.where(lane == routes[:, k : k + 1] + ROUTER_ROW, logits, 0.0), axis=1, keepdims=True)
        for k in range(2)
    ]
    peak = jnp.maximum(*chosen)
    raised = [jnp.exp(part - peak) for part in chosen]
    total = raised[0] + raised[1]
    return raised[0] / total, raised[1] / total


def second_kernel(
    capacity,
    padded,
    tokens_ref,
    pack_ref,
    query_ref,
    own_ref,
    other_ref,
    lengths_ref,
    out_weight_ref,
    routes_ref,
    slots_ref,
    residual_ref,
    moe_input_ref,
    attended_ref,
    stats_ref,
    gates_ref,
    sent_ref,
    bias_ref,
):
    rows, width = tokens_ref.shape

    def store_bias(half, block):
        bias_ref[half] = block

    bias_stage(lengths_ref, rows, store_bias)
    attend_stage(query_ref, (own_ref, other_ref), bias_ref, attended_ref, stats_ref)
    residual = tokens_ref[...].astype(F32) + mm(attended_ref[...], out_weight_ref[...])
    residual_ref[...] = residual
    pack = pack_ref[...]
    xhat, _ = normalise(residual)
    moe_input = (xhat * pack[2:3].astype(F32) + pack[3:4].astype(F32)).astype(BF16)
    moe_input_ref[...] = moe_input
    gates = gates_of(mm_nt(moe_input, pack), routes_ref[...])
    lane = iota(gates_ref.shape, 1)
    gates_ref[...] = jnp.where(lane == 0, gates[0], gates[1])
    slots = slots_ref[...]
    slot_cols = [slots[:, k : k + 1] for k in range(2)]
    place = iota((rows, 128), 1)

    def gate_rows(expert, block):
        row = jnp.sum(
            sum(
                jnp.where(slot_cols[k] - expert * padded == place, gates[k], 0.0)
                for k in range(2)
            ),
            axis=0,
            keepdims=True,
        )
        return with_rows(block, capacity, pieces(row, 2))

    def store(start, batch, block):
        sent_ref[start : start + batch] = block

    spread_stage(
        moe_input,
        slot_cols[0].astype(F32),
        slot_cols[1].astype(F32),
        sent_ref.shape[0],
        padded,
        store,
        gate_rows,
    )


def phi_terms(hidden):
    size = jnp.abs(hidden)
    bell = jnp.exp(hidden * hidden * -0.5)
    t = 1.0 / (1.0 + 0.23164188828 * size)
    tail = t * (
        0.127414796
        + t * (-0.142248368 + t * (0.7107068705 + t * (-0.7265760135 + t * 0.5307027145)))
    )
    tail = tail * bell
    return jnp.where(hidden >= 0, 1.0 - tail, tail), bell


def expert_kernel(
    capacity,
    padded,
    chunks,
    first,
    rows_ref,
    cot_ref,
    up_ref,
    down_ref,
    *refs,
):
    if first:
        back_ref, grads_ref, up_grad_ref, down_grad_ref, x, xt, g, y, dx = refs
    else:
        up_old_ref, down_old_ref, back_ref, grads_ref, up_grad_ref, down_grad_ref, x, xt, g, y, dx = refs
    experts, _, width = rows_ref.shape
    step = pl.program_id(0)
    batch = batch_of(experts, padded)
    flat = batch * padded

    @pl.when(step == 0)
    def _():
        for start in range(0, experts, batch):
            block = rows_ref[start : start + batch].astype(F32)
            cot = cot_ref[start : start + batch].astype(F32)
            x[start * padded : start * padded + flat, :] = block.reshape(flat, width).astype(BF16)
            scaled = []
            place = iota((padded, 128), 0)
            for inner in range(batch):
                gate_row = jnp.sum(
                    jnp.where(
                        (place == capacity) | (place == capacity + 1), block[inner][:, 0:128], 0.0
                    ),
                    axis=0,
                    keepdims=True,
                )
                gate = jnp.sum(
                    jnp.where(place == iota((padded, 128), 1), gate_row, 0.0), axis=1, keepdims=True
                )
                scaled.append(cot[inner] * gate)
            g[start * padded : start * padded + flat, :] = (
                jnp.stack(scaled).reshape(flat, width).astype(BF16)
            )
        xt[...] = x[...].T
        y[...] = jnp.zeros_like(y)
        dx[...] = jnp.zeros_like(dx)

    hidden = mm(x[...], up_ref[...])
    phi, bell = phi_terms(hidden)
    active = (hidden * phi).astype(BF16)
    y[...] += mm(active, down_ref[...])
    active_grad = mm_nt(g[...], down_ref[...])
    hidden_grad = (active_grad * (phi + hidden * bell * 0.3989422804)).astype(BF16)
    dx[...] += mm_nt(hidden_grad, up_ref[...])
    up_grad = mm(xt[...], hidden_grad)
    down_grad = mm_tn(active, g[...])
    if not first:
        up_grad = up_grad + up_old_ref[...]
        down_grad = down_grad + down_old_ref[...]
    up_grad_ref[...] = up_grad
    down_grad_ref[...] = down_grad

    @pl.when(step == chunks - 1)
    def _():
        for start in range(0, experts, batch):
            here = slice(start * padded, start * padded + flat)
            produced = y[here, :].reshape(batch, padded, width).astype(BF16)
            back_ref[start : start + batch] = produced
            cot = cot_ref[start : start + batch].astype(F32)
            along = jnp.sum(cot * produced.astype(F32), axis=-1, keepdims=True)
            grads = dx[here, :].reshape(batch, padded, width)
            place, lane = iota((padded, 128), 0), iota((padded, 128), 1)
            parts = []
            for inner in range(batch):
                row = jnp.sum(
                    jnp.where(place == lane, along[inner], 0.0), axis=0, keepdims=True
                )
                parts.append(with_rows(grads[inner], capacity, pieces(row, 3)))
            grads_ref[start : start + batch] = jnp.stack(parts).astype(BF16)


def gather_stage(blocks_ref, slots, weights, padded):
    experts, _, width = blocks_ref.shape
    rows = slots.shape[0]
    batch = batch_of(experts, padded)
    place = iota((rows, batch * padded), 1)
    totals = [jnp.zeros((rows, width), F32) for _ in weights]
    for start in range(0, experts, batch):
        block = (
            blocks_ref[start : start + batch].astype(F32).reshape(batch * padded, width).astype(BF16)
        )
        here = place + start * padded
        for index, chosen in enumerate(weights):
            hit = slots[:, chosen[0] : chosen[0] + 1] == here
            for k in chosen[1:]:
                hit = hit | (slots[:, k : k + 1] == here)
            totals[index] = totals[index] + mm(jnp.where(hit, 1.0, 0.0).astype(BF16), block)
    return totals


def mix_kernel(padded, back_ref, slots_ref, gates_ref, residual_ref, mixed_ref):
    gates = gates_ref[...]
    one, two = gather_stage(back_ref, slots_ref[...], ((0,), (1,)), padded)
    mixed_ref[...] = (
        residual_ref[...] + (gates[:, 0:1] * one + gates[:, 1:2] * two)
    ).astype(BF16)


def third_kernel(
    capacity,
    padded,
    grads_ref,
    slots_ref,
    gates_ref,
    routes_ref,
    cot_ref,
    residual_ref,
    moe_input_ref,
    attended_ref,
    stats_ref,
    query_ref,
    own_ref,
    other_ref,
    lengths_ref,
    pack_ref,
    out_weight_ref,
    residual_grad_ref,
    query_grad_ref,
    own_grad_ref,
    other_grad_ref,
    out_grad_ref,
    small_ref,
    bias_ref,
    attended_grad_ref,
    delta_ref,
):
    rows, width = residual_ref.shape
    head_dim = width // HEADS
    couple = 2 * head_dim
    experts = grads_ref.shape[0]
    pack = pack_ref[...]
    slots, gates, routes = slots_ref[...], gates_ref[...], routes_ref[...]

    def store_bias(half, block):
        bias_ref[half] = block

    bias_stage(lengths_ref, rows, store_bias)
    (moe_grad,) = gather_stage(grads_ref, slots, ((0, 1),), padded)
    place, lane = iota((padded, 128), 0), iota((rows, 128), 1)
    found = [jnp.zeros((rows, 128), F32) for _ in range(2)]
    for expert in range(experts):
        tail = grads_ref[expert][:, 0:128].astype(F32)
        inside = (place >= capacity) & (place < capacity + 3)
        row = jnp.sum(jnp.where(inside, tail, 0.0), axis=0, keepdims=True)
        for k in range(2):
            found[k] = found[k] + jnp.where(
                slots[:, k : k + 1] - expert * padded == lane, row, 0.0
            )
    gate_grad = [jnp.sum(part, axis=1, keepdims=True) for part in found]
    gate = [gates[:, k : k + 1] for k in range(2)]
    inner = gate[0] * gate_grad[0] + gate[1] * gate_grad[1]
    pack_lane = iota((rows, pack.shape[0]), 1)
    logit_grad = sum(
        jnp.where(
            pack_lane == routes[:, k : k + 1] + ROUTER_ROW, gate[k] * (gate_grad[k] - inner), 0.0
        )
        for k in range(2)
    )
    parts = [part.astype(BF16) for part in pieces(logit_grad, 3)]
    moe_input = moe_input_ref[...]
    moe_grad = moe_grad + sum(mm(part, pack) for part in parts)
    router_grad = sum(mm_tn(part, moe_input) for part in parts)
    upstream = cot_ref[...].astype(F32)
    xhat, scale = normalise(residual_ref[...])
    gain_grad = jnp.sum(moe_grad * xhat, axis=0, keepdims=True)
    shift_grad = jnp.sum(moe_grad, axis=0, keepdims=True)
    small_row = iota(small_ref.shape, 0)
    small_ref[...] = jnp.where(
        small_row == 2, gain_grad, jnp.where(small_row == 3, shift_grad, router_grad)
    )
    residual_grad = upstream + norm_backward(moe_grad, pack[2:3].astype(F32), xhat, scale)
    residual_grad_ref[...] = residual_grad
    branch = residual_grad.astype(BF16)
    out_grad_ref[...] = mm_tn(attended_ref[...], branch)
    attended_grad_ref[...] = mm_nt(branch, out_weight_ref[...]).astype(BF16)
    low_lane = iota((1, couple), 1) < head_dim
    pair_refs = (own_ref, other_ref)
    out_refs = (own_grad_ref, other_grad_ref)

    def step(index, _):
        lanes = pl.ds(pl.multiple_of(index * couple, couple), couple)
        value_lanes = pl.ds(pl.multiple_of(width + index * couple, couple), couple)
        query = query_ref[:, lanes].astype(F32) * head_dim**-0.5
        grad = attended_grad_ref[:, lanes].astype(F32)
        query_low, grad_low = query.astype(BF16), grad.astype(BF16)
        keys = [ref[:, lanes] for ref in pair_refs]
        values = [ref[:, value_lanes] for ref in pair_refs]
        keys_turned = [part.astype(F32).T.astype(BF16) for part in keys]
        key_grads = [[], []]
        value_grads = [[], []]
        query_grads = []
        for head in range(2):
            chosen = low_lane == (head == 0)
            mine = jnp.where(chosen, query, 0.0).astype(BF16)
            mine_grad = jnp.where(chosen, grad, 0.0).astype(BF16)
            stats = stats_ref[pl.ds(index * 2 + head, 1), :]
            weighting = [
                jnp.exp(mm_nt(keys[half], mine) + bias_ref[half] - stats) for half in range(2)
            ]
            weighting_grad = [mm_nt(values[half], mine_grad) for half in range(2)]
            delta = sum(
                jnp.sum(weighting[half] * weighting_grad[half], axis=0, keepdims=True)
                for half in range(2)
            )
            here = slice(head * head_dim, (head + 1) * head_dim)
            query_total = 0.0
            for half in range(2):
                scores_grad = (weighting[half] * (weighting_grad[half] - delta)).astype(BF16)
                value_grads[half].append(mm(weighting[half].astype(BF16), grad_low))
                key_grads[half].append(mm(scores_grad, query_low))
                query_total = query_total + mm(keys_turned[half][here], scores_grad)
            query_grads.append(query_total * head_dim**-0.5)
        query_grad_ref[:, lanes] = jnp.concatenate(query_grads, axis=0).T.astype(BF16)
        for half in range(2):
            out_refs[half][:, lanes] = jnp.where(low_lane, *key_grads[half]).astype(
                out_refs[half].dtype
            )
            out_refs[half][:, value_lanes] = jnp.where(low_lane, *value_grads[half]).astype(
                out_refs[half].dtype
            )
        return 0

    lax.fori_loop(0, HEADS // 2, step, 0)


def fourth_kernel(
    tokens_ref,
    pack_ref,
    weight_ref,
    residual_grad_ref,
    query_grad_ref,
    own_grad_ref,
    arrived_grad_ref,
    small_in_ref,
    tokens_grad_ref,
    in_grad_ref,
    small_ref,
    packed_grad,
):
    width = tokens_ref.shape[1]
    pack = pack_ref[...].astype(F32)
    xhat, scale = normalise(tokens_ref[...].astype(F32))
    low = (xhat * pack[0:1] + pack[1:2]).astype(BF16)
    packed_grad[:, 0:width] = query_grad_ref[...]
    packed_grad[:, width:] = (own_grad_ref[...] + arrived_grad_ref[...].astype(F32)).astype(BF16)
    for part in range(3):
        here = slice(part * width, (part + 1) * width)
        in_grad_ref[:, here] = mm_tn(low, packed_grad[:, here])
    first_grad = sum(
        mm_nt(
            packed_grad[:, part * width : (part + 1) * width],
            weight_ref[:, part * width : (part + 1) * width],
        )
        for part in range(3)
    )
    tokens_grad_ref[...] = (
        residual_grad_ref[...] + norm_backward(first_grad, pack[0:1], xhat, scale)
    ).astype(BF16)
    small_row = iota(small_ref.shape, 0)
    small_ref[...] = jnp.where(
        small_row == 0,
        jnp.sum(first_grad * xhat, axis=0, keepdims=True),
        jnp.where(small_row == 1, jnp.sum(first_grad, axis=0, keepdims=True), small_in_ref[...]),
    )


def shape(dims, dtype):
    return jax.ShapeDtypeStruct(dims, dtype)


def call(kernel, outs, specs, scratch=(), name=None, flops=10**9):
    return pl.pallas_call(
        kernel,
        out_shape=outs,
        in_specs=specs,
        out_specs=tuple(VMEM for _ in outs),
        scratch_shapes=scratch,
        compiler_params=pltpu.CompilerParams(vmem_limit_bytes=56 * 2**20),
        cost_estimate=pl.CostEstimate(flops=flops, bytes_accessed=10**7, transcendentals=0),
        name=name,
    )


def body(
    tokens,
    first_gain,
    first_shift,
    attention_in,
    attention_out,
    second_gain,
    second_shift,
    router_weight,
    up_weight,
    down_weight,
    routes,
    priority,
    lengths,
    out_cotangent,
):
    micro_count, _, rows, width = tokens.shape
    experts = lax.axis_size("exp") * up_weight.shape[0]
    hidden_width = up_weight.shape[2]
    capacity = (210 * rows + 100 * experts - 1) // (100 * experts)
    padded = (capacity + 3 + 7) // 8 * 8
    slots_all = experts * padded
    core = lax.axis_index("dp")
    half_seq = lax.axis_index("seq")

    def swap(value, axis):
        return lax.ppermute(value, axis, [(0, 1), (1, 0)])

    def whole(value, axis):
        got = swap(value, "dp")
        return jnp.where(
            core == 0,
            jnp.concatenate([value, got], axis=axis),
            jnp.concatenate([got, value], axis=axis),
        )

    pack_rows = (ROUTER_ROW + experts + 15) // 16 * 16
    norms = jnp.stack([first_gain, first_shift, second_gain, second_shift])
    pack = jnp.concatenate(
        [
            norms,
            jnp.zeros((ROUTER_ROW - 4, norms.shape[1]), BF16),
            router_weight.T,
            jnp.zeros((pack_rows - ROUTER_ROW - experts, norms.shape[1]), BF16),
        ]
    )
    pack = whole(pack, 1)
    in_full = whole(attention_in, 0)
    out_full = whole(attention_out, 0)
    up_full = whole(up_weight[0], 0)
    down_full = whole(down_weight[0], 0)

    block = (experts, padded, width)

    def exchange(value):
        return lax.all_to_all(value, "exp", split_axis=0, concat_axis=0, tiled=True)

    slots, cots, queries, pairs, got_pairs = [], [], [], [], []
    for m in range(micro_count):
        slot, sent = call(
            partial(dispatch_kernel, capacity, padded),
            (shape((rows, 2), jnp.int32), shape(block, BF16)),
            [VMEM] * 3,
            name="claim_slots",
        )(routes[m, 0], priority[m], out_cotangent[m, 0])
        slots.append(slot)
        cots.append(exchange(sent))
        query, pair = call(
            first_kernel,
            (shape((rows, width), BF16), shape((rows, 2 * width), BF16)),
            [VMEM] * 3,
            name="project_in",
        )(tokens[m, 0], pack, in_full)
        queries.append(query)
        pairs.append(pair)
        got_pairs.append(swap(pair, "seq"))
    residuals, moe_inputs, attendeds, statses, gateses, arrived = [], [], [], [], [], []
    for m in range(micro_count):
        residual, moe_input, attended, stats, gates, sent = call(
            partial(second_kernel, capacity, padded),
            (
                shape((rows, width), F32),
                shape((rows, width), BF16),
                shape((rows, width), BF16),
                shape((16, rows), F32),
                shape((rows, 2), F32),
                shape(block, BF16),
            ),
            [VMEM] * 5 + [SMEM] + [VMEM] * 3,
            (pltpu.VMEM((2, rows, rows), F32),),
            name="attend",
        )(
            tokens[m, 0],
            pack,
            queries[m],
            pairs[m],
            got_pairs[m],
            lengths[m, 0],
            out_full,
            routes[m, 0],
            slots[m],
        )
        residuals.append(residual)
        moe_inputs.append(moe_input)
        attendeds.append(attended)
        statses.append(stats)
        gateses.append(gates)
        arrived.append(exchange(sent))
    chunk = 256
    chunks = hidden_width // chunk
    up_sum = down_sum = None
    backs, grads = [], []
    whole_block = pl.BlockSpec(block, lambda i: (0, 0, 0))
    up_spec = pl.BlockSpec((width, chunk), lambda i: (0, i))
    down_spec = pl.BlockSpec((chunk, width), lambda i: (i, 0))
    for m in range(micro_count):
        old = () if m == 0 else (up_sum, down_sum)
        back, grad, up_sum, down_sum = pl.pallas_call(
            partial(expert_kernel, capacity, padded, chunks, m == 0),
            out_shape=(
                shape(block, BF16),
                shape(block, BF16),
                shape((width, hidden_width), F32),
                shape((hidden_width, width), F32),
            ),
            grid=(chunks,),
            in_specs=[whole_block, whole_block, up_spec, down_spec]
            + ([] if m == 0 else [up_spec, down_spec]),
            out_specs=(whole_block, whole_block, up_spec, down_spec),
            scratch_shapes=[
                pltpu.VMEM((slots_all, width), BF16),
                pltpu.VMEM((width, slots_all), BF16),
                pltpu.VMEM((slots_all, width), BF16),
                pltpu.VMEM((slots_all, width), F32),
                pltpu.VMEM((slots_all, width), F32),
            ],
            compiler_params=pltpu.CompilerParams(vmem_limit_bytes=56 * 2**20),
            cost_estimate=pl.CostEstimate(
                flops=12 * slots_all * width * hidden_width,
                bytes_accessed=10**7,
                transcendentals=0,
            ),
            name="expert",
        )(arrived[m], cots[m], up_full, down_full, *old)
        backs.append(exchange(back))
        grads.append(exchange(grad))
    mixed_parts, token_grads = [], []
    in_sum = out_sum = small_sum = 0.0
    for m in range(micro_count):
        residual_grad, query_grad, own_grad, other_grad, out_grad, small = call(
            partial(third_kernel, capacity, padded),
            (
                shape((rows, width), F32),
                shape((rows, width), BF16),
                shape((rows, 2 * width), F32),
                shape((rows, 2 * width), BF16),
                shape((width, width), F32),
                shape((pack_rows, width), F32),
            ),
            [VMEM] * 12 + [SMEM] + [VMEM] * 2,
            (
                pltpu.VMEM((2, rows, rows), F32),
                pltpu.VMEM((rows, width), BF16),
                pltpu.VMEM((16, rows), F32),
            ),
            name="attend_back",
        )(
            grads[m],
            slots[m],
            gateses[m],
            routes[m, 0],
            out_cotangent[m, 0],
            residuals[m],
            moe_inputs[m],
            attendeds[m],
            statses[m],
            queries[m],
            pairs[m],
            got_pairs[m],
            lengths[m, 0],
            pack,
            out_full,
        )
        got_grad = swap(other_grad, "seq")
        (mixed,) = call(
            partial(mix_kernel, padded), (shape((rows, width), BF16),), [VMEM] * 4, name="mix"
        )(backs[m], slots[m], gateses[m], residuals[m])
        mixed_parts.append(mixed)
        tokens_grad, in_grad, small = call(
            fourth_kernel,
            (
                shape((rows, width), BF16),
                shape((width, 3 * width), F32),
                shape((pack_rows, width), F32),
            ),
            [VMEM] * 8,
            (pltpu.VMEM((rows, 3 * width), BF16),),
            name="project_back",
        )(
            tokens[m, 0],
            pack,
            in_full,
            residual_grad,
            query_grad,
            own_grad,
            got_grad,
            small,
        )
        token_grads.append(tokens_grad)
        in_sum = in_sum + in_grad
        out_sum = out_sum + out_grad
        small_sum = small_sum + small

    def halves(value, axis):
        size = value.shape[axis] // 2
        mine = lax.dynamic_slice_in_dim(value, core * size, size, axis)
        theirs = lax.dynamic_slice_in_dim(value, (1 - core) * size, size, axis)
        return mine + swap(theirs.astype(BF16), "dp").astype(F32)

    def pair_sum(value):
        low = value.astype(BF16)
        return low.astype(F32) + swap(low, "seq").astype(F32)

    up_total = pair_sum(halves(up_sum, 0))[None]
    down_total = pair_sum(halves(down_sum, 0))[None]
    dense = halves(jnp.concatenate([in_sum, out_sum], axis=1), 0).astype(BF16)
    dense = lax.psum(dense, ("seq", "exp")).astype(F32)
    small = halves(small_sum, 1)
    small = lax.psum(small, ("seq", "exp"))
    return (
        jnp.stack(mixed_parts)[:, None],
        jnp.stack(token_grads)[:, None],
        small[0],
        small[1],
        dense[:, : 3 * width],
        dense[:, 3 * width :],
        small[2],
        small[3],
        small[ROUTER_ROW : ROUTER_ROW + experts].T,
        up_total,
        down_total,
    )


def solution(mesh):
    placed = (
        P(None, ("exp", "dp"), "seq", None),
        P("dp"),
        P("dp"),
        P("dp", None),
        P("dp", None),
        P("dp"),
        P("dp"),
        P("dp", None),
        P("exp", "dp", None),
        P("exp", "dp", None),
        P(None, ("exp", "dp"), "seq", None),
        P(None, ("exp", "dp"), "seq"),
        P(None, ("exp", "dp"), None),
        P(None, ("exp", "dp"), "seq", None),
    )
    return jax.shard_map(
        body,
        mesh=mesh,
        in_specs=placed,
        out_specs=(
            P(None, ("exp", "dp"), "seq", None),
            P(None, ("exp", "dp"), "seq", None),
            P("dp"),
            P("dp"),
            P("dp", None),
            P("dp", None),
            P("dp"),
            P("dp"),
            P("dp", None),
            P("exp", "dp", None),
            P("exp", "dp", None),
        ),
        check_vma=False,
    )
```

```python
from functools import partial

import jax
import jax.numpy as jnp
from jax import lax
from jax.experimental import pallas as pl
from jax.experimental.pallas import tpu as pltpu
from jax.sharding import PartitionSpec as P

HEADS = 12
EPSILON = 1e-06
F32 = jnp.float32
BF16 = jnp.bfloat16
VMEM = pl.BlockSpec(memory_space=pltpu.VMEM)
SMEM = pl.BlockSpec(memory_space=pltpu.SMEM)
ROUTER_ROW = 8


def mm(a, b):
    return lax.dot_general(a, b, (((1,), (0,)), ((), ())), preferred_element_type=F32)


def mm_nt(a, b):
    return lax.dot_general(a, b, (((1,), (1,)), ((), ())), preferred_element_type=F32)


def mm_tn(a, b):
    return lax.dot_general(a, b, (((0,), (0,)), ((), ())), preferred_element_type=F32)


def iota(shape, dim):
    return lax.broadcasted_iota(jnp.int32, shape, dim)


def row_of(column, size):
    return jnp.sum(jnp.where(iota((size, size), 0) == iota((size, size), 1), column, 0.0), axis=0, keepdims=True)


def column_of(row, size):
    return jnp.sum(jnp.where(iota((size, size), 0) == iota((size, size), 1), row, 0.0), axis=1, keepdims=True)


def normalise(values):
    centre = values - jnp.mean(values, axis=-1, keepdims=True)
    spread = jnp.mean(centre * centre, axis=-1, keepdims=True)
    scale = lax.rsqrt(spread + EPSILON)
    return centre * scale, scale


def norm_backward(grad, gain, xhat, scale):
    scaled = grad * gain
    along = jnp.mean(scaled * xhat, axis=-1, keepdims=True)
    return scale * (scaled - jnp.mean(scaled, axis=-1, keepdims=True) - xhat * along)


def assign_stage(routes, level, capacity, padded):
    rows = routes.shape[0]
    level_row = level.astype(F32)
    level_column = column_of(level_row, rows)
    me, other = iota((rows, rows), 0), iota((rows, rows), 1)
    ahead = (level_row > level_column) | ((level_row == level_column) & (other < me))
    lane = iota((rows, 128), 1)
    first, second = routes[:, 0:1], routes[:, 1:2]
    wants = jnp.where((lane == first) | (lane == second + 64), 1.0, 0.0)
    count = mm(jnp.where(ahead, 1.0, 0.0).astype(BF16), wants.astype(BF16))
    total = jnp.sum(wants, axis=0, keepdims=True)
    rank_one = jnp.sum(jnp.where(lane == first, count, 0.0), axis=1, keepdims=True)
    rank_two = jnp.sum(
        jnp.where(lane == second + 64, count, 0.0) + jnp.where(lane == second, total, 0.0),
        axis=1,
        keepdims=True,
    )
    slot_one = jnp.where(rank_one < capacity, first.astype(F32) * padded + rank_one, -1.0)
    slot_two = jnp.where(rank_two < capacity, second.astype(F32) * padded + rank_two, -1.0)
    return slot_one, slot_two


def batch_of(experts, padded):
    best = 1
    for count in range(1, experts + 1):
        if experts % count == 0 and count * padded <= 256 and (count * padded) % 16 == 0:
            best = count
    return best


def spread_stage(values, slot_one, slot_two, experts, padded, store, extra=None):
    rows, width = values.shape
    one, two = row_of(slot_one, rows).astype(jnp.int32), row_of(slot_two, rows).astype(jnp.int32)
    batch = batch_of(experts, padded)
    place = iota((batch * padded, rows), 0)
    for start in range(0, experts, batch):
        here = place + start * padded
        pick = jnp.where((here == one) | (here == two), 1.0, 0.0).astype(BF16)
        block = mm(pick, values).reshape(batch, padded, width)
        if extra is not None:
            parts = []
            for inner in range(batch):
                parts.append(extra(start + inner, block[inner]))
            block = jnp.stack(parts)
        store(start, batch, block.astype(BF16))


def with_rows(block, first_row, rows):
    place = iota(block.shape, 0)
    for step, row in enumerate(rows):
        wide = jnp.concatenate([row, jnp.zeros((1, block.shape[1] - row.shape[1]), F32)], axis=1)
        block = jnp.where(place == first_row + step, wide, block)
    return block


def pieces(value, count):
    parts = []
    for _ in range(count):
        part = value.astype(BF16).astype(F32)
        parts.append(part)
        value = value - part
    return parts


def bias_stage(lengths_ref, m, rows, store):
    own_start = lax.axis_index("seq") * rows
    span = lax.axis_size("seq") * rows
    ends = []
    total = 0
    for step in range(lengths_ref.shape[1]):
        total = total + lengths_ref[m, step]
        ends.append(total)

    def documents(place):
        found = jnp.zeros(place.shape, jnp.int32)
        for end in ends:
            found = found + jnp.where(place >= end, 1, 0)
        return found

    asked = documents(iota((1, rows), 1) + own_start)
    for half in range(2):
        start = own_start if half == 0 else span - rows - own_start
        held = documents(iota((rows, 1), 0) + start)
        store(half, jnp.where(held == asked, 0.0, -1e30))


def gates_of(logits, routes):
    lane = iota(logits.shape, 1)
    chosen = [
        jnp.sum(jnp.where(lane == routes[:, k : k + 1] + ROUTER_ROW, logits, 0.0), axis=1, keepdims=True)
        for k in range(2)
    ]
    peak = jnp.maximum(*chosen)
    raised = [jnp.exp(part - peak) for part in chosen]
    total = raised[0] + raised[1]
    return raised[0] / total, raised[1] / total


def phi_terms(hidden):
    size = jnp.abs(hidden)
    bell = jnp.exp(hidden * hidden * -0.5)
    t = 1.0 / (1.0 + 0.23164188828 * size)
    tail = t * (
        0.127414796
        + t * (-0.142248368 + t * (0.7107068705 + t * (-0.7265760135 + t * 0.5307027145)))
    )
    tail = tail * bell
    return jnp.where(hidden >= 0, 1.0 - tail, tail), bell


def gather_stage(blocks_ref, slots, weights, padded):
    experts, _, width = blocks_ref.shape
    rows = slots.shape[0]
    batch = batch_of(experts, padded)
    place = iota((rows, batch * padded), 1)
    totals = [jnp.zeros((rows, width), F32) for _ in weights]
    for start in range(0, experts, batch):
        block = (
            blocks_ref[start : start + batch].astype(F32).reshape(batch * padded, width).astype(BF16)
        )
        here = place + start * padded
        for index, chosen in enumerate(weights):
            hit = slots[:, chosen[0] : chosen[0] + 1] == here
            for k in chosen[1:]:
                hit = hit | (slots[:, k : k + 1] == here)
            totals[index] = totals[index] + mm(jnp.where(hit, 1.0, 0.0).astype(BF16), block)
    return totals


def mix_kernel(padded, back_ref, slots_ref, gates_ref, residual_ref, mixed_ref):
    gates = gates_ref[...]
    one, two = gather_stage(back_ref, slots_ref[...], ((0,), (1,)), padded)
    mixed_ref[...] = (
        residual_ref[...] + (gates[:, 0:1] * one + gates[:, 1:2] * two)
    ).astype(BF16)


MESH = pl.DeviceIdType.MESH
ANY = pl.BlockSpec(memory_space=pl.ANY)
CHUNK = 256


def remote(source, target, sends, arrives, device):
    return pltpu.make_async_remote_copy(
        src_ref=source,
        dst_ref=target,
        send_sem=sends,
        recv_sem=arrives,
        device_id=device,
        device_id_type=MESH,
    )


def greet(axes):
    barrier = pltpu.get_barrier_semaphore()
    count = 0
    for axis in axes:
        size, me = lax.axis_size(axis), lax.axis_index(axis)
        for step in range(1, size):
            pl.semaphore_signal(
                barrier, inc=1, device_id={axis: lax.rem(me + step, size)}, device_id_type=MESH
            )
            count += 1
    pl.semaphore_wait(barrier, count)


class Exchange:
    def __init__(self, source, target, sems, index):
        self.refs, self.index = (source, target, sems), index

    def copies(self):
        source, target, sems = self.refs
        size, me = lax.axis_size("exp"), lax.axis_index("exp")
        found = []
        for step in range(1, size):
            peer = lax.rem(me + step, size)
            found.append(
                remote(
                    source.at[peer],
                    target.at[me],
                    sems.at[self.index, 0, step],
                    sems.at[self.index, 1, step],
                    {"exp": peer},
                )
            )
        return found

    def own(self):
        source, target, sems = self.refs
        me = lax.axis_index("exp")
        return pltpu.make_async_copy(source.at[me], target.at[me], sems.at[self.index, 0, 0])

    def start(self):
        for copy in self.copies():
            copy.start()
        self.own().start()

    def arrived(self):
        for copy in self.copies():
            copy.wait_recv()
        self.own().wait()

    def sent(self):
        for copy in self.copies():
            copy.wait_send()


def project(low, weight_ref, parts, store):
    width = low.shape[1]
    for part in parts:
        block = mm(low, weight_ref[:, part * width : (part + 1) * width]).astype(BF16)
        for index in range(width // 128):
            store(part, index, block[:, index * 128 : (index + 1) * 128])


def attend_stage(query_ref, pair_ref, bias_ref, attended_ref, stats_ref):
    couples, rows, couple = query_ref.shape
    head_dim = couple // 2
    low_lane = iota((1, couple), 1) < head_dim

    def step(index, _):
        query = query_ref[index].astype(F32) * head_dim**-0.5
        keys = [pair_ref[half, 2 * index] for half in range(2)]
        values = [pair_ref[half, 2 * index + 1].astype(F32).T.astype(BF16) for half in range(2)]
        outs = []
        for head in range(2):
            mine = jnp.where(low_lane == (head == 0), query, 0.0).astype(BF16)
            scores = [mm_nt(keys[half], mine) + bias_ref[half] for half in range(2)]
            peak = jnp.maximum(*[jnp.max(part, axis=0, keepdims=True) for part in scores])
            raised = [jnp.exp(part - peak) for part in scores]
            total = sum(jnp.sum(part, axis=0, keepdims=True) for part in raised)
            here = slice(head * head_dim, (head + 1) * head_dim)
            summed = sum(mm(values[half][here], raised[half].astype(BF16)) for half in range(2))
            outs.append(summed / total)
            stats_ref[pl.ds(index * 2 + head, 1), :] = peak + jnp.log(total)
        lanes = pl.ds(pl.multiple_of(index * couple, couple), couple)
        attended_ref[:, lanes] = jnp.concatenate(outs, axis=0).T.astype(BF16)
        return 0

    lax.fori_loop(0, couples, step, 0)


def flatten_stage(rows_ref, cot_ref, x, g, capacity):
    experts, padded, width = rows_ref.shape
    batch = batch_of(experts, padded)
    flat = batch * padded
    place, lane = iota((padded, 128), 0), iota((padded, 128), 1)
    for start in range(0, experts, batch):
        block = rows_ref[start : start + batch].astype(F32)
        cot = cot_ref[start : start + batch].astype(F32)
        here = slice(start * padded, start * padded + flat)
        x[here, :] = block.reshape(flat, width).astype(BF16)
        scaled = []
        for inner in range(batch):
            inside = (place == capacity) | (place == capacity + 1)
            gate_row = jnp.sum(jnp.where(inside, block[inner][:, 0:128], 0.0), axis=0, keepdims=True)
            gate = jnp.sum(jnp.where(place == lane, gate_row, 0.0), axis=1, keepdims=True)
            scaled.append(cot[inner] * gate)
        g[here, :] = jnp.stack(scaled).reshape(flat, width).astype(BF16)


def expert_step(x, g, y, dx, up, down):
    hidden = mm(x[...], up)
    active_grad = mm_nt(g[...], down)
    phi, bell = phi_terms(hidden)
    active = (hidden * phi).astype(BF16)
    hidden_grad = (active_grad * (phi + hidden * bell * 0.3989422804)).astype(BF16)
    y[...] += mm(active, down)
    dx[...] += mm_nt(hidden_grad, up)
    return mm_tn(x[...], hidden_grad), mm_tn(active, g[...])


def finish_stage(cot_ref, y, dx, back_ref, grads_ref, capacity):
    experts, padded, width = cot_ref.shape
    batch = batch_of(experts, padded)
    place, lane = iota((padded, 128), 0), iota((padded, 128), 1)
    for start in range(0, experts, batch):
        here = slice(start * padded, (start + batch) * padded)
        produced = y[here, :].reshape(batch, padded, width).astype(BF16)
        back_ref[start : start + batch] = produced
        cot = cot_ref[start : start + batch].astype(F32)
        along = jnp.sum(cot * produced.astype(F32), axis=-1, keepdims=True)
        grads = dx[here, :].reshape(batch, padded, width)
        parts = []
        for inner in range(batch):
            row = jnp.sum(jnp.where(place == lane, along[inner], 0.0), axis=0, keepdims=True)
            parts.append(with_rows(grads[inner], capacity, pieces(row, 3)))
        grads_ref[start : start + batch] = jnp.stack(parts).astype(BF16)


def forward_kernel(
    capacity,
    tokens_ref,
    cot_ref,
    routes_ref,
    priority_ref,
    lengths_ref,
    pack_own,
    in_own,
    out_own,
    up_own,
    down_own,
    pack_out,
    in_out,
    out_out,
    token_out,
    query_out,
    pair_out,
    residual_out,
    moe_out,
    attended_out,
    stats_out,
    gates_out,
    slots_out,
    back_out,
    grads_out,
    up_old,
    down_old,
    up_keep,
    down_keep,
    up_got,
    down_got,
    up_sum,
    down_sum,
    up_arrived,
    pk,
    wi,
    wo,
    up,
    down,
    token_other,
    cot_send,
    row_send,
    cot_got,
    row_got,
    all_sems,
    weight_sems,
    token_sems,
    out_sems,
    chunk_sems,
    past_sems,
    low_sems,
    got_sems,
    cross_sems,
):
    micro_count, rows, width = tokens_ref.shape
    experts, padded = cot_send.shape[1], cot_send.shape[2]
    flat = experts * padded
    core, half_seq = lax.axis_index("dp"), lax.axis_index("seq")
    partner = {"dp": 1 - core}
    across = {"seq": 1 - half_seq}
    greet(("seq", "exp", "dp"))

    token_copies = [
        remote(
            tokens_ref.at[m], token_other.at[m], token_sems.at[m, 0], token_sems.at[m, 1], across
        )
        for m in range(micro_count)
    ]
    weights = []
    for index, (own, full) in enumerate(
        ((pack_own, pk), (in_own, wi), (out_own, wo), (up_own, up), (down_own, down))
    ):
        size = own.shape[0]
        place = full.at[core] if index == 0 else full.at[pl.ds(core * size, size)]
        weights.append(
            (
                remote(own, place, weight_sems.at[index, 0], weight_sems.at[index, 1], partner),
                pltpu.make_async_copy(own, place, weight_sems.at[index, 2]),
            )
        )
    token_copies[0].start()
    for index in range(3):
        weights[index][0].start()
        weights[index][1].start()
    token_copies[1].start()
    for index in range(3, 5):
        weights[index][0].start()
        weights[index][1].start()

    def have(index):
        weights[index][0].wait_recv()
        weights[index][1].wait()

    cots = [Exchange(cot_send.at[m], cot_got.at[m], all_sems, m) for m in range(micro_count)]
    rowses = [Exchange(row_send.at[m], row_got.at[m], all_sems, 2 + m) for m in range(micro_count)]
    gradses = [Exchange(cot_send.at[m], grads_out.at[m], all_sems, 4 + m) for m in range(micro_count)]
    lane_two = iota((rows, slots_out.shape[2]), 1)

    def claim(m):
        one, two = assign_stage(routes_ref[m], priority_ref[m], capacity, padded)
        slots_out[m] = jnp.where(lane_two == 0, one, two).astype(jnp.int32)

        def store(start, batch, block):
            cot_send[m, start : start + batch] = block

        spread_stage(cot_ref[m], one, two, experts, padded, store)

    used = [0]

    def keep(refs, later):
        index = used[0]
        used[0] += 1

        def copy():
            source, target = refs()
            return pltpu.make_async_copy(source, target, out_sems.at[index])

        copy().start()
        later.append(copy)

    late = []
    claim(0)
    cots[0].start()
    have(0)
    pack_out[...] = jnp.concatenate([pk[0], pk[1]], axis=1)

    def gain(row):
        return pack_out[row : row + 1].astype(F32)

    def first_norm(values):
        return (normalise(values.astype(F32))[0] * gain(0) + gain(1)).astype(BF16)

    def attention_phase(query, pair, bias, residual, moe, attended):
        def project_own(m):
            def store(part, index, block):
                if part == 0:
                    query[m, index] = block
                else:
                    pair[m, 0, 2 * index + part - 1] = block

            project(first_norm(tokens_ref[m]), wi, range(3), store)

        def project_other(m):
            def store(part, index, block):
                pair[m, 1, 2 * index + part - 1] = block

            project(first_norm(token_other[m]), wi, range(1, 3), store)

        have(1)
        for m in range(micro_count):
            project_own(m)
        claim(1)
        have(2)
        keep(lambda: (wi, in_out), late)
        keep(lambda: (wo, out_out), late)
        outs, local = [], []
        for m in range(micro_count):
            token_copies[m].wait_recv()
            project_other(m)
            keep(lambda m=m: (token_other.at[m], token_out.at[m]), late)
            keep(lambda m=m: (query.at[m], query_out.at[m]), outs)
            keep(lambda m=m: (pair.at[m], pair_out.at[m]), outs)

            def store_bias(half, block):
                bias[half] = block

            bias_stage(lengths_ref, m, rows, store_bias)
            for copy in local:
                copy().wait()
            attend_stage(query.at[m], pair.at[m], bias, attended, stats_out.at[m])
            summed = tokens_ref[m].astype(F32) + mm(attended[...], wo[...])
            residual[...] = summed
            moe_input = (normalise(summed)[0] * gain(2) + gain(3)).astype(BF16)
            moe[...] = moe_input
            gates = gates_of(mm_nt(moe_input, pack_out[...]), routes_ref[m])
            gates_out[m] = jnp.where(lane_two == 0, gates[0], gates[1])
            slots = slots_out[m]
            slot_cols = [slots[:, k : k + 1] for k in range(2)]
            place = iota((rows, 128), 1)

            def gate_rows(expert, block):
                row = sum(
                    jnp.where(slot_cols[k] - expert * padded == place, gates[k], 0.0)
                    for k in range(2)
                )
                return with_rows(block, capacity, pieces(jnp.sum(row, axis=0, keepdims=True), 2))

            def store(start, batch, block):
                row_send[m, start : start + batch] = block

            spread_stage(
                moe_input,
                slot_cols[0].astype(F32),
                slot_cols[1].astype(F32),
                experts,
                padded,
                store,
                gate_rows,
            )
            rowses[m].start()
            if m == 0:
                cots[1].start()
            local = []
            keep(lambda m=m: (residual, residual_out.at[m]), local)
            keep(lambda m=m: (moe, moe_out.at[m]), local)
            keep(lambda m=m: (attended, attended_out.at[m]), local)
        for copy in outs + local:
            copy().wait()

    pl.run_scoped(
        attention_phase,
        pltpu.VMEM((micro_count, width // 128, rows, 128), BF16),
        pltpu.VMEM((micro_count, 2, width // 64, rows, 128), BF16),
        pltpu.VMEM((2, rows, rows), F32),
        pltpu.VMEM((rows, width), F32),
        pltpu.VMEM((rows, width), BF16),
        pltpu.VMEM((rows, width), BF16),
    )
    have(3)
    have(4)
    chunks = up.shape[1] // CHUNK
    half_chunks = chunks // 2
    half_rows = width // 2

    def expert_phase(x, g, y, dx, up_buf, down_buf, up_past, down_past, up_low, down_low):
        def order(i):
            return lax.rem(i + core * half_chunks, chunks)

        def span(i):
            return pl.ds(pl.multiple_of(order(i) * CHUNK, CHUNK), CHUNK)

        def chunk_out(slot, i):
            return (
                pltpu.make_async_copy(up_buf.at[slot], up_old.at[i], chunk_sems.at[slot, 0]),
                pltpu.make_async_copy(down_buf.at[slot], down_old.at[i], chunk_sems.at[slot, 1]),
            )

        def chunk_past(slot, i):
            return (
                pltpu.make_async_copy(up_old.at[i], up_past.at[slot], past_sems.at[slot, 0]),
                pltpu.make_async_copy(down_old.at[i], down_past.at[slot], past_sems.at[slot, 1]),
            )

        def up_kept(slot, i):
            mine = up_buf.at[slot, pl.ds(core * half_rows, half_rows)]
            return pltpu.make_async_copy(mine, up_keep.at[order(i)], chunk_sems.at[slot, 0])

        def up_given(slot, i):
            place = order(i)
            return remote(
                up_low.at[slot], up_got.at[place], low_sems.at[slot, 0], got_sems.at[0, place], partner
            )

        def down_kept(slot, i):
            return pltpu.make_async_copy(
                down_buf.at[slot], down_keep.at[lax.rem(i, half_chunks)], chunk_sems.at[slot, 1]
            )

        def down_given(slot, i):
            place = lax.rem(i, half_chunks)
            return remote(
                down_low.at[slot],
                down_got.at[place],
                low_sems.at[slot, 1],
                got_sems.at[1, place],
                partner,
            )

        def start_expert(m):
            cots[m].arrived()
            rowses[m].arrived()
            flatten_stage(row_got.at[m], cot_got.at[m], x, g, capacity)
            y[...] = jnp.zeros_like(y)
            dx[...] = jnp.zeros_like(dx)

        def end_expert(m):
            cots[m].sent()
            rowses[m].sent()
            finish_stage(cot_got.at[m], y, dx, row_send.at[m], cot_send.at[m], capacity)
            gradses[m].start()
            keep(lambda m=m: (row_send.at[m], back_out.at[m]), late)

        start_expert(0)

        def first_pass(i, _):
            slot = lax.rem(i, 2)
            up_grad, down_grad = expert_step(x, g, y, dx, up[:, span(i)], down[span(i), :])

            @pl.when(i >= 2)
            def _():
                for copy in chunk_out(slot, i - 2):
                    copy.wait()

            up_buf[slot] = up_grad
            down_buf[slot] = down_grad
            for copy in chunk_out(slot, i):
                copy.start()
            return 0

        lax.fori_loop(0, chunks, first_pass, 0)
        end_expert(0)
        for i in range(chunks - 2, chunks):
            for copy in chunk_out(i % 2, i):
                copy.wait()
        for copy in chunk_past(0, 0):
            copy.start()
        start_expert(1)

        def second_pass(i, _):
            slot = lax.rem(i, 2)

            @pl.when(i + 1 < chunks)
            def _():
                for copy in chunk_past(1 - slot, i + 1):
                    copy.start()

            up_grad, down_grad = expert_step(x, g, y, dx, up[:, span(i)], down[span(i), :])
            for copy in chunk_past(slot, i):
                copy.wait()

            @pl.when(i >= 2)
            def _():
                up_kept(slot, i - 2).wait()
                up_given(slot, i - 2).wait_send()

                @pl.when(i - 2 < half_chunks)
                def _():
                    down_kept(slot, i - 2).wait()

                @pl.when(i - 2 >= half_chunks)
                def _():
                    down_given(slot, i - 2).wait_send()

            up_buf[slot] = up_grad + up_past[slot]
            up_kept(slot, i).start()
            up_low[slot] = up_buf[slot, pl.ds((1 - core) * half_rows, half_rows), :].astype(BF16)
            up_given(slot, i).start()

            @pl.when(i < half_chunks)
            def _():
                down_buf[slot] = down_grad + down_past[slot]
                down_kept(slot, i).start()

            @pl.when(i >= half_chunks)
            def _():
                down_low[slot] = (down_grad + down_past[slot]).astype(BF16)
                down_given(slot, i).start()

            return 0

        lax.fori_loop(0, chunks, second_pass, 0)
        end_expert(1)
        for i in range(chunks - 2, chunks):
            up_kept(i % 2, i).wait()
            up_given(i % 2, i).wait_send()
            down_given(i % 2, i).wait_send()

    pl.run_scoped(
        expert_phase,
        pltpu.VMEM((flat, width), BF16),
        pltpu.VMEM((flat, width), BF16),
        pltpu.VMEM((flat, width), F32),
        pltpu.VMEM((flat, width), F32),
        pltpu.VMEM((2, width, CHUNK), F32),
        pltpu.VMEM((2, CHUNK, width), F32),
        pltpu.VMEM((2, width, CHUNK), F32),
        pltpu.VMEM((2, CHUNK, width), F32),
        pltpu.VMEM((2, width // 2, CHUNK), BF16),
        pltpu.VMEM((2, CHUNK, width), BF16),
    )

    def sum_phase(up_mine, up_theirs, up_total, down_mine, down_theirs, down_total):
        def loads(kind, slot, i):
            mine, theirs, kept, got = (
                (up_mine, up_theirs, up_keep, up_got),
                (down_mine, down_theirs, down_keep, down_got),
            )[kind]
            return (
                pltpu.make_async_copy(kept.at[i], mine.at[slot], chunk_sems.at[slot, 0]),
                pltpu.make_async_copy(got.at[i], theirs.at[slot], chunk_sems.at[slot, 1]),
            )

        def stores(kind, slot, i):
            total, kept = ((up_total, up_sum), (down_total, down_sum))[kind]
            here = pl.ds(pl.multiple_of(i * CHUNK, CHUNK), CHUNK)
            target = kept.at[:, here] if kind == 0 else kept.at[here]
            return pltpu.make_async_copy(total.at[slot], target, past_sems.at[slot, kind])

        def taken(kind, i):
            low, got = ((up_total, up_got), (down_total, down_got))[kind]
            remote(
                low.at[0], got.at[i], low_sems.at[0, kind], got_sems.at[kind, i], partner
            ).wait_recv()

        for kind, count in ((0, chunks), (1, half_chunks)):
            mine, theirs, total = (
                (up_mine, up_theirs, up_total),
                (down_mine, down_theirs, down_total),
            )[kind]
            taken(kind, 0)
            for copy in loads(kind, 0, 0):
                copy.start()

            def step(i, _):
                slot = lax.rem(i, 2)

                @pl.when(i + 1 < count)
                def _():
                    taken(kind, i + 1)
                    for copy in loads(kind, 1 - slot, i + 1):
                        copy.start()

                for copy in loads(kind, slot, i):
                    copy.wait()

                @pl.when(i >= 2)
                def _():
                    stores(kind, slot, i - 2).wait()

                total[slot] = (mine[slot] + theirs[slot].astype(F32)).astype(BF16)
                stores(kind, slot, i).start()
                return 0

            lax.fori_loop(0, count, step, 0)
            for i in range(count - 2, count):
                stores(kind, i % 2, i).wait()
            if kind == 0:
                cross.start()

    cross = remote(up_sum, up_arrived, cross_sems.at[0], cross_sems.at[1], across)
    pl.run_scoped(
        sum_phase,
        pltpu.VMEM((2, half_rows, CHUNK), F32),
        pltpu.VMEM((2, half_rows, CHUNK), BF16),
        pltpu.VMEM((2, half_rows, CHUNK), BF16),
        pltpu.VMEM((2, CHUNK, width), F32),
        pltpu.VMEM((2, CHUNK, width), BF16),
        pltpu.VMEM((2, CHUNK, width), BF16),
    )
    for m in range(micro_count):
        token_copies[m].wait_send()
        gradses[m].arrived()
        gradses[m].sent()
    for index in range(5):
        weights[index][0].wait_send()
    for copy in late:
        copy().wait()
    cross.wait()


def back_stage(
    m,
    capacity,
    padded,
    grads_ref,
    slots,
    gates,
    routes,
    cot,
    residual,
    moe_input,
    attended_ref,
    stats_ref,
    query_ref,
    pair_ref,
    lengths_ref,
    pack,
    wo_ref,
    wi_ref,
    tokens,
    token_other,
    residual_grad_ref,
    out_grad_ref,
    in_grad_ref,
    first_grad_ref,
    other_grad_ref,
    small_ref,
    bias_ref,
    attended_grad_ref,
    packed_ref,
    add,
):
    rows, width = residual.shape
    couples, _, couple = query_ref.shape
    head_dim = couple // 2
    experts = grads_ref.shape[0]
    gain = [pack[row : row + 1].astype(F32) for row in range(4)]

    def store_bias(half, block):
        bias_ref[half] = block

    bias_stage(lengths_ref, m, rows, store_bias)
    (moe_grad,) = gather_stage(grads_ref, slots, ((0, 1),), padded)
    place, lane = iota((padded, 128), 0), iota((rows, 128), 1)
    found = [jnp.zeros((rows, 128), F32) for _ in range(2)]
    for expert in range(experts):
        tail = grads_ref[expert][:, 0:128].astype(F32)
        inside = (place >= capacity) & (place < capacity + 3)
        row = jnp.sum(jnp.where(inside, tail, 0.0), axis=0, keepdims=True)
        for k in range(2):
            found[k] = found[k] + jnp.where(
                slots[:, k : k + 1] - expert * padded == lane, row, 0.0
            )
    gate_grad = [jnp.sum(part, axis=1, keepdims=True) for part in found]
    gate = [gates[:, k : k + 1] for k in range(2)]
    inner = gate[0] * gate_grad[0] + gate[1] * gate_grad[1]
    pack_lane = iota((rows, pack.shape[0]), 1)
    logit_grad = sum(
        jnp.where(
            pack_lane == routes[:, k : k + 1] + ROUTER_ROW, gate[k] * (gate_grad[k] - inner), 0.0
        )
        for k in range(2)
    )
    parts = [part.astype(BF16) for part in pieces(logit_grad, 3)]
    moe_grad = moe_grad + sum(mm(part, pack) for part in parts)
    router_grad = sum(mm_tn(part, moe_input) for part in parts)
    xhat, scale = normalise(residual)
    small_row = iota(router_grad.shape, 0)
    small = jnp.where(
        small_row == 2,
        jnp.sum(moe_grad * xhat, axis=0, keepdims=True),
        jnp.where(small_row == 3, jnp.sum(moe_grad, axis=0, keepdims=True), router_grad),
    )
    small_ref[...] = small
    residual_grad = cot.astype(F32) + norm_backward(moe_grad, gain[2], xhat, scale)
    residual_grad_ref[...] = residual_grad
    branch = residual_grad.astype(BF16)
    add(out_grad_ref, slice(0, width), mm_tn(attended_ref[...], branch))
    attended_grad = mm_nt(branch, wo_ref[...]).astype(BF16)
    for index in range(couples):
        attended_grad_ref[index] = attended_grad[:, index * couple : (index + 1) * couple]
    low_lane = iota((1, couple), 1) < head_dim

    def step(index, _):
        query = query_ref[index].astype(F32) * head_dim**-0.5
        grad_low = attended_grad_ref[index]
        grad = grad_low.astype(F32)
        query_low = query.astype(BF16)
        keys = [pair_ref[half, 2 * index] for half in range(2)]
        values = [pair_ref[half, 2 * index + 1] for half in range(2)]
        keys_turned = [part.astype(F32).T.astype(BF16) for part in keys]
        key_grads, value_grads, query_grads = [[], []], [[], []], []
        for head in range(2):
            chosen = low_lane == (head == 0)
            mine = jnp.where(chosen, query, 0.0).astype(BF16)
            mine_grad = jnp.where(chosen, grad, 0.0).astype(BF16)
            stats = stats_ref[pl.ds(index * 2 + head, 1), :]
            weighting = [
                jnp.exp(mm_nt(keys[half], mine) + bias_ref[half] - stats) for half in range(2)
            ]
            weighting_grad = [mm_nt(values[half], mine_grad) for half in range(2)]
            delta = sum(
                jnp.sum(weighting[half] * weighting_grad[half], axis=0, keepdims=True)
                for half in range(2)
            )
            here = slice(head * head_dim, (head + 1) * head_dim)
            query_total = 0.0
            for half in range(2):
                scores_grad = (weighting[half] * (weighting_grad[half] - delta)).astype(BF16)
                value_grads[half].append(mm(weighting[half].astype(BF16), grad_low))
                key_grads[half].append(mm(scores_grad, query_low))
                query_total = query_total + mm(keys_turned[half][here], scores_grad)
            query_grads.append(query_total * head_dim**-0.5)

        def lanes(part):
            return pl.ds(pl.multiple_of(part * width + index * couple, couple), couple)

        packed_ref[0:rows, lanes(0)] = jnp.concatenate(query_grads, axis=0).T.astype(BF16)
        for half in range(2):
            here = slice(half * rows, (half + 1) * rows)
            packed_ref[here, lanes(1)] = jnp.where(low_lane, *key_grads[half]).astype(BF16)
            packed_ref[here, lanes(2)] = jnp.where(low_lane, *value_grads[half]).astype(BF16)
        return 0

    lax.fori_loop(0, couples, step, 0)
    own_xhat = normalise(tokens.astype(F32))[0]
    other_xhat = normalise(token_other.astype(F32))[0]
    low = jnp.concatenate([own_xhat, other_xhat], axis=0) * gain[0] + gain[1]
    low = low.astype(BF16)
    first_grad = mm_nt(packed_ref[0:rows, 0:width], wi_ref[:, 0:width])
    other_grad = 0.0
    add(in_grad_ref, slice(0, width), mm_tn(low[0:rows], packed_ref[0:rows, 0:width]))
    for part in range(1, 3):
        here = slice(part * width, (part + 1) * width)
        add(in_grad_ref, here, mm_tn(low, packed_ref[:, here]))
        first_grad = first_grad + mm_nt(packed_ref[0:rows, here], wi_ref[:, here])
        other_grad = other_grad + mm_nt(packed_ref[rows:, here], wi_ref[:, here])
    first_grad_ref[...] = first_grad
    other_grad_ref[...] = other_grad.astype(BF16)


def last_stage(tokens, gain, residual_grad, first_grad, arrived):
    xhat, scale = normalise(tokens.astype(F32))
    total = first_grad + arrived.astype(F32)
    return (
        (residual_grad + norm_backward(total, gain, xhat, scale)).astype(BF16),
        jnp.sum(total * xhat, axis=0, keepdims=True),
        jnp.sum(total, axis=0, keepdims=True),
    )


def put(ref, here, value):
    ref[:, here] = value


def back_kernel(
    m,
    capacity,
    padded,
    grads_ref,
    slots_ref,
    gates_ref,
    routes_ref,
    cot_ref,
    residual_ref,
    moe_ref,
    attended_ref,
    stats_ref,
    query_ref,
    pair_ref,
    lengths_ref,
    pack_ref,
    wo_ref,
    wi_ref,
    tokens_ref,
    token_other_ref,
    residual_grad_ref,
    out_grad_ref,
    in_grad_ref,
    first_grad_ref,
    other_grad_ref,
    small_ref,
    bias_ref,
    attended_grad_ref,
    packed_ref,
):
    back_stage(
        m,
        capacity,
        padded,
        grads_ref,
        slots_ref[...],
        gates_ref[...],
        routes_ref[...],
        cot_ref[...],
        residual_ref[...],
        moe_ref[...],
        attended_ref,
        stats_ref,
        query_ref,
        pair_ref,
        lengths_ref,
        pack_ref[...],
        wo_ref,
        wi_ref,
        tokens_ref[...],
        token_other_ref[...],
        residual_grad_ref,
        out_grad_ref,
        in_grad_ref,
        first_grad_ref,
        other_grad_ref,
        small_ref,
        bias_ref,
        attended_grad_ref,
        packed_ref,
        put,
    )


def last_kernel(
    tokens_ref, pack_ref, residual_grad_ref, first_grad_ref, arrived_ref, small_in, out_ref, small_ref
):
    grads, gain_grad, shift_grad = last_stage(
        tokens_ref[...],
        pack_ref[0:1].astype(F32),
        residual_grad_ref[...],
        first_grad_ref[...],
        arrived_ref[...],
    )
    out_ref[...] = grads
    row = iota(small_ref.shape, 0)
    small_ref[...] = jnp.where(row == 0, gain_grad, jnp.where(row == 1, shift_grad, small_in[...]))


def shape(dims, dtype):
    return jax.ShapeDtypeStruct(dims, dtype)


def call(kernel, outs, specs, scratch=(), name=None, flops=10**9):
    return pl.pallas_call(
        kernel,
        out_shape=outs,
        in_specs=specs,
        out_specs=tuple(VMEM for _ in outs),
        scratch_shapes=scratch,
        compiler_params=pltpu.CompilerParams(vmem_limit_bytes=56 * 2**20),
        cost_estimate=pl.CostEstimate(flops=flops, bytes_accessed=10**7, transcendentals=0),
        name=name,
    )


def body(
    tokens,
    first_gain,
    first_shift,
    attention_in,
    attention_out,
    second_gain,
    second_shift,
    router_weight,
    up_weight,
    down_weight,
    routes,
    priority,
    lengths,
    out_cotangent,
):
    micro_count, _, rows, width = tokens.shape
    experts = lax.axis_size("exp") * up_weight.shape[0]
    hidden = up_weight.shape[2]
    capacity = (210 * rows + 100 * experts - 1) // (100 * experts)
    padded = (capacity + 3 + 7) // 8 * 8
    flat = experts * padded
    core = lax.axis_index("dp")
    chunks = hidden // CHUNK
    couples = width // 128

    def swap(value, axis):
        return lax.ppermute(value, axis, [(0, 1), (1, 0)])

    pack_rows = (ROUTER_ROW + experts + 15) // 16 * 16
    norms = jnp.stack([first_gain, first_shift, second_gain, second_shift])
    pack = jnp.concatenate(
        [
            norms,
            jnp.zeros((ROUTER_ROW - 4, norms.shape[1]), BF16),
            router_weight.T,
            jnp.zeros((pack_rows - ROUTER_ROW - experts, norms.shape[1]), BF16),
        ]
    )
    blocks = (micro_count, experts, padded, width)
    token_dims = (micro_count, rows, width)
    dma = pltpu.SemaphoreType.DMA
    tokens, cot = tokens[:, 0], out_cotangent[:, 0]
    routes, lengths = routes[:, 0], lengths[:, 0]
    query_dims = (micro_count, couples, rows, 128)
    pair_dims = (micro_count, 2, 2 * couples, rows, 128)
    outs = (
        (VMEM, (pack_rows, width), BF16),
        (ANY, (width, 3 * width), BF16),
        (ANY, (width, width), BF16),
        (ANY, token_dims, BF16),
        (ANY, query_dims, BF16),
        (ANY, pair_dims, BF16),
        (ANY, token_dims, F32),
        (ANY, token_dims, BF16),
        (ANY, token_dims, BF16),
        (VMEM, (micro_count, 16, rows), F32),
        (VMEM, (micro_count, rows, 2), F32),
        (VMEM, (micro_count, rows, 2), jnp.int32),
        (ANY, blocks, BF16),
        (ANY, blocks, BF16),
        (ANY, (chunks, width, CHUNK), F32),
        (ANY, (chunks, CHUNK, width), F32),
        (ANY, (chunks, width // 2, CHUNK), F32),
        (ANY, (chunks // 2, CHUNK, width), F32),
        (ANY, (chunks, width // 2, CHUNK), BF16),
        (ANY, (chunks // 2, CHUNK, width), BF16),
        (ANY, (width // 2, hidden), BF16),
        (ANY, (hidden // 2, width), BF16),
        (ANY, (width // 2, hidden), BF16),
    )
    size = lax.axis_size("exp")
    (
        pack,
        wi,
        wo,
        token_other,
        query,
        pair,
        residual,
        moe,
        attended,
        stats,
        gates,
        slots,
        back,
        grads,
        _,
        _,
        _,
        _,
        _,
        _,
        up_sum,
        down_sum,
        up_arrived,
    ) = pl.pallas_call(
        partial(forward_kernel, capacity),
        out_shape=tuple(shape(dims, dtype) for _, dims, dtype in outs),
        in_specs=[VMEM] * 4 + [SMEM] + [ANY] * 5,
        out_specs=tuple(spec for spec, _, _ in outs),
        scratch_shapes=[
            pltpu.VMEM((2, pack_rows, width // 2), BF16),
            pltpu.VMEM((width, 3 * width), BF16),
            pltpu.VMEM((width, width), BF16),
            pltpu.VMEM((width, hidden), BF16),
            pltpu.VMEM((hidden, width), BF16),
            pltpu.VMEM(token_dims, BF16),
            pltpu.VMEM(blocks, BF16),
            pltpu.VMEM(blocks, BF16),
            pltpu.VMEM(blocks, BF16),
            pltpu.VMEM(blocks, BF16),
            dma((6, 2, size)),
            dma((5, 3)),
            dma((micro_count, 2)),
            dma((24,)),
            dma((2, 2)),
            dma((2, 2)),
            dma((2, 2)),
            dma((2, chunks)),
            dma((2,)),
        ],
        compiler_params=pltpu.CompilerParams(
            collective_id=0, has_side_effects=True, vmem_limit_bytes=61 * 2**20
        ),
        cost_estimate=pl.CostEstimate(
            flops=5 * 10**10, bytes_accessed=10**8, transcendentals=10**7
        ),
        name="forward_and_experts",
    )(tokens, cot, routes, priority, lengths, pack, attention_in, attention_out, up_weight[0], down_weight[0])
    arrived = [
        lax.all_to_all(back[m], "exp", split_axis=0, concat_axis=0, tiled=True)
        for m in range(micro_count)
    ]
    mixed_parts, token_grads = [], []
    in_sum = out_sum = small_sum = 0.0
    for m in range(micro_count):
        residual_grad, out_grad, in_grad, first_grad, other_grad, small = call(
            partial(back_kernel, m, capacity, padded),
            (
                shape((rows, width), F32),
                shape((width, width), F32),
                shape((width, 3 * width), F32),
                shape((rows, width), F32),
                shape((rows, width), BF16),
                shape((pack_rows, width), F32),
            ),
            [VMEM] * 11 + [SMEM] + [VMEM] * 5,
            (
                pltpu.VMEM((2, rows, rows), F32),
                pltpu.VMEM((couples, rows, 128), BF16),
                pltpu.VMEM((2 * rows, 3 * width), BF16),
            ),
            name="attend_back",
        )(
            grads[m],
            slots[m],
            gates[m],
            routes[m],
            cot[m],
            residual[m],
            moe[m],
            attended[m],
            stats[m],
            query[m],
            pair[m],
            lengths,
            pack,
            wo,
            wi,
            tokens[m],
            token_other[m],
        )
        tokens_grad, small = call(
            last_kernel,
            (shape((rows, width), BF16), shape((pack_rows, width), F32)),
            [VMEM] * 6,
            name="tokens_back",
        )(tokens[m], pack, residual_grad, first_grad, swap(other_grad, "seq"), small)
        (mixed,) = call(
            partial(mix_kernel, padded), (shape((rows, width), BF16),), [VMEM] * 4, name="mix"
        )(arrived[m], slots[m], gates[m], residual[m])
        mixed_parts.append(mixed)
        token_grads.append(tokens_grad)
        in_sum = in_sum + in_grad
        out_sum = out_sum + out_grad
        small_sum = small_sum + small

    def halves(value, axis):
        size = value.shape[axis] // 2
        mine = lax.dynamic_slice_in_dim(value, core * size, size, axis)
        theirs = lax.dynamic_slice_in_dim(value, (1 - core) * size, size, axis)
        return mine + swap(theirs.astype(BF16), "dp").astype(F32)

    up_total = (up_sum.astype(F32) + up_arrived.astype(F32))[None]
    down_total = (down_sum.astype(F32) + swap(down_sum, "seq").astype(F32))[None]
    dense = halves(jnp.concatenate([in_sum, out_sum], axis=1), 0).astype(BF16)
    dense = lax.psum(dense, ("seq", "exp")).astype(F32)
    small = halves(small_sum, 1)
    small = lax.psum(small, ("seq", "exp"))
    return (
        jnp.stack(mixed_parts)[:, None],
        jnp.stack(token_grads)[:, None],
        small[0],
        small[1],
        dense[:, : 3 * width],
        dense[:, 3 * width :],
        small[2],
        small[3],
        small[ROUTER_ROW : ROUTER_ROW + experts].T,
        up_total,
        down_total,
    )


def solution(mesh):
    placed = (
        P(None, ("exp", "dp"), "seq", None),
        P("dp"),
        P("dp"),
        P("dp", None),
        P("dp", None),
        P("dp"),
        P("dp"),
        P("dp", None),
        P("exp", "dp", None),
        P("exp", "dp", None),
        P(None, ("exp", "dp"), "seq", None),
        P(None, ("exp", "dp"), "seq"),
        P(None, ("exp", "dp"), None),
        P(None, ("exp", "dp"), "seq", None),
    )
    return jax.shard_map(
        body,
        mesh=mesh,
        in_specs=placed,
        out_specs=(
            P(None, ("exp", "dp"), "seq", None),
            P(None, ("exp", "dp"), "seq", None),
            P("dp"),
            P("dp"),
            P("dp", None),
            P("dp", None),
            P("dp"),
            P("dp"),
            P("dp", None),
            P("exp", "dp", None),
            P("exp", "dp", None),
        ),
        check_vma=False,
    )
```

```python
from functools import partial

import jax
import jax.numpy as jnp
from jax import lax
from jax.experimental import pallas as pl
from jax.experimental.pallas import tpu as pltpu
from jax.sharding import PartitionSpec as P

HEADS = 12
EPSILON = 1e-06
F32 = jnp.float32
BF16 = jnp.bfloat16
VMEM = pl.BlockSpec(memory_space=pltpu.VMEM)
SMEM = pl.BlockSpec(memory_space=pltpu.SMEM)
ROUTER_ROW = 8


def mm(a, b):
    return lax.dot_general(a, b, (((1,), (0,)), ((), ())), preferred_element_type=F32)


def mm_nt(a, b):
    return lax.dot_general(a, b, (((1,), (1,)), ((), ())), preferred_element_type=F32)


def mm_tn(a, b):
    return lax.dot_general(a, b, (((0,), (0,)), ((), ())), preferred_element_type=F32)


def iota(shape, dim):
    return lax.broadcasted_iota(jnp.int32, shape, dim)


def row_of(column, size):
    return jnp.sum(jnp.where(iota((size, size), 0) == iota((size, size), 1), column, 0.0), axis=0, keepdims=True)


def column_of(row, size):
    return jnp.sum(jnp.where(iota((size, size), 0) == iota((size, size), 1), row, 0.0), axis=1, keepdims=True)


def normalise(values):
    centre = values - jnp.mean(values, axis=-1, keepdims=True)
    spread = jnp.mean(centre * centre, axis=-1, keepdims=True)
    scale = lax.rsqrt(spread + EPSILON)
    return centre * scale, scale


def norm_backward(grad, gain, xhat, scale):
    scaled = grad * gain
    along = jnp.mean(scaled * xhat, axis=-1, keepdims=True)
    return scale * (scaled - jnp.mean(scaled, axis=-1, keepdims=True) - xhat * along)


def assign_stage(routes, level, capacity, padded):
    rows = routes.shape[0]
    level_row = level.astype(F32)
    level_column = column_of(level_row, rows)
    me, other = iota((rows, rows), 0), iota((rows, rows), 1)
    ahead = (level_row > level_column) | ((level_row == level_column) & (other < me))
    lane = iota((rows, 128), 1)
    first, second = routes[:, 0:1], routes[:, 1:2]
    wants = jnp.where((lane == first) | (lane == second + 64), 1.0, 0.0)
    count = mm(jnp.where(ahead, 1.0, 0.0).astype(BF16), wants.astype(BF16))
    total = jnp.sum(wants, axis=0, keepdims=True)
    rank_one = jnp.sum(jnp.where(lane == first, count, 0.0), axis=1, keepdims=True)
    rank_two = jnp.sum(
        jnp.where(lane == second + 64, count, 0.0) + jnp.where(lane == second, total, 0.0),
        axis=1,
        keepdims=True,
    )
    slot_one = jnp.where(rank_one < capacity, first.astype(F32) * padded + rank_one, -1.0)
    slot_two = jnp.where(rank_two < capacity, second.astype(F32) * padded + rank_two, -1.0)
    return slot_one, slot_two


def batch_of(experts, padded):
    best = 1
    for count in range(1, experts + 1):
        if experts % count == 0 and count * padded <= 256 and (count * padded) % 16 == 0:
            best = count
    return best


def spread_stage(values, slot_one, slot_two, experts, padded, store, extra=None):
    rows, width = values.shape
    one, two = row_of(slot_one, rows).astype(jnp.int32), row_of(slot_two, rows).astype(jnp.int32)
    batch = batch_of(experts, padded)
    place = iota((batch * padded, rows), 0)
    for start in range(0, experts, batch):
        here = place + start * padded
        pick = jnp.where((here == one) | (here == two), 1.0, 0.0).astype(BF16)
        block = mm(pick, values).reshape(batch, padded, width)
        if extra is not None:
            parts = []
            for inner in range(batch):
                parts.append(extra(start + inner, block[inner]))
            block = jnp.stack(parts)
        store(start, batch, block.astype(BF16))


def with_rows(block, first_row, rows):
    place = iota(block.shape, 0)
    for step, row in enumerate(rows):
        wide = jnp.concatenate([row, jnp.zeros((1, block.shape[1] - row.shape[1]), F32)], axis=1)
        block = jnp.where(place == first_row + step, wide, block)
    return block


def pieces(value, count):
    parts = []
    for _ in range(count):
        part = value.astype(BF16).astype(F32)
        parts.append(part)
        value = value - part
    return parts


def bias_stage(lengths_ref, m, rows, store):
    own_start = lax.axis_index("seq") * rows
    span = lax.axis_size("seq") * rows
    ends = []
    total = 0
    for step in range(lengths_ref.shape[1]):
        total = total + lengths_ref[m, step]
        ends.append(total)

    def documents(place):
        found = jnp.zeros(place.shape, jnp.int32)
        for end in ends:
            found = found + jnp.where(place >= end, 1, 0)
        return found

    asked = documents(iota((1, rows), 1) + own_start)
    for half in range(2):
        start = own_start if half == 0 else span - rows - own_start
        held = documents(iota((rows, 1), 0) + start)
        store(half, jnp.where(held == asked, 0.0, -1e30))


def gates_of(logits, routes):
    lane = iota(logits.shape, 1)
    chosen = [
        jnp.sum(jnp.where(lane == routes[:, k : k + 1] + ROUTER_ROW, logits, 0.0), axis=1, keepdims=True)
        for k in range(2)
    ]
    peak = jnp.maximum(*chosen)
    raised = [jnp.exp(part - peak) for part in chosen]
    total = raised[0] + raised[1]
    return raised[0] / total, raised[1] / total


def phi_terms(hidden):
    size = jnp.abs(hidden)
    bell = jnp.exp(hidden * hidden * -0.5)
    t = 1.0 / (1.0 + 0.23164188828 * size)
    tail = t * (
        0.127414796
        + t * (-0.142248368 + t * (0.7107068705 + t * (-0.7265760135 + t * 0.5307027145)))
    )
    tail = tail * bell
    return jnp.where(hidden >= 0, 1.0 - tail, tail), bell


def gather_stage(blocks_ref, slots, weights, padded):
    experts, _, width = blocks_ref.shape
    rows = slots.shape[0]
    batch = batch_of(experts, padded)
    place = iota((rows, batch * padded), 1)
    totals = [jnp.zeros((rows, width), F32) for _ in weights]
    for start in range(0, experts, batch):
        block = (
            blocks_ref[start : start + batch].astype(F32).reshape(batch * padded, width).astype(BF16)
        )
        here = place + start * padded
        for index, chosen in enumerate(weights):
            hit = slots[:, chosen[0] : chosen[0] + 1] == here
            for k in chosen[1:]:
                hit = hit | (slots[:, k : k + 1] == here)
            totals[index] = totals[index] + mm(jnp.where(hit, 1.0, 0.0).astype(BF16), block)
    return totals


MESH = pl.DeviceIdType.MESH
ANY = pl.BlockSpec(memory_space=pl.ANY)
CHUNK = 256


def remote(source, target, sends, arrives, device):
    return pltpu.make_async_remote_copy(
        src_ref=source,
        dst_ref=target,
        send_sem=sends,
        recv_sem=arrives,
        device_id=device,
        device_id_type=MESH,
    )


def greet(axes):
    barrier = pltpu.get_barrier_semaphore()
    count = 0
    for axis in axes:
        size, me = lax.axis_size(axis), lax.axis_index(axis)
        for step in range(1, size):
            pl.semaphore_signal(
                barrier, inc=1, device_id={axis: lax.rem(me + step, size)}, device_id_type=MESH
            )
            count += 1
    pl.semaphore_wait(barrier, count)


class Exchange:
    def __init__(self, source, target, sems, index):
        self.refs, self.index = (source, target, sems), index

    def copies(self):
        source, target, sems = self.refs
        size, me = lax.axis_size("exp"), lax.axis_index("exp")
        found = []
        for step in range(1, size):
            peer = lax.rem(me + step, size)
            found.append(
                remote(
                    source.at[peer],
                    target.at[me],
                    sems.at[self.index, 0, step],
                    sems.at[self.index, 1, step],
                    {"exp": peer},
                )
            )
        return found

    def own(self):
        source, target, sems = self.refs
        me = lax.axis_index("exp")
        return pltpu.make_async_copy(source.at[me], target.at[me], sems.at[self.index, 0, 0])

    def start(self):
        for copy in self.copies():
            copy.start()
        self.own().start()

    def arrived(self):
        for copy in self.copies():
            copy.wait_recv()
        self.own().wait()

    def sent(self):
        for copy in self.copies():
            copy.wait_send()


def project(low, weight_ref, parts, store):
    width = low.shape[1]
    for part in parts:
        block = mm(low, weight_ref[:, part * width : (part + 1) * width]).astype(BF16)
        for index in range(width // 128):
            store(part, index, block[:, index * 128 : (index + 1) * 128])


def attend_stage(query_ref, pair_ref, bias_ref, attended_ref, stats_ref):
    couples, rows, couple = query_ref.shape
    head_dim = couple // 2
    low_lane = iota((1, couple), 1) < head_dim

    def step(index, _):
        query = query_ref[index].astype(F32) * head_dim**-0.5
        keys = [pair_ref[half, 2 * index] for half in range(2)]
        values = [pair_ref[half, 2 * index + 1].astype(F32).T.astype(BF16) for half in range(2)]
        outs = []
        for head in range(2):
            mine = jnp.where(low_lane == (head == 0), query, 0.0).astype(BF16)
            scores = [mm_nt(keys[half], mine) + bias_ref[half] for half in range(2)]
            peak = jnp.maximum(*[jnp.max(part, axis=0, keepdims=True) for part in scores])
            raised = [jnp.exp(part - peak) for part in scores]
            total = sum(jnp.sum(part, axis=0, keepdims=True) for part in raised)
            here = slice(head * head_dim, (head + 1) * head_dim)
            summed = sum(mm(values[half][here], raised[half].astype(BF16)) for half in range(2))
            outs.append(summed / total)
            stats_ref[pl.ds(index * 2 + head, 1), :] = peak + jnp.log(total)
        lanes = pl.ds(pl.multiple_of(index * couple, couple), couple)
        attended_ref[:, lanes] = jnp.concatenate(outs, axis=0).T.astype(BF16)
        return 0

    lax.fori_loop(0, couples, step, 0)


def flatten_stage(rows_ref, cot_ref, x, g, capacity):
    experts, padded, width = rows_ref.shape
    batch = batch_of(experts, padded)
    flat = batch * padded
    place, lane = iota((padded, 128), 0), iota((padded, 128), 1)
    for start in range(0, experts, batch):
        block = rows_ref[start : start + batch].astype(F32)
        cot = cot_ref[start : start + batch].astype(F32)
        here = slice(start * padded, start * padded + flat)
        x[here, :] = block.reshape(flat, width).astype(BF16)
        scaled = []
        for inner in range(batch):
            inside = (place == capacity) | (place == capacity + 1)
            gate_row = jnp.sum(jnp.where(inside, block[inner][:, 0:128], 0.0), axis=0, keepdims=True)
            gate = jnp.sum(jnp.where(place == lane, gate_row, 0.0), axis=1, keepdims=True)
            scaled.append(cot[inner] * gate)
        g[here, :] = jnp.stack(scaled).reshape(flat, width).astype(BF16)


def expert_step(x, g, y, dx, up, down):
    hidden = mm(x[...], up)
    active_grad = mm_nt(g[...], down)
    phi, bell = phi_terms(hidden)
    active = (hidden * phi).astype(BF16)
    hidden_grad = (active_grad * (phi + hidden * bell * 0.3989422804)).astype(BF16)
    y[...] += mm(active, down)
    dx[...] += mm_nt(hidden_grad, up)
    return mm_tn(x[...], hidden_grad), mm_tn(active, g[...])


def finish_stage(cot_ref, y, dx, back_ref, grads_ref, capacity):
    experts, padded, width = cot_ref.shape
    batch = batch_of(experts, padded)
    place, lane = iota((padded, 128), 0), iota((padded, 128), 1)
    for start in range(0, experts, batch):
        here = slice(start * padded, (start + batch) * padded)
        produced = y[here, :].reshape(batch, padded, width).astype(BF16)
        back_ref[start : start + batch] = produced
        cot = cot_ref[start : start + batch].astype(F32)
        along = jnp.sum(cot * produced.astype(F32), axis=-1, keepdims=True)
        grads = dx[here, :].reshape(batch, padded, width)
        parts = []
        for inner in range(batch):
            row = jnp.sum(jnp.where(place == lane, along[inner], 0.0), axis=0, keepdims=True)
            parts.append(with_rows(grads[inner], capacity, pieces(row, 3)))
        grads_ref[start : start + batch] = jnp.stack(parts).astype(BF16)


def forward_kernel(
    capacity,
    tokens_ref,
    cot_ref,
    routes_ref,
    priority_ref,
    lengths_ref,
    pack_own,
    in_own,
    out_own,
    up_own,
    down_own,
    pack_out,
    in_out,
    out_out,
    token_out,
    query_out,
    pair_out,
    residual_out,
    moe_out,
    attended_out,
    stats_out,
    gates_out,
    slots_out,
    back_out,
    grads_out,
    up_old,
    down_old,
    up_keep,
    down_keep,
    up_got,
    down_got,
    up_sum,
    down_sum,
    up_arrived,
    pk,
    wi,
    wo,
    up,
    down,
    token_other,
    cot_send,
    row_send,
    cot_got,
    row_got,
    all_sems,
    weight_sems,
    token_sems,
    out_sems,
    chunk_sems,
    past_sems,
    low_sems,
    got_sems,
    cross_sems,
):
    micro_count, rows, width = tokens_ref.shape
    experts, padded = cot_send.shape[1], cot_send.shape[2]
    flat = experts * padded
    core, half_seq = lax.axis_index("dp"), lax.axis_index("seq")
    partner = {"dp": 1 - core}
    across = {"seq": 1 - half_seq}
    greet(("seq", "exp", "dp"))

    token_copies = [
        remote(
            tokens_ref.at[m], token_other.at[m], token_sems.at[m, 0], token_sems.at[m, 1], across
        )
        for m in range(micro_count)
    ]
    weights = []
    for index, (own, full) in enumerate(
        ((pack_own, pk), (in_own, wi), (out_own, wo), (up_own, up), (down_own, down))
    ):
        size = own.shape[0]
        place = full.at[core] if index == 0 else full.at[pl.ds(core * size, size)]
        weights.append(
            (
                remote(own, place, weight_sems.at[index, 0], weight_sems.at[index, 1], partner),
                pltpu.make_async_copy(own, place, weight_sems.at[index, 2]),
            )
        )
    token_copies[0].start()
    for index in range(3):
        weights[index][0].start()
        weights[index][1].start()
    token_copies[1].start()
    for index in range(3, 5):
        weights[index][0].start()
        weights[index][1].start()

    def have(index):
        weights[index][0].wait_recv()
        weights[index][1].wait()

    cots = [Exchange(cot_send.at[m], cot_got.at[m], all_sems, m) for m in range(micro_count)]
    rowses = [Exchange(row_send.at[m], row_got.at[m], all_sems, 2 + m) for m in range(micro_count)]
    gradses = [Exchange(cot_send.at[m], grads_out.at[m], all_sems, 4 + m) for m in range(micro_count)]
    lane_two, lane_four = iota((rows, 2), 1), iota((rows, 4), 1)

    def claim(m):
        one, two = assign_stage(routes_ref[m], priority_ref[m], capacity, padded)
        routes = routes_ref[m]
        found = jnp.where(lane_four == 0, one, two).astype(jnp.int32)
        chosen = jnp.where(lane_four == 2, routes[:, 0:1], routes[:, 1:2])
        slots_out[m] = jnp.where(lane_four < 2, found, chosen)

        def store(start, batch, block):
            cot_send[m, start : start + batch] = block

        spread_stage(cot_ref[m], one, two, experts, padded, store)

    used = [0]

    def keep(refs, later):
        index = used[0]
        used[0] += 1

        def copy():
            source, target = refs()
            return pltpu.make_async_copy(source, target, out_sems.at[index])

        copy().start()
        later.append(copy)

    late = []
    claim(0)
    cots[0].start()
    have(0)
    pack_out[...] = jnp.concatenate([pk[0], pk[1]], axis=1)

    def gain(row):
        return pack_out[row : row + 1].astype(F32)

    def first_norm(values):
        return (normalise(values.astype(F32))[0] * gain(0) + gain(1)).astype(BF16)

    def attention_phase(query, pair, bias, residual, moe, attended):
        def project_own(m):
            def store(part, index, block):
                if part == 0:
                    query[m, index] = block
                else:
                    pair[m, 0, 2 * index + part - 1] = block

            project(first_norm(tokens_ref[m]), wi, range(3), store)

        def project_other(m):
            def store(part, index, block):
                pair[m, 1, 2 * index + part - 1] = block

            project(first_norm(token_other[m]), wi, range(1, 3), store)

        have(1)
        for m in range(micro_count):
            project_own(m)
        claim(1)
        have(2)
        keep(lambda: (wi, in_out), late)
        keep(lambda: (wo, out_out), late)
        outs, local = [], []
        for m in range(micro_count):
            token_copies[m].wait_recv()
            project_other(m)
            keep(lambda m=m: (token_other.at[m], token_out.at[m]), late)
            keep(lambda m=m: (query.at[m], query_out.at[m]), outs)
            keep(lambda m=m: (pair.at[m], pair_out.at[m]), outs)

            def store_bias(half, block):
                bias[half] = block

            bias_stage(lengths_ref, m, rows, store_bias)
            for copy in local:
                copy().wait()
            attend_stage(query.at[m], pair.at[m], bias, attended, stats_out.at[m])
            summed = tokens_ref[m].astype(F32) + mm(attended[...], wo[...])
            residual[...] = summed
            moe_input = (normalise(summed)[0] * gain(2) + gain(3)).astype(BF16)
            moe[...] = moe_input
            gates = gates_of(mm_nt(moe_input, pack_out[...]), routes_ref[m])
            gates_out[m] = jnp.where(lane_two == 0, gates[0], gates[1])
            slots = slots_out[m]
            slot_cols = [slots[:, k : k + 1] for k in range(2)]
            place = iota((rows, 128), 1)

            def gate_rows(expert, block):
                row = sum(
                    jnp.where(slot_cols[k] - expert * padded == place, gates[k], 0.0)
                    for k in range(2)
                )
                return with_rows(block, capacity, pieces(jnp.sum(row, axis=0, keepdims=True), 2))

            def store(start, batch, block):
                row_send[m, start : start + batch] = block

            spread_stage(
                moe_input,
                slot_cols[0].astype(F32),
                slot_cols[1].astype(F32),
                experts,
                padded,
                store,
                gate_rows,
            )
            rowses[m].start()
            if m == 0:
                cots[1].start()
            local = []
            keep(lambda m=m: (residual, residual_out.at[m]), local)
            keep(lambda m=m: (moe, moe_out.at[m]), local)
            keep(lambda m=m: (attended, attended_out.at[m]), local)
        for copy in outs + local:
            copy().wait()

    pl.run_scoped(
        attention_phase,
        pltpu.VMEM((micro_count, width // 128, rows, 128), BF16),
        pltpu.VMEM((micro_count, 2, width // 64, rows, 128), BF16),
        pltpu.VMEM((2, rows, rows), F32),
        pltpu.VMEM((rows, width), F32),
        pltpu.VMEM((rows, width), BF16),
        pltpu.VMEM((rows, width), BF16),
    )
    have(3)
    have(4)
    chunks = up.shape[1] // CHUNK
    half_chunks = chunks // 2
    half_rows = width // 2

    def expert_phase(x, g, y, dx, up_buf, down_buf, up_past, down_past, up_low, down_low):
        def order(i):
            return lax.rem(i + core * half_chunks, chunks)

        def span(i):
            return pl.ds(pl.multiple_of(order(i) * CHUNK, CHUNK), CHUNK)

        def chunk_out(slot, i):
            return (
                pltpu.make_async_copy(up_buf.at[slot], up_old.at[i], chunk_sems.at[slot, 0]),
                pltpu.make_async_copy(down_buf.at[slot], down_old.at[i], chunk_sems.at[slot, 1]),
            )

        def chunk_past(slot, i):
            return (
                pltpu.make_async_copy(up_old.at[i], up_past.at[slot], past_sems.at[slot, 0]),
                pltpu.make_async_copy(down_old.at[i], down_past.at[slot], past_sems.at[slot, 1]),
            )

        def up_kept(slot, i):
            mine = up_buf.at[slot, pl.ds(core * half_rows, half_rows)]
            return pltpu.make_async_copy(mine, up_keep.at[order(i)], chunk_sems.at[slot, 0])

        def up_given(slot, i):
            place = order(i)
            return remote(
                up_low.at[slot], up_got.at[place], low_sems.at[slot, 0], got_sems.at[0, place], partner
            )

        def down_kept(slot, i):
            return pltpu.make_async_copy(
                down_buf.at[slot], down_keep.at[lax.rem(i, half_chunks)], chunk_sems.at[slot, 1]
            )

        def down_given(slot, i):
            place = lax.rem(i, half_chunks)
            return remote(
                down_low.at[slot],
                down_got.at[place],
                low_sems.at[slot, 1],
                got_sems.at[1, place],
                partner,
            )

        def start_expert(m):
            cots[m].arrived()
            rowses[m].arrived()
            flatten_stage(row_got.at[m], cot_got.at[m], x, g, capacity)
            y[...] = jnp.zeros_like(y)
            dx[...] = jnp.zeros_like(dx)

        def end_expert(m):
            cots[m].sent()
            rowses[m].sent()
            finish_stage(cot_got.at[m], y, dx, row_send.at[m], cot_send.at[m], capacity)
            gradses[m].start()
            keep(lambda m=m: (row_send.at[m], back_out.at[m]), late)

        start_expert(0)

        def first_pass(i, _):
            slot = lax.rem(i, 2)
            up_grad, down_grad = expert_step(x, g, y, dx, up[:, span(i)], down[span(i), :])

            @pl.when(i >= 2)
            def _():
                for copy in chunk_out(slot, i - 2):
                    copy.wait()

            up_buf[slot] = up_grad
            down_buf[slot] = down_grad
            for copy in chunk_out(slot, i):
                copy.start()
            return 0

        lax.fori_loop(0, chunks, first_pass, 0)
        end_expert(0)
        for i in range(chunks - 2, chunks):
            for copy in chunk_out(i % 2, i):
                copy.wait()
        for copy in chunk_past(0, 0):
            copy.start()
        start_expert(1)

        def second_pass(i, _):
            slot = lax.rem(i, 2)

            @pl.when(i + 1 < chunks)
            def _():
                for copy in chunk_past(1 - slot, i + 1):
                    copy.start()

            up_grad, down_grad = expert_step(x, g, y, dx, up[:, span(i)], down[span(i), :])
            for copy in chunk_past(slot, i):
                copy.wait()

            @pl.when(i >= 2)
            def _():
                up_kept(slot, i - 2).wait()
                up_given(slot, i - 2).wait_send()

                @pl.when(i - 2 < half_chunks)
                def _():
                    down_kept(slot, i - 2).wait()

                @pl.when(i - 2 >= half_chunks)
                def _():
                    down_given(slot, i - 2).wait_send()

            up_buf[slot] = up_grad + up_past[slot]
            up_kept(slot, i).start()
            up_low[slot] = up_buf[slot, pl.ds((1 - core) * half_rows, half_rows), :].astype(BF16)
            up_given(slot, i).start()

            @pl.when(i < half_chunks)
            def _():
                down_buf[slot] = down_grad + down_past[slot]
                down_kept(slot, i).start()

            @pl.when(i >= half_chunks)
            def _():
                down_low[slot] = (down_grad + down_past[slot]).astype(BF16)
                down_given(slot, i).start()

            return 0

        lax.fori_loop(0, chunks, second_pass, 0)
        end_expert(1)
        for i in range(chunks - 2, chunks):
            up_kept(i % 2, i).wait()
            up_given(i % 2, i).wait_send()
            down_given(i % 2, i).wait_send()

    pl.run_scoped(
        expert_phase,
        pltpu.VMEM((flat, width), BF16),
        pltpu.VMEM((flat, width), BF16),
        pltpu.VMEM((flat, width), F32),
        pltpu.VMEM((flat, width), F32),
        pltpu.VMEM((2, width, CHUNK), F32),
        pltpu.VMEM((2, CHUNK, width), F32),
        pltpu.VMEM((2, width, CHUNK), F32),
        pltpu.VMEM((2, CHUNK, width), F32),
        pltpu.VMEM((2, width // 2, CHUNK), BF16),
        pltpu.VMEM((2, CHUNK, width), BF16),
    )

    def sum_phase(up_mine, up_theirs, up_total, down_mine, down_theirs, down_total):
        def loads(kind, slot, i):
            mine, theirs, kept, got = (
                (up_mine, up_theirs, up_keep, up_got),
                (down_mine, down_theirs, down_keep, down_got),
            )[kind]
            return (
                pltpu.make_async_copy(kept.at[i], mine.at[slot], chunk_sems.at[slot, 0]),
                pltpu.make_async_copy(got.at[i], theirs.at[slot], chunk_sems.at[slot, 1]),
            )

        def stores(kind, slot, i):
            total, kept = ((up_total, up_sum), (down_total, down_sum))[kind]
            here = pl.ds(pl.multiple_of(i * CHUNK, CHUNK), CHUNK)
            target = kept.at[:, here] if kind == 0 else kept.at[here]
            return pltpu.make_async_copy(total.at[slot], target, past_sems.at[slot, kind])

        def taken(kind, i):
            low, got = ((up_total, up_got), (down_total, down_got))[kind]
            remote(
                low.at[0], got.at[i], low_sems.at[0, kind], got_sems.at[kind, i], partner
            ).wait_recv()

        for kind, count in ((0, chunks), (1, half_chunks)):
            mine, theirs, total = (
                (up_mine, up_theirs, up_total),
                (down_mine, down_theirs, down_total),
            )[kind]
            taken(kind, 0)
            for copy in loads(kind, 0, 0):
                copy.start()

            def step(i, _):
                slot = lax.rem(i, 2)

                @pl.when(i + 1 < count)
                def _():
                    taken(kind, i + 1)
                    for copy in loads(kind, 1 - slot, i + 1):
                        copy.start()

                for copy in loads(kind, slot, i):
                    copy.wait()

                @pl.when(i >= 2)
                def _():
                    stores(kind, slot, i - 2).wait()

                total[slot] = (mine[slot] + theirs[slot].astype(F32)).astype(BF16)
                stores(kind, slot, i).start()
                return 0

            lax.fori_loop(0, count, step, 0)
            for i in range(count - 2, count):
                stores(kind, i % 2, i).wait()
            if kind == 0:
                cross.start()

    cross = remote(up_sum, up_arrived, cross_sems.at[0], cross_sems.at[1], across)
    pl.run_scoped(
        sum_phase,
        pltpu.VMEM((2, half_rows, CHUNK), F32),
        pltpu.VMEM((2, half_rows, CHUNK), BF16),
        pltpu.VMEM((2, half_rows, CHUNK), BF16),
        pltpu.VMEM((2, CHUNK, width), F32),
        pltpu.VMEM((2, CHUNK, width), BF16),
        pltpu.VMEM((2, CHUNK, width), BF16),
    )
    for m in range(micro_count):
        token_copies[m].wait_send()
        gradses[m].arrived()
        gradses[m].sent()
    for index in range(5):
        weights[index][0].wait_send()
    for copy in late:
        copy().wait()
    cross.wait()


class Reduction:
    def __init__(self, index, columns, seq_first, refs):
        self.acc, self.give, self.land, self.give2, self.land2, self.give3, self.land3 = refs[:7]
        self.more_give, self.more_land, self.final, self.sems = refs[7:]
        self.index, self.cols = index, columns
        size, me = lax.axis_size("exp"), lax.axis_index("exp")
        self.size, self.me = size, me
        seq, low = lax.axis_index("seq"), lax.rem(me, 2)
        flip = {"exp": me + 1 - 2 * low}
        across = {"seq": 1 - seq}
        self.first, self.second = (seq, low) if seq_first else (low, seq)
        self.to_first, self.to_second = (across, flip) if seq_first else (flip, across)
        self.turn = lax.rem(lax.div(me, 2), 4)
        self.quad = self.first * 8 + self.second * 4

    def peer(self, step):
        turn = lax.rem(self.turn + step, 4)
        return turn, {"exp": self.me + 2 * (turn - self.turn)}

    def copy(self, step, source, target, device):
        return remote(
            source, target, self.sems.at[self.index, step, 0], self.sems.at[self.index, step, 1], device
        )

    def one(self):
        return self.copy(0, self.give.at[:, :, self.cols], self.land.at[:, :, self.cols], self.to_first)

    def two(self):
        return self.copy(1, self.give2.at[:, :, self.cols], self.land2.at[:, :, self.cols], self.to_second)

    def three(self, step):
        turn, device = self.peer(step)
        return self.copy(
            1 + step, self.give3.at[turn, :, self.cols], self.land3.at[self.turn, :, self.cols], device
        )

    def more(self, step):
        block = 8 << step
        device = {"exp": self.me + block * (1 - 2 * lax.rem(lax.div(self.me, block), 2))}
        return self.copy(
            10 + step, self.more_give.at[step, :, self.cols], self.more_land.at[step, :, self.cols], device
        )

    def four(self, step):
        place = self.final.at[self.quad + self.turn, :, self.cols]
        return self.copy(4 + step, place, place, self.peer(step)[1])

    def five(self):
        place = self.final.at[pl.ds(self.quad, 4), :, self.cols]
        return self.copy(8, place, place, self.to_second)

    def six(self):
        place = self.final.at[pl.ds(self.first * 8, 8), :, self.cols]
        return self.copy(9, place, place, self.to_first)

    def start_one(self):
        self.give[:, :, self.cols] = self.acc[pl.ds((1 - self.first) * 8, 8), :, self.cols].astype(BF16)
        self.one().start()

    def start_two(self):
        self.one().wait_recv()
        mine = pl.ds(self.first * 8, 8)
        self.acc[mine, :, self.cols] = self.acc[mine, :, self.cols] + self.land[
            :, :, self.cols
        ].astype(F32)
        self.give2[:, :, self.cols] = self.acc[
            pl.ds(self.first * 8 + (1 - self.second) * 4, 4), :, self.cols
        ].astype(BF16)
        self.two().start()

    def start_three(self):
        self.two().wait_recv()
        total = self.acc[pl.ds(self.quad, 4), :, self.cols] + self.land2[:, :, self.cols].astype(F32)
        self.acc[pl.ds(self.quad, 4), :, self.cols] = total
        self.give3[:, :, self.cols] = total.astype(BF16)
        for step in range(1, 4):
            self.three(step).start()

    def start_four(self):
        total = self.acc[self.quad + self.turn, :, self.cols]
        for step in range(1, 4):
            self.three(step).wait_recv()
        for step in range(1, 4):
            total = total + self.land3[self.peer(step)[0], :, self.cols].astype(F32)
        steps = (self.size // 8).bit_length() - 1
        for step in range(steps):
            low = total.astype(BF16)
            self.more_give[step, :, self.cols] = low
            copy = self.more(step)
            copy.start()
            copy.wait_recv()
            total = low.astype(F32) + self.more_land[step, :, self.cols].astype(F32)
            copy.wait_send()
        self.final[self.quad + self.turn, :, self.cols] = total.astype(BF16)
        for step in range(1, 4):
            self.four(step).start()

    def start_five(self):
        for step in range(1, 4):
            turn, device = self.peer(step)
            place = self.final.at[self.quad + turn, :, self.cols]
            self.copy(4 + 4 - step, place, place, device).wait_recv()
        self.five().start()

    def start_six(self):
        self.five().wait_recv()
        self.six().start()

    def finish(self):
        self.six().wait_recv()
        self.one().wait_send()
        self.two().wait_send()
        for step in range(1, 4):
            self.three(step).wait_send()
            self.four(step).wait_send()
        self.five().wait_send()
        self.six().wait_send()


def backward_kernel(
    capacity,
    cot_ref,
    slots_ref,
    gates_ref,
    residual_ref,
    stats_ref,
    pack_ref,
    wo,
    wi,
    tokens_ref,
    token_other,
    lengths_ref,
    grads_in,
    back_in,
    moe_in,
    attended_in,
    query_in,
    pair_in,
    down_sum,
    mixed_out,
    tokens_out,
    small_out,
    final_out,
    back_got,
    down_arrived,
    grads,
    moe,
    attended,
    query,
    pair,
    bias,
    attended_grad,
    packed,
    low,
    residual_grad,
    first_grad,
    other_got,
    dense,
    core_give,
    core_got,
    land,
    land2,
    land3,
    more_give,
    more_land,
    small,
    small_give,
    small_got,
    all_sems,
    load_sems,
    other_sems,
    cross_sems,
    core_sems,
    sum_sems,
    small_sems,
):
    micro_count, rows, width = tokens_ref.shape
    experts, padded = grads.shape[0], grads.shape[1]
    couples, _, couple = query.shape
    head_dim = couple // 2
    core, half_seq = lax.axis_index("dp"), lax.axis_index("seq")
    partner, across = {"dp": 1 - core}, {"seq": 1 - half_seq}
    low_lane = iota((1, couple), 1) < head_dim

    def load(index, m):
        source, target = (
            (grads_in, grads),
            (moe_in, moe),
            (attended_in, attended),
            (query_in, query),
            (pair_in, pair),
            (back_got, grads),
        )[index]
        return pltpu.make_async_copy(source.at[m], target, load_sems.at[index])

    for index in range(5):
        load(index, 0).start()
    greet(("seq", "exp", "dp"))
    backs = [Exchange(back_in.at[m], back_got.at[m], all_sems, m) for m in range(micro_count)]
    for m in range(micro_count):
        backs[m].start()

    def cross():
        return remote(down_sum, down_arrived, cross_sems.at[0], cross_sems.at[1], across)

    cross().start()

    def gain(row):
        return pack_ref[row : row + 1].astype(F32)

    def gather(value):
        return value.reshape(2, 16, width // 32, value.shape[1])

    def store(m, start, value):
        here = slice(start, start + value.shape[1])
        value = gather(value)
        dense[:, :, :, here] = value if m == 0 else dense[:, :, :, here] + value

    def before(m):
        def store_bias(half, block):
            bias[half] = block

        bias_stage(lengths_ref, m, rows, store_bias)
        load(0, m).wait()
        load(1, m).wait()
        load(2, m).wait()
        slots, gates = slots_ref[m], gates_ref[m]
        routes = slots[:, 2:4]
        pack = pack_ref[...]
        (moe_grad,) = gather_stage(grads, slots, ((0, 1),), padded)
        place, lane = iota((padded, 128), 0), iota((rows, 128), 1)
        found = [jnp.zeros((rows, 128), F32) for _ in range(2)]
        for expert in range(experts):
            tail = grads[expert][:, 0:128].astype(F32)
            inside = (place >= capacity) & (place < capacity + 3)
            row = jnp.sum(jnp.where(inside, tail, 0.0), axis=0, keepdims=True)
            for k in range(2):
                found[k] = found[k] + jnp.where(
                    slots[:, k : k + 1] - expert * padded == lane, row, 0.0
                )
        gate_grad = [jnp.sum(part, axis=1, keepdims=True) for part in found]
        gate = [gates[:, k : k + 1] for k in range(2)]
        inner = gate[0] * gate_grad[0] + gate[1] * gate_grad[1]
        pack_lane = iota((rows, pack.shape[0]), 1)
        logit_grad = sum(
            jnp.where(
                pack_lane == routes[:, k : k + 1] + ROUTER_ROW,
                gate[k] * (gate_grad[k] - inner),
                0.0,
            )
            for k in range(2)
        )
        parts = [part.astype(BF16) for part in pieces(logit_grad, 3)]
        moe_grad = moe_grad + sum(mm(part, pack) for part in parts)
        router_grad = sum(mm_tn(part, moe[...]) for part in parts)
        xhat, scale = normalise(residual_ref[m])
        small_row = iota(router_grad.shape, 0)
        terms = jnp.where(
            small_row == 2,
            jnp.sum(moe_grad * xhat, axis=0, keepdims=True),
            jnp.where(small_row == 3, jnp.sum(moe_grad, axis=0, keepdims=True), router_grad),
        )
        small[...] = terms if m == 0 else small[...] + terms
        total = cot_ref[m].astype(F32) + norm_backward(moe_grad, gain(2), xhat, scale)
        residual_grad[m] = total
        branch = total.astype(BF16)
        store(m, 0, mm_tn(attended[...], branch))
        turned = mm_nt(branch, wo[...]).astype(BF16)
        for index in range(couples):
            attended_grad[index] = turned[:, index * couple : (index + 1) * couple]
        for half, ref in enumerate((tokens_ref, token_other)):
            low[half * rows : (half + 1) * rows] = (
                normalise(ref[m].astype(F32))[0] * gain(0) + gain(1)
            ).astype(BF16)

    def heads(m, begin, end):
        def step(index, _):
            asked = query[index].astype(F32) * head_dim**-0.5
            grad_low = attended_grad[index]
            grad = grad_low.astype(F32)
            asked_low = asked.astype(BF16)
            keys = [pair[half, 2 * index] for half in range(2)]
            values = [pair[half, 2 * index + 1] for half in range(2)]
            keys_turned = [part.astype(F32).T.astype(BF16) for part in keys]
            key_grads, value_grads, query_grads = [[], []], [[], []], []
            for head in range(2):
                chosen = low_lane == (head == 0)
                mine = jnp.where(chosen, asked, 0.0).astype(BF16)
                mine_grad = jnp.where(chosen, grad, 0.0).astype(BF16)
                stats = stats_ref[m, pl.ds(index * 2 + head, 1), :]
                weighting = [
                    jnp.exp(mm_nt(keys[half], mine) + bias[half] - stats) for half in range(2)
                ]
                weighting_grad = [mm_nt(values[half], mine_grad) for half in range(2)]
                delta = sum(
                    jnp.sum(weighting[half] * weighting_grad[half], axis=0, keepdims=True)
                    for half in range(2)
                )
                here = slice(head * head_dim, (head + 1) * head_dim)
                query_total = 0.0
                for half in range(2):
                    scores_grad = (weighting[half] * (weighting_grad[half] - delta)).astype(BF16)
                    value_grads[half].append(mm(weighting[half].astype(BF16), grad_low))
                    key_grads[half].append(mm(scores_grad, asked_low))
                    query_total = query_total + mm(keys_turned[half][here], scores_grad)
                query_grads.append(query_total * head_dim**-0.5)

            def lanes(part):
                return pl.ds(pl.multiple_of(part * width + index * couple, couple), couple)

            packed[0:rows, lanes(0)] = jnp.concatenate(query_grads, axis=0).T.astype(BF16)
            for half in range(2):
                here = slice(half * rows, (half + 1) * rows)
                packed[here, lanes(1)] = jnp.where(low_lane, *key_grads[half]).astype(BF16)
                packed[here, lanes(2)] = jnp.where(low_lane, *value_grads[half]).astype(BF16)
            return 0

        lax.fori_loop(begin, end, step, 0)

    third = width // 2

    def project_grads(m, group):
        for part in range(3):
            tall = rows if part == 0 else 2 * rows
            source = slice(part * width + group * third, part * width + (group + 1) * third)
            value = mm_tn(low[0:tall], packed[0:tall, source])
            store(m, width + (3 * group + part) * third, value)

    def other_copy(m):
        return remote(
            tokens_out.at[m], other_got.at[m], other_sems.at[m, 0], other_sems.at[m, 1], across
        )

    def firsts(m):
        own = mm_nt(packed[0:rows, 0:width], wi[:, 0:width])
        other = 0.0
        for part in range(1, 3):
            here = slice(part * width, (part + 1) * width)
            own = own + mm_nt(packed[0:rows, here], wi[:, here])
            other = other + mm_nt(packed[rows:, here], wi[:, here])
        tokens_out[m] = other.astype(BF16)
        other_copy(m).start()
        first_grad[m] = own
        own_hat = normalise(tokens_ref[m].astype(F32))[0]
        other_hat = normalise(token_other[m].astype(F32))[0]
        gain_grad = jnp.sum(own * own_hat + other * other_hat, axis=0, keepdims=True)
        shift_grad = jnp.sum(own + other, axis=0, keepdims=True)
        row = iota(small.shape, 0)
        small[...] = small[...] + jnp.where(
            row == 0, gain_grad, jnp.where(row == 1, shift_grad, 0.0)
        )

    def lasts(m):
        other_copy(m).wait()
        total = first_grad[m] + other_got[m].astype(F32)
        xhat, scale = normalise(tokens_ref[m].astype(F32))
        tokens_out[m] = (residual_grad[m] + norm_backward(total, gain(0), xhat, scale)).astype(BF16)

    def mix(m):
        backs[m].arrived()
        load(5, m).start()
        load(5, m).wait()
        gates = gates_ref[m]
        one, two = gather_stage(grads, slots_ref[m], ((0,), (1,)), padded)
        mixed_out[m] = (residual_ref[m] + (gates[:, 0:1] * one + gates[:, 1:2] * two)).astype(BF16)

    group_width = 3 * third
    edges = [(0, width), (width, width + group_width), (width + group_width, 4 * width)]
    sums = []
    for index, (begin, end) in enumerate(edges):
        middle = begin + ((end - begin) // 128 + 1) // 2 * 128
        for part, (start, stop) in enumerate(((begin, middle), (middle, end))):
            sums.append(
                Reduction(
                    2 * index + part,
                    slice(start, stop),
                    part == 0,
                    (
                        dense.at[core],
                        core_got.at[pl.ds(0, 8)],
                        land,
                        core_got.at[pl.ds(8, 4)],
                        land2,
                        core_got.at[pl.ds(12, 4)],
                        land3,
                        more_give,
                        more_land,
                        core_give,
                        sum_sems,
                    ),
                )
            )

    def core_copy(group):
        here = slice(*edges[group])
        return remote(
            core_give.at[:, :, here],
            core_got.at[:, :, here],
            core_sems.at[group, 0],
            core_sems.at[group, 1],
            partner,
        )

    def start_core(group):
        here = slice(*edges[group])
        core_give[:, :, here] = dense[1 - core, :, :, here].astype(BF16)
        core_copy(group).start()

    def advance(group, name):
        if name == "one":
            here = slice(*edges[group])
            core_copy(group).wait()
            dense[core, :, :, here] = dense[core, :, :, here] + core_got[:, :, here].astype(F32)
        for item in sums[2 * group : 2 * group + 2]:
            getattr(item, "finish" if name == "finish" else "start_" + name)()

    half_width = width // 2

    def small_copy(step):
        size, me = lax.axis_size("exp"), lax.axis_index("exp")
        if step == 0:
            device = partner
        elif step == 1:
            device = across
        else:
            block = 1 << (step - 2)
            device = {"exp": me + block * (1 - 2 * lax.rem(lax.div(me, block), 2))}
        return remote(
            small_give.at[step],
            small_got.at[step],
            small_sems.at[step, 0],
            small_sems.at[step, 1],
            device,
        )

    small_steps = small_give.shape[0]

    def start_small(step):
        if step == 0:
            place = pl.ds(pl.multiple_of((1 - core) * half_width, 128), half_width)
            small_give[0] = small[:, place]
            small_out[...] = small[:, pl.ds(pl.multiple_of(core * half_width, 128), half_width)]
        else:
            small_copy(step - 1).wait_recv()
            small_out[...] = small_out[...] + small_got[step - 1]
            if step == small_steps:
                return
            small_give[step] = small_out[...]
        small_copy(step).start()

    before(0)
    for index in range(3):
        load(index, 1).start()
    load(3, 0).wait()
    load(4, 0).wait()
    heads(0, 0, couples)
    load(3, 1).start()
    load(4, 1).start()
    project_grads(0, 0)
    project_grads(0, 1)
    firsts(0)
    before(1)
    start_core(0)
    load(3, 1).wait()
    load(4, 1).wait()
    heads(1, 0, couples // 2)
    project_grads(1, 0)
    start_core(1)
    advance(0, "one")
    heads(1, couples // 2, couples)
    project_grads(1, 1)
    start_core(2)
    advance(1, "one")
    advance(0, "two")
    firsts(1)
    start_small(0)
    advance(2, "one")
    advance(1, "two")
    advance(0, "three")
    start_small(1)
    lasts(0)
    advance(2, "two")
    advance(1, "three")
    advance(0, "four")
    start_small(2)
    mix(0)
    advance(2, "three")
    advance(1, "four")
    advance(0, "five")
    start_small(3)
    lasts(1)
    advance(2, "four")
    advance(1, "five")
    advance(0, "six")
    mix(1)
    for step in range(4, small_steps + 1):
        start_small(step)
    advance(2, "five")
    advance(1, "six")
    advance(0, "finish")
    advance(2, "six")
    advance(1, "finish")
    advance(2, "finish")
    result = pltpu.make_async_copy(core_give, final_out, load_sems.at[0])
    result.start()
    for step in range(small_steps):
        small_copy(step).wait_send()
    for m in range(micro_count):
        backs[m].sent()
    cross().wait()
    result.wait()


def shape(dims, dtype):
    return jax.ShapeDtypeStruct(dims, dtype)


def body(
    tokens,
    first_gain,
    first_shift,
    attention_in,
    attention_out,
    second_gain,
    second_shift,
    router_weight,
    up_weight,
    down_weight,
    routes,
    priority,
    lengths,
    out_cotangent,
):
    micro_count, _, rows, width = tokens.shape
    experts = lax.axis_size("exp") * up_weight.shape[0]
    hidden = up_weight.shape[2]
    capacity = (210 * rows + 100 * experts - 1) // (100 * experts)
    padded = (capacity + 3 + 7) // 8 * 8
    flat = experts * padded
    core = lax.axis_index("dp")
    chunks = hidden // CHUNK
    couples = width // 128

    pack_rows = (ROUTER_ROW + experts + 15) // 16 * 16
    norms = jnp.stack([first_gain, first_shift, second_gain, second_shift])
    pack = jnp.concatenate(
        [
            norms,
            jnp.zeros((ROUTER_ROW - 4, norms.shape[1]), BF16),
            router_weight.T,
            jnp.zeros((pack_rows - ROUTER_ROW - experts, norms.shape[1]), BF16),
        ]
    )
    blocks = (micro_count, experts, padded, width)
    token_dims = (micro_count, rows, width)
    dma = pltpu.SemaphoreType.DMA
    tokens, cot = tokens[:, 0], out_cotangent[:, 0]
    routes, lengths = routes[:, 0], lengths[:, 0]
    query_dims = (micro_count, couples, rows, 128)
    pair_dims = (micro_count, 2, 2 * couples, rows, 128)
    outs = (
        (VMEM, (pack_rows, width), BF16),
        (ANY, (width, 3 * width), BF16),
        (ANY, (width, width), BF16),
        (ANY, token_dims, BF16),
        (ANY, query_dims, BF16),
        (ANY, pair_dims, BF16),
        (ANY, token_dims, F32),
        (ANY, token_dims, BF16),
        (ANY, token_dims, BF16),
        (VMEM, (micro_count, 16, rows), F32),
        (VMEM, (micro_count, rows, 2), F32),
        (VMEM, (micro_count, rows, 4), jnp.int32),
        (ANY, blocks, BF16),
        (ANY, blocks, BF16),
        (ANY, (chunks, width, CHUNK), F32),
        (ANY, (chunks, CHUNK, width), F32),
        (ANY, (chunks, width // 2, CHUNK), F32),
        (ANY, (chunks // 2, CHUNK, width), F32),
        (ANY, (chunks, width // 2, CHUNK), BF16),
        (ANY, (chunks // 2, CHUNK, width), BF16),
        (ANY, (width // 2, hidden), BF16),
        (ANY, (hidden // 2, width), BF16),
        (ANY, (width // 2, hidden), BF16),
    )
    size = lax.axis_size("exp")
    (
        pack,
        wi,
        wo,
        token_other,
        query,
        pair,
        residual,
        moe,
        attended,
        stats,
        gates,
        slots,
        back,
        grads,
        _,
        _,
        _,
        _,
        _,
        _,
        up_sum,
        down_sum,
        up_arrived,
    ) = pl.pallas_call(
        partial(forward_kernel, capacity),
        out_shape=tuple(shape(dims, dtype) for _, dims, dtype in outs),
        in_specs=[VMEM] * 4 + [SMEM] + [ANY] * 5,
        out_specs=tuple(spec for spec, _, _ in outs),
        scratch_shapes=[
            pltpu.VMEM((2, pack_rows, width // 2), BF16),
            pltpu.VMEM((width, 3 * width), BF16),
            pltpu.VMEM((width, width), BF16),
            pltpu.VMEM((width, hidden), BF16),
            pltpu.VMEM((hidden, width), BF16),
            pltpu.VMEM(token_dims, BF16),
            pltpu.VMEM(blocks, BF16),
            pltpu.VMEM(blocks, BF16),
            pltpu.VMEM(blocks, BF16),
            pltpu.VMEM(blocks, BF16),
            dma((6, 2, size)),
            dma((5, 3)),
            dma((micro_count, 2)),
            dma((24,)),
            dma((2, 2)),
            dma((2, 2)),
            dma((2, 2)),
            dma((2, chunks)),
            dma((2,)),
        ],
        compiler_params=pltpu.CompilerParams(
            collective_id=0, has_side_effects=True, vmem_limit_bytes=61 * 2**20
        ),
        cost_estimate=pl.CostEstimate(
            flops=5 * 10**10, bytes_accessed=10**8, transcendentals=10**7
        ),
        name="forward_and_experts",
    )(tokens, cot, routes, priority, lengths, pack, attention_in, attention_out, up_weight[0], down_weight[0])
    reds = (16, width // 32, 4 * width)
    extra = max((size // 8).bit_length() - 1, 1)
    steps = 2 + size.bit_length() - 1

    def reduced(count):
        return pltpu.VMEM((count,) + reds[1:], BF16)

    outs = (
        (VMEM, token_dims, BF16),
        (VMEM, token_dims, BF16),
        (VMEM, (pack_rows, width // 2), F32),
        (ANY, reds, BF16),
        (ANY, blocks, BF16),
        (ANY, (hidden // 2, width), BF16),
    )
    mixed, tokens_grad, small, final, _, down_arrived = pl.pallas_call(
        partial(backward_kernel, capacity),
        out_shape=tuple(shape(dims, dtype) for _, dims, dtype in outs),
        in_specs=[VMEM] * 10 + [SMEM] + [ANY] * 7,
        out_specs=tuple(spec for spec, _, _ in outs),
        scratch_shapes=[
            pltpu.VMEM(blocks[1:], BF16),
            pltpu.VMEM((rows, width), BF16),
            pltpu.VMEM((rows, width), BF16),
            pltpu.VMEM(query_dims[1:], BF16),
            pltpu.VMEM(pair_dims[1:], BF16),
            pltpu.VMEM((2, rows, rows), F32),
            pltpu.VMEM(query_dims[1:], BF16),
            pltpu.VMEM((2 * rows, 3 * width), BF16),
            pltpu.VMEM((2 * rows, width), BF16),
            pltpu.VMEM(token_dims, F32),
            pltpu.VMEM(token_dims, F32),
            pltpu.VMEM(token_dims, BF16),
            pltpu.VMEM((2,) + reds, F32),
            reduced(16),
            reduced(16),
            reduced(8),
            reduced(4),
            reduced(4),
            reduced(extra),
            reduced(extra),
            pltpu.VMEM((pack_rows, width), F32),
            pltpu.VMEM((steps, pack_rows, width // 2), F32),
            pltpu.VMEM((steps, pack_rows, width // 2), F32),
            dma((2, 2, size)),
            dma((6,)),
            dma((micro_count, 2)),
            dma((2,)),
            dma((3, 2)),
            dma((6, 12, 2)),
            dma((steps, 2)),
        ],
        compiler_params=pltpu.CompilerParams(
            collective_id=1, has_side_effects=True, vmem_limit_bytes=62 * 2**20
        ),
        cost_estimate=pl.CostEstimate(
            flops=2 * 10**10, bytes_accessed=5 * 10**7, transcendentals=10**7
        ),
        name="backward_and_sums",
    )(
        cot,
        slots,
        gates,
        residual,
        stats,
        pack,
        wo,
        wi,
        tokens,
        token_other,
        lengths,
        grads,
        back,
        moe,
        attended,
        query,
        pair,
        down_sum,
    )
    final = final.reshape(width // 2, 4 * width).astype(F32)
    third = width // 2
    in_grad = jnp.concatenate(
        [
            final[:, width + (3 * group + part) * third : width + (3 * group + part + 1) * third]
            for part in range(3)
            for group in range(2)
        ],
        axis=1,
    )
    return (
        mixed[:, None],
        tokens_grad[:, None],
        small[0],
        small[1],
        in_grad,
        final[:, :width],
        small[2],
        small[3],
        small[ROUTER_ROW : ROUTER_ROW + experts].T,
        (up_sum.astype(F32) + up_arrived.astype(F32))[None],
        (down_sum.astype(F32) + down_arrived.astype(F32))[None],
    )


def solution(mesh):
    placed = (
        P(None, ("exp", "dp"), "seq", None),
        P("dp"),
        P("dp"),
        P("dp", None),
        P("dp", None),
        P("dp"),
        P("dp"),
        P("dp", None),
        P("exp", "dp", None),
        P("exp", "dp", None),
        P(None, ("exp", "dp"), "seq", None),
        P(None, ("exp", "dp"), "seq"),
        P(None, ("exp", "dp"), None),
        P(None, ("exp", "dp"), "seq", None),
    )
    return jax.shard_map(
        body,
        mesh=mesh,
        in_specs=placed,
        out_specs=(
            P(None, ("exp", "dp"), "seq", None),
            P(None, ("exp", "dp"), "seq", None),
            P("dp"),
            P("dp"),
            P("dp", None),
            P("dp", None),
            P("dp"),
            P("dp"),
            P("dp", None),
            P("exp", "dp", None),
            P("exp", "dp", None),
        ),
        check_vma=False,
    )
```

```python
from functools import partial

import jax
import jax.numpy as jnp
from jax import lax
from jax.experimental import pallas as pl
from jax.experimental.pallas import tpu as pltpu
from jax.sharding import PartitionSpec as P

HEADS = 12
EPSILON = 1e-06
F32 = jnp.float32
BF16 = jnp.bfloat16
VMEM = pl.BlockSpec(memory_space=pltpu.VMEM)
SMEM = pl.BlockSpec(memory_space=pltpu.SMEM)
ROUTER_ROW = 8


def mm(a, b):
    return lax.dot_general(a, b, (((1,), (0,)), ((), ())), preferred_element_type=F32)


def mm_nt(a, b):
    return lax.dot_general(a, b, (((1,), (1,)), ((), ())), preferred_element_type=F32)


def mm_tn(a, b):
    return lax.dot_general(a, b, (((0,), (0,)), ((), ())), preferred_element_type=F32)


def iota(shape, dim):
    return lax.broadcasted_iota(jnp.int32, shape, dim)


def row_of(column, size):
    return jnp.sum(jnp.where(iota((size, size), 0) == iota((size, size), 1), column, 0.0), axis=0, keepdims=True)


def column_of(row, size):
    return jnp.sum(jnp.where(iota((size, size), 0) == iota((size, size), 1), row, 0.0), axis=1, keepdims=True)


def normalise(values):
    centre = values - jnp.mean(values, axis=-1, keepdims=True)
    spread = jnp.mean(centre * centre, axis=-1, keepdims=True)
    scale = lax.rsqrt(spread + EPSILON)
    return centre * scale, scale


def norm_backward(grad, gain, xhat, scale):
    scaled = grad * gain
    along = jnp.mean(scaled * xhat, axis=-1, keepdims=True)
    return scale * (scaled - jnp.mean(scaled, axis=-1, keepdims=True) - xhat * along)


def assign_stage(routes, level, capacity, padded):
    rows = routes.shape[0]
    level_row = level.astype(F32)
    level_column = column_of(level_row, rows)
    me, other = iota((rows, rows), 0), iota((rows, rows), 1)
    ahead = (level_row > level_column) | ((level_row == level_column) & (other < me))
    lane = iota((rows, 128), 1)
    first, second = routes[:, 0:1], routes[:, 1:2]
    wants = jnp.where((lane == first) | (lane == second + 64), 1.0, 0.0)
    count = mm(jnp.where(ahead, 1.0, 0.0).astype(BF16), wants.astype(BF16))
    total = jnp.sum(wants, axis=0, keepdims=True)
    rank_one = jnp.sum(jnp.where(lane == first, count, 0.0), axis=1, keepdims=True)
    rank_two = jnp.sum(
        jnp.where(lane == second + 64, count, 0.0) + jnp.where(lane == second, total, 0.0),
        axis=1,
        keepdims=True,
    )
    slot_one = jnp.where(rank_one < capacity, first.astype(F32) * padded + rank_one, -1.0)
    slot_two = jnp.where(rank_two < capacity, second.astype(F32) * padded + rank_two, -1.0)
    return slot_one, slot_two


def batch_of(experts, padded):
    best = 1
    for count in range(1, experts + 1):
        if experts % count == 0 and count * padded <= 256 and (count * padded) % 16 == 0:
            best = count
    return best


def spread_stage(values_ref, slots_ref, target_ref, extra=None):
    rows, width = values_ref.shape
    experts, padded = target_ref.shape[0], target_ref.shape[1]
    batch = batch_of(experts, padded)

    def step(index, _):
        slots = slots_ref[...].astype(F32)
        one, two = [row_of(slots[:, k : k + 1], rows).astype(jnp.int32) for k in range(2)]
        start = index * batch
        here = iota((batch * padded, rows), 0) + start * padded
        pick = jnp.where((here == one) | (here == two), 1.0, 0.0).astype(BF16)
        block = mm(pick, values_ref[...]).reshape(batch, padded, width)
        if extra is not None:
            block = jnp.stack([extra(start + inner, block[inner]) for inner in range(batch)])
        target_ref[pl.ds(start, batch)] = block.astype(BF16)
        return 0

    lax.fori_loop(0, experts // batch, step, 0)


def with_rows(block, first_row, rows):
    place = iota(block.shape, 0)
    for step, row in enumerate(rows):
        wide = jnp.concatenate([row, jnp.zeros((1, block.shape[1] - row.shape[1]), F32)], axis=1)
        block = jnp.where(place == first_row + step, wide, block)
    return block


def pieces(value, count):
    parts = []
    for _ in range(count):
        part = value.astype(BF16).astype(F32)
        parts.append(part)
        value = value - part
    return parts


def bias_stage(lengths_ref, m, rows, store):
    own_start = lax.axis_index("seq") * rows
    span = lax.axis_size("seq") * rows
    ends = []
    total = 0
    for step in range(lengths_ref.shape[1]):
        total = total + lengths_ref[m, step]
        ends.append(total)

    def documents(place):
        found = jnp.zeros(place.shape, jnp.int32)
        for end in ends:
            found = found + jnp.where(place >= end, 1, 0)
        return found

    asked = documents(iota((1, rows), 1) + own_start)
    for half in range(2):
        start = own_start if half == 0 else span - rows - own_start
        held = documents(iota((rows, 1), 0) + start)
        store(half, jnp.where(held == asked, 0.0, -1e30))


def gates_of(logits, routes):
    lane = iota(logits.shape, 1)
    chosen = [
        jnp.sum(jnp.where(lane == routes[:, k : k + 1] + ROUTER_ROW, logits, 0.0), axis=1, keepdims=True)
        for k in range(2)
    ]
    peak = jnp.maximum(*chosen)
    raised = [jnp.exp(part - peak) for part in chosen]
    total = raised[0] + raised[1]
    return raised[0] / total, raised[1] / total


def phi_terms(hidden):
    size = jnp.abs(hidden)
    bell = jnp.exp(hidden * hidden * -0.5)
    t = 1.0 / (1.0 + 0.23164188828 * size)
    tail = t * (
        0.127414796
        + t * (-0.142248368 + t * (0.7107068705 + t * (-0.7265760135 + t * 0.5307027145)))
    )
    tail = tail * bell
    return jnp.where(hidden >= 0, 1.0 - tail, tail), bell


def gather_stage(blocks_ref, slots, weights, padded):
    experts, _, width = blocks_ref.shape
    rows = slots.shape[0]
    batch = batch_of(experts, padded)
    place = iota((rows, batch * padded), 1)
    totals = [jnp.zeros((rows, width), F32) for _ in weights]
    for start in range(0, experts, batch):
        block = (
            blocks_ref[start : start + batch].astype(F32).reshape(batch * padded, width).astype(BF16)
        )
        here = place + start * padded
        for index, chosen in enumerate(weights):
            hit = slots[:, chosen[0] : chosen[0] + 1] == here
            for k in chosen[1:]:
                hit = hit | (slots[:, k : k + 1] == here)
            totals[index] = totals[index] + mm(jnp.where(hit, 1.0, 0.0).astype(BF16), block)
    return totals


MESH = pl.DeviceIdType.MESH
ANY = pl.BlockSpec(memory_space=pl.ANY)

def remote(source, target, sends, arrives, device):
    return pltpu.make_async_remote_copy(
        src_ref=source,
        dst_ref=target,
        send_sem=sends,
        recv_sem=arrives,
        device_id=device,
        device_id_type=MESH,
    )


def greet(axes):
    barrier = pltpu.get_barrier_semaphore()
    count = 0
    for axis in axes:
        size, me = lax.axis_size(axis), lax.axis_index(axis)
        for step in range(1, size):
            pl.semaphore_signal(
                barrier, inc=1, device_id={axis: lax.rem(me + step, size)}, device_id_type=MESH
            )
            count += 1
    pl.semaphore_wait(barrier, count)


class Exchange:
    def __init__(self, source, target, sems, index):
        self.refs, self.index = (source, target, sems), index

    def copies(self):
        source, target, sems = self.refs
        size, me = lax.axis_size("exp"), lax.axis_index("exp")
        found = []
        for step in range(1, size):
            peer = lax.rem(me + step, size)
            found.append(
                remote(
                    source.at[peer],
                    target.at[me],
                    sems.at[self.index, 0, step],
                    sems.at[self.index, 1, step],
                    {"exp": peer},
                )
            )
        return found

    def own(self):
        source, target, sems = self.refs
        me = lax.axis_index("exp")
        return pltpu.make_async_copy(source.at[me], target.at[me], sems.at[self.index, 0, 0])

    def start(self):
        for copy in self.copies():
            copy.start()
        self.own().start()

    def arrived(self):
        for copy in self.copies():
            copy.wait_recv()
        self.own().wait()

    def sent(self):
        for copy in self.copies():
            copy.wait_send()


def project(low, weight_ref, parts, store):
    width = low.shape[1]
    for part in parts:
        block = mm(low, weight_ref[:, part * width : (part + 1) * width]).astype(BF16)
        for index in range(width // 128):
            store(part, index, block[:, index * 128 : (index + 1) * 128])


def attend_stage(query_ref, pair_ref, bias_ref, attended_ref, stats_ref):
    couples, rows, couple = query_ref.shape
    head_dim = couple // 2
    low_lane = iota((1, couple), 1) < head_dim

    def step(index, _):
        query = query_ref[index].astype(F32) * head_dim**-0.5
        keys = [pair_ref[half, 2 * index] for half in range(2)]
        values = [pair_ref[half, 2 * index + 1].astype(F32).T.astype(BF16) for half in range(2)]
        outs = []
        for head in range(2):
            mine = jnp.where(low_lane == (head == 0), query, 0.0).astype(BF16)
            scores = [mm_nt(keys[half], mine) + bias_ref[half] for half in range(2)]
            peak = jnp.maximum(*[jnp.max(part, axis=0, keepdims=True) for part in scores])
            raised = [jnp.exp(part - peak) for part in scores]
            total = sum(jnp.sum(part, axis=0, keepdims=True) for part in raised)
            here = slice(head * head_dim, (head + 1) * head_dim)
            summed = sum(mm(values[half][here], raised[half].astype(BF16)) for half in range(2))
            outs.append(summed / total)
            stats_ref[pl.ds(index * 2 + head, 1), :] = peak + jnp.log(total)
        lanes = pl.ds(pl.multiple_of(index * couple, couple), couple)
        attended_ref[:, lanes] = jnp.concatenate(outs, axis=0).T.astype(BF16)
        return 0

    lax.fori_loop(0, couples, step, 0)


def flatten_stage(rows_ref, cot_ref, x, g, capacity):
    experts, padded, width = rows_ref.shape
    batch = batch_of(experts, padded)
    flat = batch * padded

    def step(index, _):
        place, lane = iota((padded, 128), 0), iota((padded, 128), 1)
        inside = (place == capacity) | (place == capacity + 1)
        block = rows_ref[pl.ds(index * batch, batch)].astype(F32)
        cot = cot_ref[pl.ds(index * batch, batch)].astype(F32)
        here = pl.ds(pl.multiple_of(index * flat, 16), flat)
        x[here, :] = block.reshape(flat, width).astype(BF16)
        scaled = []
        for inner in range(batch):
            gate_row = jnp.sum(jnp.where(inside, block[inner][:, 0:128], 0.0), axis=0, keepdims=True)
            gate = jnp.sum(jnp.where(place == lane, gate_row, 0.0), axis=1, keepdims=True)
            scaled.append(cot[inner] * gate)
        g[here, :] = jnp.stack(scaled).reshape(flat, width).astype(BF16)
        return 0

    lax.fori_loop(0, experts // batch, step, 0)


def expert_step(x, g, y, dx, up, down):
    hidden = mm(x[...], up)
    active_grad = mm_nt(g[...], down)
    phi, bell = phi_terms(hidden)
    active = (hidden * phi).astype(BF16)
    hidden_grad = (active_grad * (phi + hidden * bell * 0.3989422804)).astype(BF16)
    y[...] += mm(active, down)
    dx[...] += mm_nt(hidden_grad, up)
    return active, hidden_grad


def finish_stage(cot_ref, y, dx, back_ref, grads_ref, capacity):
    experts, padded, width = cot_ref.shape
    batch = batch_of(experts, padded)
    flat = batch * padded

    def step(index, _):
        place, lane = iota((padded, 128), 0), iota((padded, 128), 1)
        here = pl.ds(pl.multiple_of(index * flat, 16), flat)
        there = pl.ds(index * batch, batch)
        produced = y[here, :].reshape(batch, padded, width).astype(BF16)
        back_ref[there] = produced
        cot = cot_ref[there].astype(F32)
        along = jnp.sum(cot * produced.astype(F32), axis=-1, keepdims=True)
        grads = dx[here, :].reshape(batch, padded, width)
        parts = []
        for inner in range(batch):
            row = jnp.sum(jnp.where(place == lane, along[inner], 0.0), axis=0, keepdims=True)
            parts.append(with_rows(grads[inner], capacity, pieces(row, 3)))
        grads_ref[there] = jnp.stack(parts).astype(BF16)
        return 0

    lax.fori_loop(0, experts // batch, step, 0)


class Backward:
    def __init__(self, m, fresh, capacity, padded, **refs):
        self.m, self.fresh, self.capacity, self.padded = m, fresh, capacity, padded
        self.__dict__.update(refs)
        self.saved = []

    def gain(self, row):
        return self.pack[row : row + 1].astype(F32)

    def store(self, start, value):
        here = slice(start, start + value.shape[1])
        value = value.reshape(2, 16, value.shape[0] // 32, value.shape[1])
        if self.stage is None:
            self.dense[:, :, :, here] = self.dense[:, :, :, here] + value
            return
        parts = [slice(0, value.shape[3])]
        if start > 0:
            side = len(self.saved) % 2
            parts = [slice(side * value.shape[3], (side + 1) * value.shape[3])]
            if len(self.saved) > 2:
                self.save(len(self.saved) - 2).wait()
            elif len(self.saved) == 1:
                self.save(0).wait()
        self.saved.append((parts[0], here))
        self.stage[:, :, :, parts[0]] = value
        self.save(len(self.saved) - 1).start()

    def save(self, index):
        source, target = self.saved[index]
        return pltpu.make_async_copy(
            self.stage.at[:, :, :, source],
            self.dense.at[:, :, :, target],
            self.save_sems.at[index % 2],
        )

    def drain(self):
        for index in (len(self.saved) - 2, len(self.saved) - 1):
            self.save(index).wait()

    def before(self):
        grads, capacity, padded = self.grads, self.capacity, self.padded
        rows = self.tokens.shape[0]
        couples, _, couple = self.query.shape

        def store_bias(half, block):
            self.bias[half] = block

        bias_stage(self.lengths, self.m, rows, store_bias)
        slots, gates = self.slots[...], self.gates[...]
        routes = slots[:, 2:4]
        pack = self.pack[...]
        batch = batch_of(grads.shape[0], padded)
        flat = batch * padded
        place, lane = iota((padded, 128), 0), iota((padded, 128), 1)
        inside = (place >= capacity) & (place < capacity + 3)
        wide_lane, here = iota((flat, 128), 1), iota((rows, flat), 1)
        moe_grad = 0.0
        found = [0.0, 0.0]
        for start in range(0, grads.shape[0], batch):
            block = grads[start : start + batch].astype(F32)
            columns = []
            for inner in range(batch):
                row = jnp.sum(
                    jnp.where(inside, block[inner][:, 0:128], 0.0), axis=0, keepdims=True
                )
                columns.append(
                    jnp.sum(jnp.where(place == lane, row, 0.0), axis=1, keepdims=True)
                )
            column = jnp.stack(columns).reshape(flat, 1)
            spread = 0.0
            for index, piece in enumerate(pieces(column, 3)):
                spread = spread + jnp.where(wide_lane == index, piece, 0.0)
            spread = spread.astype(BF16)
            hits = [slots[:, k : k + 1] - start * padded == here for k in range(2)]
            for k in range(2):
                found[k] = found[k] + mm(jnp.where(hits[k], 1.0, 0.0).astype(BF16), spread)
            pick = jnp.where(hits[0] | hits[1], 1.0, 0.0).astype(BF16)
            moe_grad = moe_grad + mm(pick, block.reshape(flat, block.shape[2]).astype(BF16))
        gate_grad = [jnp.sum(part, axis=1, keepdims=True) for part in found]
        gate = [gates[:, k : k + 1] for k in range(2)]
        inner = gate[0] * gate_grad[0] + gate[1] * gate_grad[1]
        pack_lane = iota((rows, pack.shape[0]), 1)
        logit_grad = sum(
            jnp.where(
                pack_lane == routes[:, k : k + 1] + ROUTER_ROW,
                gate[k] * (gate_grad[k] - inner),
                0.0,
            )
            for k in range(2)
        )
        parts = [part.astype(BF16) for part in pieces(logit_grad, 3)]
        moe_grad = moe_grad + sum(mm(part, pack) for part in parts)
        router_grad = sum(mm_tn(part, self.moe[...]) for part in parts)
        xhat, scale = normalise(self.residual[...])
        small_row = iota(router_grad.shape, 0)
        terms = jnp.where(
            small_row == 2,
            jnp.sum(moe_grad * xhat, axis=0, keepdims=True),
            jnp.where(small_row == 3, jnp.sum(moe_grad, axis=0, keepdims=True), router_grad),
        )
        self.small[...] = terms if self.fresh else self.small[...] + terms
        total = self.cot[...].astype(F32) + norm_backward(moe_grad, self.gain(2), xhat, scale)
        self.residual_grad[...] = total
        branch = total.astype(BF16)
        self.store(0, mm_tn(self.attended[...], branch))
        turned = mm_nt(branch, self.wo[...]).astype(BF16)
        for index in range(couples):
            self.attended_grad[index] = turned[:, index * couple : (index + 1) * couple]
        for half, ref in enumerate((self.tokens, self.token_other)):
            self.low[half * rows : (half + 1) * rows] = (
                normalise(ref[...].astype(F32))[0] * self.gain(0) + self.gain(1)
            ).astype(BF16)

    def heads(self, begin, end):
        rows, width = self.tokens.shape
        couple = self.query.shape[2]
        head_dim = couple // 2
        low_lane = iota((1, couple), 1) < head_dim
        query, pair, bias, packed = self.query, self.pair, self.bias, self.packed

        def step(index, _):
            asked = query[index].astype(F32) * head_dim**-0.5
            grad_low = self.attended_grad[index]
            grad = grad_low.astype(F32)
            asked_low = asked.astype(BF16)
            keys = [pair[half, 2 * index] for half in range(2)]
            values = [pair[half, 2 * index + 1] for half in range(2)]
            keys_turned = [part.astype(F32).T.astype(BF16) for part in keys]
            key_grads, value_grads, query_grads = [[], []], [[], []], []
            for head in range(2):
                chosen = low_lane == (head == 0)
                mine = jnp.where(chosen, asked, 0.0).astype(BF16)
                mine_grad = jnp.where(chosen, grad, 0.0).astype(BF16)
                stats = self.stats[pl.ds(index * 2 + head, 1), :]
                weighting = [
                    jnp.exp(mm_nt(keys[half], mine) + bias[half] - stats) for half in range(2)
                ]
                weighting_grad = [mm_nt(values[half], mine_grad) for half in range(2)]
                delta = sum(
                    jnp.sum(weighting[half] * weighting_grad[half], axis=0, keepdims=True)
                    for half in range(2)
                )
                here = slice(head * head_dim, (head + 1) * head_dim)
                query_total = 0.0
                for half in range(2):
                    scores_grad = (weighting[half] * (weighting_grad[half] - delta)).astype(BF16)
                    value_grads[half].append(mm(weighting[half].astype(BF16), grad_low))
                    key_grads[half].append(mm(scores_grad, asked_low))
                    query_total = query_total + mm(keys_turned[half][here], scores_grad)
                query_grads.append(query_total * head_dim**-0.5)

            def lanes(part):
                return pl.ds(pl.multiple_of(part * width + index * couple, couple), couple)

            packed[0:rows, lanes(0)] = jnp.concatenate(query_grads, axis=0).T.astype(BF16)
            for half in range(2):
                here = slice(half * rows, (half + 1) * rows)
                packed[here, lanes(1)] = jnp.where(low_lane, *key_grads[half]).astype(BF16)
                packed[here, lanes(2)] = jnp.where(low_lane, *value_grads[half]).astype(BF16)
            return 0

        lax.fori_loop(begin, end, step, 0)

    def project_grads(self, group):
        rows, width = self.tokens.shape
        third = width // 2
        for part in range(3):
            tall = rows if part == 0 else 2 * rows
            source = slice(part * width + group * third, part * width + (group + 1) * third)
            value = mm_tn(self.low[0:tall], self.packed[0:tall, source])
            self.store(width + (3 * group + part) * third, value)

    def firsts(self):
        rows, width = self.tokens.shape
        packed, wi = self.packed, self.wi
        own = mm_nt(packed[0:rows, 0:width], wi[:, 0:width])
        other = 0.0
        for part in range(1, 3):
            here = slice(part * width, (part + 1) * width)
            own = own + mm_nt(packed[0:rows, here], wi[:, here])
            other = other + mm_nt(packed[rows:, here], wi[:, here])
        self.other_grad[...] = other.astype(BF16)
        self.first_grad[...] = own
        own_hat = normalise(self.tokens[...].astype(F32))[0]
        other_hat = normalise(self.token_other[...].astype(F32))[0]
        gain_grad = jnp.sum(own * own_hat + other * other_hat, axis=0, keepdims=True)
        shift_grad = jnp.sum(own + other, axis=0, keepdims=True)
        row = iota(self.small.shape, 0)
        self.small[...] = self.small[...] + jnp.where(
            row == 0, gain_grad, jnp.where(row == 1, shift_grad, 0.0)
        )


def forward_kernel(
    capacity,
    tokens_ref,
    cot_ref,
    routes_ref,
    priority_ref,
    lengths_ref,
    pack_own,
    in_own,
    out_own,
    up_own,
    down_own,
    pack_out,
    in_out,
    out_out,
    in_half,
    out_half,
    token_out,
    query_out,
    pair_out,
    residual_out,
    moe_out,
    attended_out,
    stats_out,
    gates_out,
    slots_out,
    back_out,
    grads_out,
    up_old,
    down_old,
    up_sum,
    down_sum,
    up_arrived,
    down_arrived,
    small_out,
    residual_grad_out,
    first_grad_out,
    other_grad_out,
    dense_out,
    pk,
    up,
    down,
    token_other,
    cot_send,
    row_send,
    cot_got,
    row_got,
    up_got,
    down_got,
    all_sems,
    weight_sems,
    token_sems,
    out_sems,
    chunk_sems,
    past_sems,
    low_sems,
    got_sems,
    cross_sems,
    load_sems,
    save_sems,
):
    micro_count, rows, width = tokens_ref.shape
    experts, padded = cot_send.shape[1], cot_send.shape[2]
    flat = experts * padded
    core, half_seq = lax.axis_index("dp"), lax.axis_index("seq")
    partner = {"dp": 1 - core}
    across = {"seq": 1 - half_seq}
    greet(("seq", "exp", "dp"))

    token_copies = [
        remote(
            tokens_ref.at[m], token_other.at[m], token_sems.at[m, 0], token_sems.at[m, 1], across
        )
        for m in range(micro_count)
    ]
    weights = []
    for index, (own, full) in enumerate(
        ((pack_own, pk), (in_own, in_half), (out_own, out_half), (up_own, up), (down_own, down))
    ):
        size = own.shape[0]
        whole_there = index in (1, 2)
        place = full.at[core] if index == 0 else full.at[pl.ds(core * size, size)]
        weights.append(
            (
                remote(
                    own,
                    full if whole_there else place,
                    weight_sems.at[index, 0],
                    weight_sems.at[index, 1],
                    partner,
                ),
                None if whole_there else pltpu.make_async_copy(own, place, weight_sems.at[index, 2]),
            )
        )
    token_copies[0].start()
    weights[0][1].start()
    for index in range(3):
        weights[index][0].start()
    token_copies[1].start()
    for index in range(3, 5):
        weights[index][0].start()
        weights[index][1].start()

    def have(index):
        weights[index][0].wait_recv()
        if weights[index][1] is not None:
            weights[index][1].wait()

    cots = [Exchange(cot_send.at[m], cot_got.at[m], all_sems, m) for m in range(micro_count)]
    rowses = [Exchange(row_send.at[m], row_got.at[m], all_sems, 2 + m) for m in range(micro_count)]
    gradses = [Exchange(cot_send.at[m], grads_out.at[m], all_sems, 4 + m) for m in range(micro_count)]
    lane_two, lane_four = iota((rows, 2), 1), iota((rows, 4), 1)

    def claim(m):
        one, two = assign_stage(routes_ref[m], priority_ref[m], capacity, padded)
        routes = routes_ref[m]
        found = jnp.where(lane_four == 0, one, two).astype(jnp.int32)
        chosen = jnp.where(lane_four == 2, routes[:, 0:1], routes[:, 1:2])
        slots_out[m] = jnp.where(lane_four < 2, found, chosen)
        spread_stage(cot_ref.at[m], slots_out.at[m], cot_send.at[m])

    used = [0]

    def keep(refs, later):
        index = used[0]
        used[0] += 1

        def copy():
            source, target = refs()
            return pltpu.make_async_copy(source, target, out_sems.at[index])

        copy().start()
        later.append(copy)

    late = []
    claim(0)
    cots[0].start()
    have(0)
    pack_out[...] = jnp.concatenate([pk[0], pk[1]], axis=1)

    def gain(row):
        return pack_out[row : row + 1].astype(F32)

    def first_norm(values):
        return (normalise(values.astype(F32))[0] * gain(0) + gain(1)).astype(BF16)

    def attention_phase(query, pair, bias, residual, moe, attended, wi, wo):
        half = width // 2
        weight_loads = []
        for index, (own, got, full) in enumerate(((in_own, in_half, wi), (out_own, out_half, wo))):
            mine, theirs = [full.at[pl.ds(place * half, half)] for place in (core, 1 - core)]
            weight_loads.append(
                (
                    pltpu.make_async_copy(own, mine, load_sems.at[2 * index]),
                    pltpu.make_async_copy(got, theirs, load_sems.at[2 * index + 1]),
                )
            )
            weight_loads[index][0].start()

        def project_own(m):
            def store(part, index, block):
                if part == 0:
                    query[m, index] = block
                else:
                    pair[m, 0, 2 * index + part - 1] = block

            project(first_norm(tokens_ref[m]), wi, range(3), store)

        def project_other(m):
            def store(part, index, block):
                pair[m, 1, 2 * index + part - 1] = block

            project(first_norm(token_other[m]), wi, range(1, 3), store)

        have(1)
        weight_loads[0][1].start()
        weight_loads[0][1].wait()
        weight_loads[0][0].wait()
        for m in range(micro_count):
            project_own(m)
        claim(1)
        have(2)
        weight_loads[1][1].start()
        weight_loads[1][1].wait()
        weight_loads[1][0].wait()
        outs, local = [], []
        keep(lambda: (wi, in_out), outs)
        keep(lambda: (wo, out_out), outs)
        for m in range(micro_count):
            token_copies[m].wait_recv()
            project_other(m)
            keep(lambda m=m: (token_other.at[m], token_out.at[m]), late)
            keep(lambda m=m: (query.at[m], query_out.at[m]), outs)
            keep(lambda m=m: (pair.at[m], pair_out.at[m]), outs)

            def store_bias(half, block):
                bias[half] = block

            bias_stage(lengths_ref, m, rows, store_bias)
            for copy in local:
                copy().wait()
            attend_stage(query.at[m], pair.at[m], bias, attended, stats_out.at[m])
            summed = tokens_ref[m].astype(F32) + mm(attended[...], wo[...])
            residual[...] = summed
            moe_input = (normalise(summed)[0] * gain(2) + gain(3)).astype(BF16)
            moe[...] = moe_input
            gates = gates_of(mm_nt(moe_input, pack_out[...]), routes_ref[m])
            gates_out[m] = jnp.where(lane_two == 0, gates[0], gates[1])

            def gate_rows(expert, block):
                slots, gates = slots_out[m], gates_out[m]
                place = iota((rows, 128), 1)
                row = sum(
                    jnp.where(
                        slots[:, k : k + 1] - expert * padded == place, gates[:, k : k + 1], 0.0
                    )
                    for k in range(2)
                )
                return with_rows(block, capacity, pieces(jnp.sum(row, axis=0, keepdims=True), 2))

            spread_stage(moe, slots_out.at[m], row_send.at[m], gate_rows)
            rowses[m].start()
            if m == 0:
                cots[1].start()
            local = []
            keep(lambda m=m: (residual, residual_out.at[m]), local)
            keep(lambda m=m: (moe, moe_out.at[m]), local)
            keep(lambda m=m: (attended, attended_out.at[m]), local)
        for copy in outs + local:
            copy().wait()

    pl.run_scoped(
        attention_phase,
        pltpu.VMEM((micro_count, width // 128, rows, 128), BF16),
        pltpu.VMEM((micro_count, 2, width // 64, rows, 128), BF16),
        pltpu.VMEM((2, rows, rows), F32),
        pltpu.VMEM((rows, width), F32),
        pltpu.VMEM((rows, width), BF16),
        pltpu.VMEM((rows, width), BF16),
        pltpu.VMEM((width, 3 * width), BF16),
        pltpu.VMEM((width, width), BF16),
    )
    have(3)
    have(4)
    chunks, _, chunk = up_old.shape
    half_chunks = chunks // 2
    half_rows = width // 2

    def span(i):
        return pl.ds(pl.multiple_of(i * chunk, chunk), chunk)

    def own_columns():
        return pl.ds(pl.multiple_of(core * half_rows, 128), half_rows)

    def other_columns():
        return pl.ds(pl.multiple_of((1 - core) * half_rows, 128), half_rows)

    def mine(i):
        return lax.div(i, half_chunks) == core

    def cross(i):
        return remote(
            up_sum.at[:, span(i)],
            up_arrived.at[:, span(i)],
            cross_sems.at[i, 0],
            cross_sems.at[i, 1],
            across,
        )

    early = half_chunks // 2

    def cross_down(i):
        return remote(
            down_sum.at[span(i)],
            down_arrived.at[span(i)],
            cross_sems.at[chunks + i, 0],
            cross_sems.at[chunks + i, 1],
            across,
        )

    def expert_phase(x, g, active, hidden):
        def expert(m):
            cots[m].arrived()
            rowses[m].arrived()
            flatten_stage(row_got.at[m], cot_got.at[m], x, g, capacity)

            def passes(y, dx):
                y[...] = jnp.zeros_like(y)
                dx[...] = jnp.zeros_like(dx)

                def step(i, _):
                    active[i], hidden[i] = expert_step(
                        x, g, y, dx, up[:, span(i)], down[span(i), :]
                    )
                    return 0

                lax.fori_loop(0, chunks, step, 0)
                cots[m].sent()
                rowses[m].sent()
                finish_stage(cot_got.at[m], y, dx, row_send.at[m], cot_send.at[m], capacity)

            pl.run_scoped(passes, pltpu.VMEM((flat, width), F32), pltpu.VMEM((flat, width), F32))
            gradses[m].start()
            keep(lambda m=m: (row_send.at[m], back_out.at[m]), late)

        def first_weights(up_buf, down_buf):
            def chunk_out(slot, i):
                return (
                    pltpu.make_async_copy(up_buf.at[slot], up_old.at[i], chunk_sems.at[slot, 0]),
                    pltpu.make_async_copy(down_buf.at[slot], down_old.at[i], chunk_sems.at[slot, 1]),
                )

            def step(i, _):
                slot = lax.rem(i, 2)

                @pl.when(i >= 2)
                def _():
                    for copy in chunk_out(slot, i - 2):
                        copy.wait()

                up_buf[slot] = mm_tn(x[...], hidden[i])
                down_buf[slot] = mm_tn(active[i], g[...])
                for copy in chunk_out(slot, i):
                    copy.start()
                return 0

            lax.fori_loop(0, chunks, step, 0)
            for i in range(chunks - 2, chunks):
                for copy in chunk_out(i % 2, i):
                    copy.wait()

        def second_weights(
            up_past, down_past, up_ring, down_ring, up_low, down_low, up_total, down_total
        ):
            def past(slot, i):
                return (
                    pltpu.make_async_copy(up_old.at[i], up_past.at[slot], past_sems.at[slot, 0]),
                    pltpu.make_async_copy(down_old.at[i], down_past.at[slot], past_sems.at[slot, 1]),
                )

            def up_given(i):
                slot = lax.rem(i, 2)
                return remote(
                    up_low.at[slot], up_got.at[i], low_sems.at[slot, 0], got_sems.at[0, i], partner
                )

            def down_given(i):
                slot, place = lax.rem(i, 2), lax.rem(i, half_chunks)
                return remote(
                    down_low.at[slot],
                    down_got.at[place],
                    low_sems.at[slot, 1],
                    got_sems.at[1, place],
                    partner,
                )

            def up_store(i):
                slot = lax.rem(i, 2)
                return pltpu.make_async_copy(
                    up_total.at[slot], up_sum.at[:, span(i)], chunk_sems.at[slot, 0]
                )

            def down_store(i):
                slot = lax.rem(i, 2)
                return pltpu.make_async_copy(
                    down_total.at[slot],
                    down_sum.at[span(lax.rem(i, half_chunks))],
                    chunk_sems.at[slot, 1],
                )

            for copy in past(0, 0):
                copy.start()

            def step(i, _):
                slot, ring = lax.rem(i, 2), lax.rem(i, 3)

                @pl.when(i >= 3)
                def _():
                    up_store(i - 3).wait()
                    cross(i - 3).start()

                    @pl.when(mine(i - 3))
                    def _():
                        down_store(i - 3).wait()

                        @pl.when(lax.rem(i - 3, half_chunks) < early)
                        def _():
                            cross_down(lax.rem(i - 3, half_chunks)).start()

                @pl.when(i + 1 < chunks)
                def _():
                    for copy in past(1 - slot, i + 1):
                        copy.start()

                @pl.when(i < chunks)
                def _():
                    @pl.when(i >= 2)
                    def _():
                        up_given(i - 2).wait_send()

                        @pl.when(jnp.logical_not(mine(i - 2)))
                        def _():
                            down_given(i - 2).wait_send()

                    for copy in past(slot, i):
                        copy.wait()
                    low = mm_tn(x[:, other_columns()], hidden[i])
                    low = low + up_past[slot, other_columns(), :]
                    up_low[slot] = low.astype(BF16)
                    up_given(i).start()
                    kept = mm_tn(x[:, own_columns()], hidden[i])
                    up_ring[ring] = kept + up_past[slot, own_columns(), :]
                    down_grad = mm_tn(active[i], g[...]) + down_past[slot]

                    @pl.when(mine(i))
                    def _():
                        down_ring[ring] = down_grad

                    @pl.when(jnp.logical_not(mine(i)))
                    def _():
                        down_low[slot] = down_grad.astype(BF16)
                        down_given(i).start()

                @pl.when((i >= 2) & (i < chunks + 2))
                def _():
                    last = i - 2
                    up_given(last).wait_recv()
                    total = up_ring[lax.rem(last, 3)] + up_got[last].astype(F32)
                    up_total[slot] = total.astype(BF16)
                    up_store(last).start()

                    @pl.when(mine(last))
                    def _():
                        down_given(last).wait_recv()
                        total = down_ring[lax.rem(last, 3)] + down_got[
                            lax.rem(last, half_chunks)
                        ].astype(F32)
                        down_total[slot] = total.astype(BF16)
                        down_store(last).start()

                return 0

            lax.fori_loop(0, chunks + 3, step, 0)
            for i in range(chunks - 2, chunks):
                up_given(i).wait_send()

                @pl.when(jnp.logical_not(mine(i)))
                def _():
                    down_given(i).wait_send()

        expert(0)
        pl.run_scoped(
            first_weights,
            pltpu.VMEM((2, width, chunk), F32),
            pltpu.VMEM((2, chunk, width), F32),
        )
        expert(1)
        pl.run_scoped(
            second_weights,
            pltpu.VMEM((2, width, chunk), F32),
            pltpu.VMEM((2, chunk, width), F32),
            pltpu.VMEM((3, half_rows, chunk), F32),
            pltpu.VMEM((3, chunk, width), F32),
            pltpu.VMEM((2, half_rows, chunk), BF16),
            pltpu.VMEM((2, chunk, width), BF16),
            pltpu.VMEM((2, half_rows, chunk), BF16),
            pltpu.VMEM((2, chunk, width), BF16),
        )

    pl.run_scoped(
        expert_phase,
        pltpu.VMEM((flat, width), BF16),
        pltpu.VMEM((flat, width), BF16),
        pltpu.VMEM((chunks, flat, chunk), BF16),
        pltpu.VMEM((chunks, flat, chunk), BF16),
    )

    def back_phase(
        grads,
        moe,
        attended,
        query,
        pair,
        residual,
        bias,
        attended_grad,
        packed,
        low,
        residual_grad,
        first_grad,
        other_grad,
        stage,
        wi,
        wo,
    ):
        gradses[0].arrived()
        loads = [
            pltpu.make_async_copy(source.at[0] if index < 6 else source, target, load_sems.at[index])
            for index, (source, target) in enumerate(
                (
                    (grads_out, grads),
                    (moe_out, moe),
                    (attended_out, attended),
                    (residual_out, residual),
                    (query_out, query),
                    (pair_out, pair),
                    (in_out, wi),
                    (out_out, wo),
                )
            )
        ]
        for copy in loads:
            copy.start()
        for copy in loads:
            copy.wait()
        item = Backward(
            0,
            True,
            capacity,
            padded,
            pack=pack_out,
            dense=dense_out,
            stage=stage,
            save_sems=save_sems,
            grads=grads,
            tokens=tokens_ref.at[0],
            token_other=token_other.at[0],
            query=query,
            pair=pair,
            bias=bias,
            lengths=lengths_ref,
            slots=slots_out.at[0],
            gates=gates_out.at[0],
            moe=moe,
            residual=residual,
            small=small_out,
            cot=cot_ref.at[0],
            residual_grad=residual_grad,
            attended=attended,
            attended_grad=attended_grad,
            wo=wo,
            wi=wi,
            low=low,
            packed=packed,
            stats=stats_out.at[0],
            first_grad=first_grad,
            other_grad=other_grad,
        )
        item.before()
        item.heads(0, query.shape[0])
        item.project_grads(0)
        item.project_grads(1)
        item.firsts()
        saves = [
            pltpu.make_async_copy(source, target, load_sems.at[index])
            for index, (source, target) in enumerate(
                (
                    (residual_grad, residual_grad_out),
                    (first_grad, first_grad_out),
                    (other_grad, other_grad_out),
                )
            )
        ]
        for copy in saves:
            copy.start()
        for copy in saves:
            copy.wait()
        item.drain()

    pl.run_scoped(
        back_phase,
        pltpu.VMEM((experts, padded, width), BF16),
        pltpu.VMEM((rows, width), BF16),
        pltpu.VMEM((rows, width), BF16),
        pltpu.VMEM((width // 128, rows, 128), BF16),
        pltpu.VMEM((2, width // 64, rows, 128), BF16),
        pltpu.VMEM((rows, width), F32),
        pltpu.VMEM((2, rows, rows), F32),
        pltpu.VMEM((width // 128, rows, 128), BF16),
        pltpu.VMEM((2 * rows, 3 * width), BF16),
        pltpu.VMEM((2 * rows, width), BF16),
        pltpu.VMEM((rows, width), F32),
        pltpu.VMEM((rows, width), F32),
        pltpu.VMEM((rows, width), BF16),
        pltpu.VMEM((2, 16, width // 32, width), F32),
        pltpu.VMEM((width, 3 * width), BF16),
        pltpu.VMEM((width, width), BF16),
    )
    gradses[1].arrived()
    for m in range(micro_count):
        token_copies[m].wait_send()
        gradses[m].sent()
    for index in range(5):
        weights[index][0].wait_send()
    for copy in late:
        copy().wait()

    def crossed(i, _):
        cross(i).wait()
        return 0

    lax.fori_loop(0, chunks, crossed, 0)

    def crossed_down(i, _):
        cross_down(i).wait()
        return 0

    lax.fori_loop(0, early, crossed_down, 0)


class Reduction:
    def __init__(self, index, columns, seq_first, refs):
        self.acc, self.give, self.land, self.give2, self.land2, self.give3, self.land3 = refs[:7]
        self.more_give, self.more_land, self.final, self.sems = refs[7:]
        self.index, self.cols = index, columns
        size, me = lax.axis_size("exp"), lax.axis_index("exp")
        self.size, self.me = size, me
        seq, low = lax.axis_index("seq"), lax.rem(me, 2)
        flip = {"exp": me + 1 - 2 * low}
        across = {"seq": 1 - seq}
        self.first, self.second = (seq, low) if seq_first else (low, seq)
        self.to_first, self.to_second = (across, flip) if seq_first else (flip, across)
        self.turn = lax.rem(lax.div(me, 2), 4)
        self.quad = self.first * 8 + self.second * 4

    def peer(self, step):
        turn = lax.rem(self.turn + step, 4)
        return turn, {"exp": self.me + 2 * (turn - self.turn)}

    def copy(self, step, source, target, device):
        return remote(
            source, target, self.sems.at[self.index, step, 0], self.sems.at[self.index, step, 1], device
        )

    def one(self):
        return self.copy(0, self.give.at[:, :, self.cols], self.land.at[:, :, self.cols], self.to_first)

    def two(self):
        return self.copy(1, self.give2.at[:, :, self.cols], self.land2.at[:, :, self.cols], self.to_second)

    def three(self, step):
        turn, device = self.peer(step)
        return self.copy(
            1 + step, self.give3.at[turn, :, self.cols], self.land3.at[self.turn, :, self.cols], device
        )

    def more(self, step):
        block = 8 << step
        device = {"exp": self.me + block * (1 - 2 * lax.rem(lax.div(self.me, block), 2))}
        return self.copy(
            10 + step, self.more_give.at[step, :, self.cols], self.more_land.at[step, :, self.cols], device
        )

    def four(self, step):
        place = self.final.at[self.quad + self.turn, :, self.cols]
        return self.copy(4 + step, place, place, self.peer(step)[1])

    def five(self):
        place = self.final.at[pl.ds(self.quad, 4), :, self.cols]
        return self.copy(8, place, place, self.to_second)

    def six(self):
        place = self.final.at[pl.ds(self.first * 8, 8), :, self.cols]
        return self.copy(9, place, place, self.to_first)

    def start_one(self):
        self.give[:, :, self.cols] = self.acc[pl.ds((1 - self.first) * 8, 8), :, self.cols].astype(BF16)
        self.one().start()

    def start_two(self):
        self.one().wait_recv()
        mine = pl.ds(self.first * 8, 8)
        self.acc[mine, :, self.cols] = self.acc[mine, :, self.cols] + self.land[
            :, :, self.cols
        ].astype(F32)
        self.give2[:, :, self.cols] = self.acc[
            pl.ds(self.first * 8 + (1 - self.second) * 4, 4), :, self.cols
        ].astype(BF16)
        self.two().start()

    def start_three(self):
        self.two().wait_recv()
        total = self.acc[pl.ds(self.quad, 4), :, self.cols] + self.land2[:, :, self.cols].astype(F32)
        self.acc[pl.ds(self.quad, 4), :, self.cols] = total
        self.give3[:, :, self.cols] = total.astype(BF16)
        for step in range(1, 4):
            self.three(step).start()

    def start_four(self):
        total = self.acc[self.quad + self.turn, :, self.cols]
        for step in range(1, 4):
            self.three(step).wait_recv()
        for step in range(1, 4):
            total = total + self.land3[self.peer(step)[0], :, self.cols].astype(F32)
        steps = (self.size // 8).bit_length() - 1
        for step in range(steps):
            low = total.astype(BF16)
            self.more_give[step, :, self.cols] = low
            copy = self.more(step)
            copy.start()
            copy.wait_recv()
            total = low.astype(F32) + self.more_land[step, :, self.cols].astype(F32)
            copy.wait_send()
        self.final[self.quad + self.turn, :, self.cols] = total.astype(BF16)
        for step in range(1, 4):
            self.four(step).start()

    def start_five(self):
        for step in range(1, 4):
            turn, device = self.peer(step)
            place = self.final.at[self.quad + turn, :, self.cols]
            self.copy(4 + 4 - step, place, place, device).wait_recv()
        self.five().start()

    def start_six(self):
        self.five().wait_recv()
        self.six().start()

    def finish(self):
        self.six().wait_recv()
        self.one().wait_send()
        self.two().wait_send()
        for step in range(1, 4):
            self.three(step).wait_send()
            self.four(step).wait_send()
        self.five().wait_send()
        self.six().wait_send()


def backward_kernel(
    capacity,
    cot_ref,
    slots_ref,
    gates_ref,
    residual_ref,
    stats_ref,
    pack_ref,
    wo,
    wi,
    tokens_ref,
    token_other,
    small_first,
    residual_grad_first,
    first_grad_first,
    lengths_ref,
    other_grad_first,
    dense_first,
    grads_in,
    back_in,
    moe_in,
    attended_in,
    query_in,
    pair_in,
    down_sum,
    _,
    mixed_out,
    tokens_out,
    small_out,
    final_out,
    back_got,
    down_arrived,
    grads,
    moe,
    attended,
    query,
    pair,
    bias,
    attended_grad,
    packed,
    low,
    residual_grad,
    first_grad,
    other_got,
    dense,
    core_give,
    core_got,
    land,
    land2,
    land3,
    more_give,
    more_land,
    small,
    small_give,
    small_got,
    all_sems,
    load_sems,
    other_sems,
    cross_sems,
    core_sems,
    sum_sems,
    small_sems,
):
    micro_count, rows, width = tokens_ref.shape
    padded = grads.shape[1]
    couples = query.shape[0]
    core, half_seq = lax.axis_index("dp"), lax.axis_index("seq")
    partner, across = {"dp": 1 - core}, {"seq": 1 - half_seq}
    third = width // 2
    one = micro_count - 1

    def load(index, m=one):
        source, target = (
            (grads_in, grads),
            (moe_in, moe),
            (attended_in, attended),
            (query_in, query),
            (pair_in, pair),
            (back_got, grads),
        )[index]
        return pltpu.make_async_copy(source.at[m], target, load_sems.at[index])

    past = pltpu.make_async_copy(dense_first, dense, load_sems.at[6])
    for index in range(3):
        load(index).start()
    past.start()
    for index in range(3, 5):
        load(index).start()
    greet(("seq", "exp", "dp"))
    backs = [Exchange(back_in.at[m], back_got.at[m], all_sems, m) for m in range(micro_count)]
    for m in range(micro_count):
        backs[m].start()

    def other_copy(m):
        return remote(
            other_grad_first if m == 0 else tokens_out.at[m],
            other_got.at[m],
            other_sems.at[m, 0],
            other_sems.at[m, 1],
            across,
        )

    other_copy(0).start()

    def cross():
        size = down_sum.shape[0] // 2
        there = pl.ds(size, size)
        return remote(
            down_sum.at[there], down_arrived.at[there], cross_sems.at[0], cross_sems.at[1], across
        )

    cross().start()

    small[...] = small_first[...]
    item = Backward(
        one,
        False,
        capacity,
        padded,
        pack=pack_ref,
        dense=dense,
        stage=None,
        grads=grads,
        tokens=tokens_ref.at[one],
        token_other=token_other.at[one],
        query=query,
        pair=pair,
        bias=bias,
        lengths=lengths_ref,
        slots=slots_ref.at[one],
        gates=gates_ref.at[one],
        moe=moe,
        residual=residual_ref.at[one],
        small=small,
        cot=cot_ref.at[one],
        residual_grad=residual_grad,
        attended=attended,
        attended_grad=attended_grad,
        wo=wo,
        wi=wi,
        low=low,
        packed=packed,
        stats=stats_ref.at[one],
        first_grad=first_grad,
        other_grad=tokens_out.at[one],
    )

    def lasts(m):
        other_copy(m).wait()
        first = first_grad_first if m == 0 else first_grad
        through = residual_grad_first if m == 0 else residual_grad
        total = first[...] + other_got[m].astype(F32)
        xhat, scale = normalise(tokens_ref[m].astype(F32))
        back = norm_backward(total, pack_ref[0:1].astype(F32), xhat, scale)
        tokens_out[m] = (through[...] + back).astype(BF16)

    def mix(m):
        backs[m].arrived()
        load(5, m).start()
        load(5, m).wait()
        gates = gates_ref[m]
        one, two = gather_stage(grads, slots_ref[m], ((0,), (1,)), padded)
        mixed_out[m] = (residual_ref[m] + (gates[:, 0:1] * one + gates[:, 1:2] * two)).astype(BF16)

    group_width = 3 * third
    edges = [(0, width), (width, width + group_width), (width + group_width, 4 * width)]
    sums = []
    for index, (begin, end) in enumerate(edges):
        middle = begin + ((end - begin) // 128 + 1) // 2 * 128
        for part, (start, stop) in enumerate(((begin, middle), (middle, end))):
            sums.append(
                Reduction(
                    2 * index + part,
                    slice(start, stop),
                    part == 0,
                    (
                        dense.at[core],
                        core_got.at[pl.ds(0, 8)],
                        land,
                        core_got.at[pl.ds(8, 4)],
                        land2,
                        core_got.at[pl.ds(12, 4)],
                        land3,
                        more_give,
                        more_land,
                        core_give,
                        sum_sems,
                    ),
                )
            )

    def core_copy(group):
        here = slice(*edges[group])
        return remote(
            core_give.at[:, :, here],
            core_got.at[:, :, here],
            core_sems.at[group, 0],
            core_sems.at[group, 1],
            partner,
        )

    def start_core(group):
        here = slice(*edges[group])
        core_give[:, :, here] = dense[1 - core, :, :, here].astype(BF16)
        core_copy(group).start()

    def advance(group, name):
        if name == "one":
            here = slice(*edges[group])
            core_copy(group).wait()
            dense[core, :, :, here] = dense[core, :, :, here] + core_got[:, :, here].astype(F32)
        for item in sums[2 * group : 2 * group + 2]:
            getattr(item, "finish" if name == "finish" else "start_" + name)()

    half_width = width // 2

    def small_copy(step):
        size, me = lax.axis_size("exp"), lax.axis_index("exp")
        if step == 0:
            device = partner
        elif step == 1:
            device = across
        else:
            block = 1 << (step - 2)
            device = {"exp": me + block * (1 - 2 * lax.rem(lax.div(me, block), 2))}
        return remote(
            small_give.at[step],
            small_got.at[step],
            small_sems.at[step, 0],
            small_sems.at[step, 1],
            device,
        )

    small_steps = small_give.shape[0]

    def start_small(step):
        if step == 0:
            place = pl.ds(pl.multiple_of((1 - core) * half_width, 128), half_width)
            small_give[0] = small[:, place]
            small_out[...] = small[:, pl.ds(pl.multiple_of(core * half_width, 128), half_width)]
        else:
            small_copy(step - 1).wait_recv()
            small_out[...] = small_out[...] + small_got[step - 1]
            if step == small_steps:
                return
            small_give[step] = small_out[...]
        small_copy(step).start()

    for index in range(3):
        load(index).wait()
    past.wait()
    item.before()
    start_core(0)
    load(3).wait()
    load(4).wait()
    item.heads(0, couples // 2)
    item.project_grads(0)
    start_core(1)
    advance(0, "one")
    item.heads(couples // 2, couples)
    item.project_grads(1)
    start_core(2)
    advance(1, "one")
    advance(0, "two")
    item.firsts()
    other_copy(one).start()
    start_small(0)
    advance(2, "one")
    advance(1, "two")
    advance(0, "three")
    start_small(1)
    lasts(0)
    advance(2, "two")
    advance(1, "three")
    advance(0, "four")
    start_small(2)
    mix(0)
    advance(2, "three")
    advance(1, "four")
    advance(0, "five")
    start_small(3)
    lasts(1)
    advance(2, "four")
    advance(1, "five")
    advance(0, "six")
    mix(1)
    for step in range(4, small_steps + 1):
        start_small(step)
    advance(2, "five")
    advance(1, "six")
    advance(0, "finish")
    advance(2, "six")
    advance(1, "finish")
    advance(2, "finish")
    result = pltpu.make_async_copy(core_give, final_out, load_sems.at[0])
    result.start()
    for step in range(small_steps):
        small_copy(step).wait_send()
    for m in range(micro_count):
        backs[m].sent()
    cross().wait()
    result.wait()


def shape(dims, dtype):
    return jax.ShapeDtypeStruct(dims, dtype)


def body(
    tokens,
    first_gain,
    first_shift,
    attention_in,
    attention_out,
    second_gain,
    second_shift,
    router_weight,
    up_weight,
    down_weight,
    routes,
    priority,
    lengths,
    out_cotangent,
):
    micro_count, _, rows, width = tokens.shape
    experts = lax.axis_size("exp") * up_weight.shape[0]
    hidden = up_weight.shape[2]
    capacity = (210 * rows + 100 * experts - 1) // (100 * experts)
    padded = (capacity + 3 + 7) // 8 * 8
    flat = experts * padded
    core = lax.axis_index("dp")
    chunk = 256 if flat <= 896 else 128
    chunks = hidden // chunk
    couples = width // 128

    pack_rows = (ROUTER_ROW + experts + 15) // 16 * 16
    norms = jnp.stack([first_gain, first_shift, second_gain, second_shift])
    pack = jnp.concatenate(
        [
            norms,
            jnp.zeros((ROUTER_ROW - 4, norms.shape[1]), BF16),
            router_weight.T,
            jnp.zeros((pack_rows - ROUTER_ROW - experts, norms.shape[1]), BF16),
        ]
    )
    blocks = (micro_count, experts, padded, width)
    token_dims = (micro_count, rows, width)
    dma = pltpu.SemaphoreType.DMA
    tokens, cot = tokens[:, 0], out_cotangent[:, 0]
    routes, lengths = routes[:, 0], lengths[:, 0]
    query_dims = (micro_count, couples, rows, 128)
    pair_dims = (micro_count, 2, 2 * couples, rows, 128)
    outs = (
        (VMEM, (pack_rows, width), BF16),
        (ANY, (width, 3 * width), BF16),
        (ANY, (width, width), BF16),
        (ANY, (width // 2, 3 * width), BF16),
        (ANY, (width // 2, width), BF16),
        (ANY, token_dims, BF16),
        (ANY, query_dims, BF16),
        (ANY, pair_dims, BF16),
        (ANY, token_dims, F32),
        (ANY, token_dims, BF16),
        (ANY, token_dims, BF16),
        (VMEM, (micro_count, 16, rows), F32),
        (VMEM, (micro_count, rows, 2), F32),
        (VMEM, (micro_count, rows, 4), jnp.int32),
        (ANY, blocks, BF16),
        (ANY, blocks, BF16),
        (ANY, (chunks, width, chunk), F32),
        (ANY, (chunks, chunk, width), F32),
        (ANY, (width // 2, hidden), BF16),
        (ANY, (hidden // 2, width), BF16),
        (ANY, (width // 2, hidden), BF16),
        (ANY, (hidden // 2, width), BF16),
        (VMEM, (pack_rows, width), F32),
        (ANY, (rows, width), F32),
        (ANY, (rows, width), F32),
        (ANY, (rows, width), BF16),
        (ANY, (2, 16, width // 32, 4 * width), F32),
    )
    size = lax.axis_size("exp")
    (
        pack,
        wi,
        wo,
        _,
        _,
        token_other,
        query,
        pair,
        residual,
        moe,
        attended,
        stats,
        gates,
        slots,
        back,
        grads,
        _,
        _,
        up_sum,
        down_sum,
        up_arrived,
        down_arrived,
        small,
        residual_grad,
        first_grad,
        other_grad,
        dense,
    ) = pl.pallas_call(
        partial(forward_kernel, capacity),
        out_shape=tuple(shape(dims, dtype) for _, dims, dtype in outs),
        in_specs=[VMEM] * 4 + [SMEM] + [ANY] * 5,
        out_specs=tuple(spec for spec, _, _ in outs),
        scratch_shapes=[
            pltpu.VMEM((2, pack_rows, width // 2), BF16),
            pltpu.VMEM((width, hidden), BF16),
            pltpu.VMEM((hidden, width), BF16),
            pltpu.VMEM(token_dims, BF16),
            pltpu.VMEM(blocks, BF16),
            pltpu.VMEM(blocks, BF16),
            pltpu.VMEM(blocks, BF16),
            pltpu.VMEM(blocks, BF16),
            pltpu.VMEM((chunks, width // 2, chunk), BF16),
            pltpu.VMEM((chunks // 2, chunk, width), BF16),
            dma((6, 2, size)),
            dma((5, 3)),
            dma((micro_count, 2)),
            dma((24,)),
            dma((2, 2)),
            dma((2, 2)),
            dma((2, 2)),
            dma((2, chunks)),
            dma((chunks + chunks // 4, 2)),
            dma((8,)),
            dma((2,)),
        ],
        compiler_params=pltpu.CompilerParams(
            collective_id=0, has_side_effects=True, vmem_limit_bytes=61 * 2**20
        ),
        cost_estimate=pl.CostEstimate(
            flops=5 * 10**10, bytes_accessed=10**8, transcendentals=10**7
        ),
        name="forward_and_experts",
    )(tokens, cot, routes, priority, lengths, pack, attention_in, attention_out, up_weight[0], down_weight[0])
    reds = (16, width // 32, 4 * width)
    extra = max((size // 8).bit_length() - 1, 1)
    steps = 2 + size.bit_length() - 1

    def reduced(count):
        return pltpu.VMEM((count,) + reds[1:], BF16)

    outs = (
        (VMEM, token_dims, BF16),
        (VMEM, token_dims, BF16),
        (VMEM, (pack_rows, width // 2), F32),
        (ANY, reds, BF16),
        (ANY, blocks, BF16),
        (ANY, (hidden // 2, width), BF16),
    )
    mixed, tokens_grad, small, final, _, down_arrived = pl.pallas_call(
        partial(backward_kernel, capacity),
        out_shape=tuple(shape(dims, dtype) for _, dims, dtype in outs),
        in_specs=[VMEM] * 13 + [SMEM] + [ANY] * 10,
        input_output_aliases={23: 5},
        out_specs=tuple(spec for spec, _, _ in outs),
        scratch_shapes=[
            pltpu.VMEM(blocks[1:], BF16),
            pltpu.VMEM((rows, width), BF16),
            pltpu.VMEM((rows, width), BF16),
            pltpu.VMEM(query_dims[1:], BF16),
            pltpu.VMEM(pair_dims[1:], BF16),
            pltpu.VMEM((2, rows, rows), F32),
            pltpu.VMEM(query_dims[1:], BF16),
            pltpu.VMEM((2 * rows, 3 * width), BF16),
            pltpu.VMEM((2 * rows, width), BF16),
            pltpu.VMEM((rows, width), F32),
            pltpu.VMEM((rows, width), F32),
            pltpu.VMEM(token_dims, BF16),
            pltpu.VMEM((2,) + reds, F32),
            reduced(16),
            reduced(16),
            reduced(8),
            reduced(4),
            reduced(4),
            reduced(extra),
            reduced(extra),
            pltpu.VMEM((pack_rows, width), F32),
            pltpu.VMEM((steps, pack_rows, width // 2), F32),
            pltpu.VMEM((steps, pack_rows, width // 2), F32),
            dma((2, 2, size)),
            dma((7,)),
            dma((micro_count, 2)),
            dma((2,)),
            dma((3, 2)),
            dma((6, 12, 2)),
            dma((steps, 2)),
        ],
        compiler_params=pltpu.CompilerParams(
            collective_id=1, has_side_effects=True, vmem_limit_bytes=62 * 2**20
        ),
        cost_estimate=pl.CostEstimate(
            flops=2 * 10**10, bytes_accessed=5 * 10**7, transcendentals=10**7
        ),
        name="backward_and_sums",
    )(
        cot,
        slots,
        gates,
        residual,
        stats,
        pack,
        wo,
        wi,
        tokens,
        token_other,
        small,
        residual_grad,
        first_grad,
        lengths,
        other_grad,
        dense,
        grads,
        back,
        moe,
        attended,
        query,
        pair,
        down_sum,
        down_arrived,
    )
    final = final.reshape(width // 2, 4 * width).astype(F32)
    third = width // 2
    in_grad = jnp.concatenate(
        [
            final[:, width + (3 * group + part) * third : width + (3 * group + part + 1) * third]
            for part in range(3)
            for group in range(2)
        ],
        axis=1,
    )
    return (
        mixed[:, None],
        tokens_grad[:, None],
        small[0],
        small[1],
        in_grad,
        final[:, :width],
        small[2],
        small[3],
        small[ROUTER_ROW : ROUTER_ROW + experts].T,
        (up_sum.astype(F32) + up_arrived.astype(F32))[None],
        (down_sum.astype(F32) + down_arrived.astype(F32))[None],
    )


def solution(mesh):
    placed = (
        P(None, ("exp", "dp"), "seq", None),
        P("dp"),
        P("dp"),
        P("dp", None),
        P("dp", None),
        P("dp"),
        P("dp"),
        P("dp", None),
        P("exp", "dp", None),
        P("exp", "dp", None),
        P(None, ("exp", "dp"), "seq", None),
        P(None, ("exp", "dp"), "seq"),
        P(None, ("exp", "dp"), None),
        P(None, ("exp", "dp"), "seq", None),
    )
    return jax.shard_map(
        body,
        mesh=mesh,
        in_specs=placed,
        out_specs=(
            P(None, ("exp", "dp"), "seq", None),
            P(None, ("exp", "dp"), "seq", None),
            P("dp"),
            P("dp"),
            P("dp", None),
            P("dp", None),
            P("dp"),
            P("dp"),
            P("dp", None),
            P("exp", "dp", None),
            P("exp", "dp", None),
        ),
        check_vma=False,
    )
```

```python
from functools import partial

import jax
import jax.numpy as jnp
from jax import lax
from jax.experimental import pallas as pl
from jax.experimental.pallas import tpu as pltpu
from jax.sharding import PartitionSpec as P

HEADS = 12
EPSILON = 1e-06
F32 = jnp.float32
BF16 = jnp.bfloat16
VMEM = pl.BlockSpec(memory_space=pltpu.VMEM)
SMEM = pl.BlockSpec(memory_space=pltpu.SMEM)
ROUTER_ROW = 8


def mm(a, b):
    return lax.dot_general(a, b, (((1,), (0,)), ((), ())), preferred_element_type=F32)


def mm_nt(a, b):
    return lax.dot_general(a, b, (((1,), (1,)), ((), ())), preferred_element_type=F32)


def mm_tn(a, b):
    return lax.dot_general(a, b, (((0,), (0,)), ((), ())), preferred_element_type=F32)


def iota(shape, dim):
    return lax.broadcasted_iota(jnp.int32, shape, dim)


def row_of(column, size):
    return jnp.sum(jnp.where(iota((size, size), 0) == iota((size, size), 1), column, 0.0), axis=0, keepdims=True)


def column_of(row, size):
    return jnp.sum(jnp.where(iota((size, size), 0) == iota((size, size), 1), row, 0.0), axis=1, keepdims=True)


def normalise(values):
    centre = values - jnp.mean(values, axis=-1, keepdims=True)
    spread = jnp.mean(centre * centre, axis=-1, keepdims=True)
    scale = lax.rsqrt(spread + EPSILON)
    return centre * scale, scale


def norm_backward(grad, gain, xhat, scale):
    scaled = grad * gain
    along = jnp.mean(scaled * xhat, axis=-1, keepdims=True)
    return scale * (scaled - jnp.mean(scaled, axis=-1, keepdims=True) - xhat * along)


def assign_stage(routes, level, capacity, padded):
    rows = routes.shape[0]
    level_row = level.astype(F32)
    level_column = column_of(level_row, rows)
    me, other = iota((rows, rows), 0), iota((rows, rows), 1)
    ahead = (level_row > level_column) | ((level_row == level_column) & (other < me))
    lane = iota((rows, 128), 1)
    first, second = routes[:, 0:1], routes[:, 1:2]
    wants = jnp.where((lane == first) | (lane == second + 64), 1.0, 0.0)
    count = mm(jnp.where(ahead, 1.0, 0.0).astype(BF16), wants.astype(BF16))
    total = jnp.sum(wants, axis=0, keepdims=True)
    rank_one = jnp.sum(jnp.where(lane == first, count, 0.0), axis=1, keepdims=True)
    rank_two = jnp.sum(
        jnp.where(lane == second + 64, count, 0.0) + jnp.where(lane == second, total, 0.0),
        axis=1,
        keepdims=True,
    )
    slot_one = jnp.where(rank_one < capacity, first.astype(F32) * padded + rank_one, -1.0)
    slot_two = jnp.where(rank_two < capacity, second.astype(F32) * padded + rank_two, -1.0)
    return slot_one, slot_two


def batch_of(experts, padded):
    best = 1
    for count in range(1, experts + 1):
        if experts % count == 0 and count * padded <= 256 and (count * padded) % 16 == 0:
            best = count
    return best


def spread_stage(values_ref, slots_ref, target_ref, extra=None):
    rows, width = values_ref.shape
    experts, padded = target_ref.shape[0], target_ref.shape[1]
    batch = batch_of(experts, padded)

    def step(index, _):
        slots = slots_ref[...].astype(F32)
        one, two = [row_of(slots[:, k : k + 1], rows).astype(jnp.int32) for k in range(2)]
        start = index * batch
        here = iota((batch * padded, rows), 0) + start * padded
        pick = jnp.where((here == one) | (here == two), 1.0, 0.0).astype(BF16)
        block = mm(pick, values_ref[...]).reshape(batch, padded, width)
        if extra is not None:
            block = jnp.stack([extra(start + inner, block[inner]) for inner in range(batch)])
        target_ref[pl.ds(start, batch)] = block.astype(BF16)
        return 0

    lax.fori_loop(0, experts // batch, step, 0)


def with_rows(block, first_row, rows):
    place = iota(block.shape, 0)
    for step, row in enumerate(rows):
        wide = jnp.concatenate([row, jnp.zeros((1, block.shape[1] - row.shape[1]), F32)], axis=1)
        block = jnp.where(place == first_row + step, wide, block)
    return block


def pieces(value, count):
    parts = []
    for _ in range(count):
        part = value.astype(BF16).astype(F32)
        parts.append(part)
        value = value - part
    return parts


def bias_stage(lengths_ref, m, rows, store):
    own_start = lax.axis_index("seq") * rows
    span = lax.axis_size("seq") * rows
    ends = []
    total = 0
    for step in range(lengths_ref.shape[1]):
        total = total + lengths_ref[m, step]
        ends.append(total)

    def documents(place):
        found = jnp.zeros(place.shape, jnp.int32)
        for end in ends:
            found = found + jnp.where(place >= end, 1, 0)
        return found

    asked = documents(iota((1, rows), 1) + own_start)
    for half in range(2):
        start = own_start if half == 0 else span - rows - own_start
        held = documents(iota((rows, 1), 0) + start)
        store(half, jnp.where(held == asked, 0.0, -1e30))


def gates_of(logits, routes):
    lane = iota(logits.shape, 1)
    chosen = [
        jnp.sum(jnp.where(lane == routes[:, k : k + 1] + ROUTER_ROW, logits, 0.0), axis=1, keepdims=True)
        for k in range(2)
    ]
    peak = jnp.maximum(*chosen)
    raised = [jnp.exp(part - peak) for part in chosen]
    total = raised[0] + raised[1]
    return raised[0] / total, raised[1] / total


def phi_terms(hidden):
    size = jnp.abs(hidden)
    bell = jnp.exp(hidden * hidden * -0.5)
    t = 1.0 / (1.0 + 0.23164188828 * size)
    tail = t * (
        0.127414796
        + t * (-0.142248368 + t * (0.7107068705 + t * (-0.7265760135 + t * 0.5307027145)))
    )
    tail = tail * bell
    return jnp.where(hidden >= 0, 1.0 - tail, tail), bell


def gather_stage(blocks_ref, slots, weights, padded):
    experts, _, width = blocks_ref.shape
    rows = slots.shape[0]
    batch = batch_of(experts, padded)
    place = iota((rows, batch * padded), 1)
    totals = [jnp.zeros((rows, width), F32) for _ in weights]
    for start in range(0, experts, batch):
        block = (
            blocks_ref[start : start + batch].astype(F32).reshape(batch * padded, width).astype(BF16)
        )
        here = place + start * padded
        for index, chosen in enumerate(weights):
            hit = slots[:, chosen[0] : chosen[0] + 1] == here
            for k in chosen[1:]:
                hit = hit | (slots[:, k : k + 1] == here)
            totals[index] = totals[index] + mm(jnp.where(hit, 1.0, 0.0).astype(BF16), block)
    return totals


MESH = pl.DeviceIdType.MESH
ANY = pl.BlockSpec(memory_space=pl.ANY)

def remote(source, target, sends, arrives, device):
    return pltpu.make_async_remote_copy(
        src_ref=source,
        dst_ref=target,
        send_sem=sends,
        recv_sem=arrives,
        device_id=device,
        device_id_type=MESH,
    )


def greet(axes):
    barrier = pltpu.get_barrier_semaphore()
    count = 0
    for axis in axes:
        size, me = lax.axis_size(axis), lax.axis_index(axis)
        for step in range(1, size):
            pl.semaphore_signal(
                barrier, inc=1, device_id={axis: lax.rem(me + step, size)}, device_id_type=MESH
            )
            count += 1
    pl.semaphore_wait(barrier, count)


class Exchange:
    def __init__(self, source, target, sems, index):
        self.refs, self.index = (source, target, sems), index

    def copies(self):
        source, target, sems = self.refs
        size, me = lax.axis_size("exp"), lax.axis_index("exp")
        found = []
        for step in range(1, size):
            peer = lax.rem(me + step, size)
            found.append(
                remote(
                    source.at[peer],
                    target.at[me],
                    sems.at[self.index, 0, step],
                    sems.at[self.index, 1, step],
                    {"exp": peer},
                )
            )
        return found

    def own(self):
        source, target, sems = self.refs
        me = lax.axis_index("exp")
        return pltpu.make_async_copy(source.at[me], target.at[me], sems.at[self.index, 0, 0])

    def start(self):
        for copy in self.copies():
            copy.start()
        self.own().start()

    def arrived(self):
        for copy in self.copies():
            copy.wait_recv()
        self.own().wait()

    def sent(self):
        for copy in self.copies():
            copy.wait_send()


def project(low, weight_ref, parts, store):
    width = low.shape[1]
    for part in parts:
        block = mm(low, weight_ref[:, part * width : (part + 1) * width]).astype(BF16)
        for index in range(width // 128):
            store(part, index, block[:, index * 128 : (index + 1) * 128])


def attend_stage(query_ref, pair_ref, bias_ref, attended_ref, stats_ref):
    couples, rows, couple = query_ref.shape
    head_dim = couple // 2
    low_lane = iota((1, couple), 1) < head_dim

    def step(index, _):
        query = query_ref[index].astype(F32) * head_dim**-0.5
        keys = [pair_ref[half, 2 * index] for half in range(2)]
        values = [pair_ref[half, 2 * index + 1].astype(F32).T.astype(BF16) for half in range(2)]
        outs = []
        for head in range(2):
            mine = jnp.where(low_lane == (head == 0), query, 0.0).astype(BF16)
            scores = [mm_nt(keys[half], mine) + bias_ref[half] for half in range(2)]
            peak = jnp.maximum(*[jnp.max(part, axis=0, keepdims=True) for part in scores])
            raised = [jnp.exp(part - peak) for part in scores]
            total = sum(jnp.sum(part, axis=0, keepdims=True) for part in raised)
            here = slice(head * head_dim, (head + 1) * head_dim)
            summed = sum(mm(values[half][here], raised[half].astype(BF16)) for half in range(2))
            outs.append(summed / total)
            stats_ref[pl.ds(index * 2 + head, 1), :] = peak + jnp.log(total)
        lanes = pl.ds(pl.multiple_of(index * couple, couple), couple)
        attended_ref[:, lanes] = jnp.concatenate(outs, axis=0).T.astype(BF16)
        return 0

    lax.fori_loop(0, couples, step, 0)


def flatten_stage(rows_ref, cot_ref, x, g, capacity):
    experts, padded, width = rows_ref.shape
    batch = batch_of(experts, padded)
    flat = batch * padded

    def step(index, _):
        place, lane = iota((padded, 128), 0), iota((padded, 128), 1)
        inside = (place == capacity) | (place == capacity + 1)
        block = rows_ref[pl.ds(index * batch, batch)].astype(F32)
        cot = cot_ref[pl.ds(index * batch, batch)].astype(F32)
        here = pl.ds(pl.multiple_of(index * flat, 16), flat)
        x[here, :] = block.reshape(flat, width).astype(BF16)
        scaled = []
        for inner in range(batch):
            gate_row = jnp.sum(jnp.where(inside, block[inner][:, 0:128], 0.0), axis=0, keepdims=True)
            gate = jnp.sum(jnp.where(place == lane, gate_row, 0.0), axis=1, keepdims=True)
            scaled.append(cot[inner] * gate)
        g[here, :] = jnp.stack(scaled).reshape(flat, width).astype(BF16)
        return 0

    lax.fori_loop(0, experts // batch, step, 0)


def expert_step(x, g, y, dx, up, down):
    hidden = mm(x[...], up)
    active_grad = mm_nt(g[...], down)
    phi, bell = phi_terms(hidden)
    active = (hidden * phi).astype(BF16)
    hidden_grad = (active_grad * (phi + hidden * bell * 0.3989422804)).astype(BF16)
    y[...] += mm(active, down)
    dx[...] += mm_nt(hidden_grad, up)
    return active, hidden_grad


def finish_stage(cot_ref, y, dx, back_ref, grads_ref, capacity):
    experts, padded, width = cot_ref.shape
    batch = batch_of(experts, padded)
    flat = batch * padded

    def step(index, _):
        place, lane = iota((padded, 128), 0), iota((padded, 128), 1)
        here = pl.ds(pl.multiple_of(index * flat, 16), flat)
        there = pl.ds(index * batch, batch)
        produced = y[here, :].reshape(batch, padded, width).astype(BF16)
        back_ref[there] = produced
        cot = cot_ref[there].astype(F32)
        along = jnp.sum(cot * produced.astype(F32), axis=-1, keepdims=True)
        grads = dx[here, :].reshape(batch, padded, width)
        parts = []
        for inner in range(batch):
            row = jnp.sum(jnp.where(place == lane, along[inner], 0.0), axis=0, keepdims=True)
            parts.append(with_rows(grads[inner], capacity, pieces(row, 3)))
        grads_ref[there] = jnp.stack(parts).astype(BF16)
        return 0

    lax.fori_loop(0, experts // batch, step, 0)


class Backward:
    def __init__(self, m, fresh, capacity, padded, **refs):
        self.m, self.fresh, self.capacity, self.padded = m, fresh, capacity, padded
        self.__dict__.update(refs)

    def gain(self, row):
        return self.pack[row : row + 1].astype(F32)

    def place(self, index):
        third = self.tokens.shape[1] // 2
        return slice(index * third, (index + 1) * third)

    def past(self, index):
        return pltpu.make_async_copy(
            self.dense.at[:, :, :, self.place(index)], self.stage.at[index % 2], self.save_sems.at[index % 2]
        )

    def save(self, index):
        return pltpu.make_async_copy(
            self.stage.at[index % 2], self.dense.at[:, :, :, self.place(index)], self.save_sems.at[index % 2]
        )

    def keep(self, index):
        return pltpu.make_async_copy(
            self.stage.at[index % 2, lax.axis_index("dp")],
            self.kept.at[:, :, self.place(index)],
            self.save_sems.at[2 + index % 2],
        )

    def give(self, index):
        return remote(
            self.low_stage.at[index % 2],
            self.got.at[:, :, self.place(index)],
            self.give_sems.at[index, 0],
            self.give_sems.at[index, 1],
            {"dp": 1 - lax.axis_index("dp")},
        )

    def store(self, start, value):
        third = self.tokens.shape[1] // 2
        for index in range(value.shape[1] // third):
            self.store_piece(start // third + index, value[:, index * third : (index + 1) * third])

    def store_piece(self, index, value):
        slot = index % 2
        value = value.reshape(2, 16, value.shape[0] // 32, value.shape[1])
        if self.fresh:
            if index >= 2:
                self.save(index - 2).wait()
            self.stage[slot] = value
            self.save(index).start()
            return
        self.past(index).wait()
        self.stage[slot] = self.stage[slot] + value
        self.keep(index).start()
        if index >= 2:
            self.give(index - 2).wait_send()
        self.low_stage[slot] = self.stage[slot, 1 - lax.axis_index("dp")].astype(BF16)
        self.give(index).start()
        if index + 1 < 8:
            if index >= 1:
                self.keep(index - 1).wait()
            self.past(index + 1).start()

    def drain(self):
        for index in (6, 7):
            if self.fresh:
                self.save(index).wait()
            else:
                self.keep(index).wait()
                self.give(index).wait_send()

    def before(self):
        grads, capacity, padded = self.grads, self.capacity, self.padded
        rows = self.tokens.shape[0]
        couples, _, couple = self.query.shape

        def store_bias(half, block):
            self.bias[half] = block

        bias_stage(self.lengths, self.m, rows, store_bias)
        slots, gates = self.slots[...], self.gates[...]
        routes = slots[:, 2:4]
        pack = self.pack[...]
        batch = batch_of(grads.shape[0], padded)
        flat = batch * padded
        place, lane = iota((padded, 128), 0), iota((padded, 128), 1)
        inside = (place >= capacity) & (place < capacity + 3)
        wide_lane, here = iota((flat, 128), 1), iota((rows, flat), 1)
        moe_grad = 0.0
        found = [0.0, 0.0]
        for start in range(0, grads.shape[0], batch):
            block = grads[start : start + batch].astype(F32)
            columns = []
            for inner in range(batch):
                row = jnp.sum(
                    jnp.where(inside, block[inner][:, 0:128], 0.0), axis=0, keepdims=True
                )
                columns.append(
                    jnp.sum(jnp.where(place == lane, row, 0.0), axis=1, keepdims=True)
                )
            column = jnp.stack(columns).reshape(flat, 1)
            spread = 0.0
            for index, piece in enumerate(pieces(column, 3)):
                spread = spread + jnp.where(wide_lane == index, piece, 0.0)
            spread = spread.astype(BF16)
            hits = [slots[:, k : k + 1] - start * padded == here for k in range(2)]
            for k in range(2):
                found[k] = found[k] + mm(jnp.where(hits[k], 1.0, 0.0).astype(BF16), spread)
            pick = jnp.where(hits[0] | hits[1], 1.0, 0.0).astype(BF16)
            moe_grad = moe_grad + mm(pick, block.reshape(flat, block.shape[2]).astype(BF16))
        gate_grad = [jnp.sum(part, axis=1, keepdims=True) for part in found]
        gate = [gates[:, k : k + 1] for k in range(2)]
        inner = gate[0] * gate_grad[0] + gate[1] * gate_grad[1]
        pack_lane = iota((rows, pack.shape[0]), 1)
        logit_grad = sum(
            jnp.where(
                pack_lane == routes[:, k : k + 1] + ROUTER_ROW,
                gate[k] * (gate_grad[k] - inner),
                0.0,
            )
            for k in range(2)
        )
        parts = [part.astype(BF16) for part in pieces(logit_grad, 3)]
        moe_grad = moe_grad + sum(mm(part, pack) for part in parts)
        router_grad = sum(mm_tn(part, self.moe[...]) for part in parts)
        xhat, scale = normalise(self.residual[...])
        small_row = iota(router_grad.shape, 0)
        terms = jnp.where(
            small_row == 2,
            jnp.sum(moe_grad * xhat, axis=0, keepdims=True),
            jnp.where(small_row == 3, jnp.sum(moe_grad, axis=0, keepdims=True), router_grad),
        )
        self.small[...] = terms if self.fresh else self.small[...] + terms
        total = self.cot[...].astype(F32) + norm_backward(moe_grad, self.gain(2), xhat, scale)
        self.residual_grad[...] = total
        branch = total.astype(BF16)
        self.store(0, mm_tn(self.attended[...], branch))
        turned = mm_nt(branch, self.wo[...]).astype(BF16)
        for index in range(couples):
            self.attended_grad[index] = turned[:, index * couple : (index + 1) * couple]
        for half, ref in enumerate((self.tokens, self.token_other)):
            self.low[half * rows : (half + 1) * rows] = (
                normalise(ref[...].astype(F32))[0] * self.gain(0) + self.gain(1)
            ).astype(BF16)

    def heads(self, begin, end):
        rows, width = self.tokens.shape
        couple = self.query.shape[2]
        head_dim = couple // 2
        low_lane = iota((1, couple), 1) < head_dim
        query, pair, bias, packed = self.query, self.pair, self.bias, self.packed

        def step(index, _):
            asked = query[index].astype(F32) * head_dim**-0.5
            grad_low = self.attended_grad[index]
            grad = grad_low.astype(F32)
            asked_low = asked.astype(BF16)
            keys = [pair[half, 2 * index] for half in range(2)]
            values = [pair[half, 2 * index + 1] for half in range(2)]
            keys_turned = [part.astype(F32).T.astype(BF16) for part in keys]
            key_grads, value_grads, query_grads = [[], []], [[], []], []
            for head in range(2):
                chosen = low_lane == (head == 0)
                mine = jnp.where(chosen, asked, 0.0).astype(BF16)
                mine_grad = jnp.where(chosen, grad, 0.0).astype(BF16)
                stats = self.stats[pl.ds(index * 2 + head, 1), :]
                weighting = [
                    jnp.exp(mm_nt(keys[half], mine) + bias[half] - stats) for half in range(2)
                ]
                weighting_grad = [mm_nt(values[half], mine_grad) for half in range(2)]
                delta = sum(
                    jnp.sum(weighting[half] * weighting_grad[half], axis=0, keepdims=True)
                    for half in range(2)
                )
                here = slice(head * head_dim, (head + 1) * head_dim)
                query_total = 0.0
                for half in range(2):
                    scores_grad = (weighting[half] * (weighting_grad[half] - delta)).astype(BF16)
                    value_grads[half].append(mm(weighting[half].astype(BF16), grad_low))
                    key_grads[half].append(mm(scores_grad, asked_low))
                    query_total = query_total + mm(keys_turned[half][here], scores_grad)
                query_grads.append(query_total * head_dim**-0.5)

            def lanes(part):
                return pl.ds(pl.multiple_of(part * width + index * couple, couple), couple)

            packed[0:rows, lanes(0)] = jnp.concatenate(query_grads, axis=0).T.astype(BF16)
            for half in range(2):
                here = slice(half * rows, (half + 1) * rows)
                packed[here, lanes(1)] = jnp.where(low_lane, *key_grads[half]).astype(BF16)
                packed[here, lanes(2)] = jnp.where(low_lane, *value_grads[half]).astype(BF16)
            return 0

        lax.fori_loop(begin, end, step, 0)

    def project_grads(self, group):
        rows, width = self.tokens.shape
        third = width // 2
        for part in range(3):
            tall = rows if part == 0 else 2 * rows
            source = slice(part * width + group * third, part * width + (group + 1) * third)
            value = mm_tn(self.low[0:tall], self.packed[0:tall, source])
            self.store(width + (3 * group + part) * third, value)

    def firsts(self):
        rows, width = self.tokens.shape
        packed, wi = self.packed, self.wi
        own = mm_nt(packed[0:rows, 0:width], wi[:, 0:width])
        other = 0.0
        for part in range(1, 3):
            here = slice(part * width, (part + 1) * width)
            own = own + mm_nt(packed[0:rows, here], wi[:, here])
            other = other + mm_nt(packed[rows:, here], wi[:, here])
        self.other_grad[...] = other.astype(BF16)
        self.first_grad[...] = own
        own_hat = normalise(self.tokens[...].astype(F32))[0]
        other_hat = normalise(self.token_other[...].astype(F32))[0]
        gain_grad = jnp.sum(own * own_hat + other * other_hat, axis=0, keepdims=True)
        shift_grad = jnp.sum(own + other, axis=0, keepdims=True)
        row = iota(self.small.shape, 0)
        self.small[...] = self.small[...] + jnp.where(
            row == 0, gain_grad, jnp.where(row == 1, shift_grad, 0.0)
        )


def forward_kernel(
    capacity,
    tokens_ref,
    cot_ref,
    routes_ref,
    priority_ref,
    lengths_ref,
    pack_own,
    in_own,
    out_own,
    up_own,
    down_own,
    pack_out,
    in_out,
    out_out,
    in_half,
    out_half,
    token_out,
    query_out,
    pair_out,
    residual_out,
    moe_out,
    attended_out,
    stats_out,
    gates_out,
    slots_out,
    back_got,
    grads_out,
    up_old,
    down_old,
    up_sum,
    down_sum,
    up_arrived,
    down_arrived,
    small_out,
    residual_grad_out,
    first_grad_out,
    other_grad_out,
    other_got_out,
    dense_out,
    kept_out,
    core_got_out,
    pk,
    up,
    down,
    token_other,
    cot_send,
    row_send,
    cot_got,
    row_got,
    up_got,
    down_got,
    all_sems,
    weight_sems,
    token_sems,
    out_sems,
    chunk_sems,
    past_sems,
    low_sems,
    got_sems,
    cross_sems,
    load_sems,
    save_sems,
    give_sems,
):
    micro_count, rows, width = tokens_ref.shape
    experts, padded = cot_send.shape[1], cot_send.shape[2]
    flat = experts * padded
    core, half_seq = lax.axis_index("dp"), lax.axis_index("seq")
    partner = {"dp": 1 - core}
    across = {"seq": 1 - half_seq}
    greet(("seq", "exp", "dp"))

    token_copies = [
        remote(
            tokens_ref.at[m], token_other.at[m], token_sems.at[m, 0], token_sems.at[m, 1], across
        )
        for m in range(micro_count)
    ]
    weights = []
    for index, (own, full) in enumerate(
        ((pack_own, pk), (in_own, in_half), (out_own, out_half), (up_own, up), (down_own, down))
    ):
        size = own.shape[0]
        whole_there = index in (1, 2)
        place = full.at[core] if index == 0 else full.at[pl.ds(core * size, size)]
        weights.append(
            (
                remote(
                    own,
                    full if whole_there else place,
                    weight_sems.at[index, 0],
                    weight_sems.at[index, 1],
                    partner,
                ),
                None if whole_there else pltpu.make_async_copy(own, place, weight_sems.at[index, 2]),
            )
        )
    token_copies[0].start()
    weights[0][1].start()
    for index in range(3):
        weights[index][0].start()
    token_copies[1].start()
    for index in range(3, 5):
        weights[index][0].start()
        weights[index][1].start()

    def have(index):
        weights[index][0].wait_recv()
        if weights[index][1] is not None:
            weights[index][1].wait()

    cots = [Exchange(cot_send.at[m], cot_got.at[m], all_sems, m) for m in range(micro_count)]
    rowses = [Exchange(row_send.at[m], row_got.at[m], all_sems, 2 + m) for m in range(micro_count)]
    gradses = [Exchange(cot_send.at[m], grads_out.at[m], all_sems, 4 + m) for m in range(micro_count)]
    backs = [Exchange(row_send.at[m], back_got.at[m], all_sems, 6 + m) for m in range(micro_count)]
    lane_two, lane_four = iota((rows, 2), 1), iota((rows, 4), 1)

    def claim(m):
        one, two = assign_stage(routes_ref[m], priority_ref[m], capacity, padded)
        routes = routes_ref[m]
        found = jnp.where(lane_four == 0, one, two).astype(jnp.int32)
        chosen = jnp.where(lane_four == 2, routes[:, 0:1], routes[:, 1:2])
        slots_out[m] = jnp.where(lane_four < 2, found, chosen)
        spread_stage(cot_ref.at[m], slots_out.at[m], cot_send.at[m])

    used = [0]

    def keep(refs, later):
        index = used[0]
        used[0] += 1

        def copy():
            source, target = refs()
            return pltpu.make_async_copy(source, target, out_sems.at[index])

        copy().start()
        later.append(copy)

    late = []
    claim(0)
    cots[0].start()
    have(0)
    pack_out[...] = jnp.concatenate([pk[0], pk[1]], axis=1)

    def gain(row):
        return pack_out[row : row + 1].astype(F32)

    def first_norm(values):
        return (normalise(values.astype(F32))[0] * gain(0) + gain(1)).astype(BF16)

    def attention_phase(query, pair, bias, residual, moe, attended, wi, wo):
        half = width // 2
        weight_loads = []
        for index, (own, got, full) in enumerate(((in_own, in_half, wi), (out_own, out_half, wo))):
            mine, theirs = [full.at[pl.ds(place * half, half)] for place in (core, 1 - core)]
            weight_loads.append(
                (
                    pltpu.make_async_copy(own, mine, load_sems.at[2 * index]),
                    pltpu.make_async_copy(got, theirs, load_sems.at[2 * index + 1]),
                )
            )
            weight_loads[index][0].start()

        def project_own(m):
            def store(part, index, block):
                if part == 0:
                    query[m, index] = block
                else:
                    pair[m, 0, 2 * index + part - 1] = block

            project(first_norm(tokens_ref[m]), wi, range(3), store)

        def project_other(m):
            def store(part, index, block):
                pair[m, 1, 2 * index + part - 1] = block

            project(first_norm(token_other[m]), wi, range(1, 3), store)

        have(1)
        weight_loads[0][1].start()
        weight_loads[0][1].wait()
        weight_loads[0][0].wait()
        for m in range(micro_count):
            project_own(m)
        claim(1)
        have(2)
        weight_loads[1][1].start()
        weight_loads[1][1].wait()
        weight_loads[1][0].wait()
        outs, local = [], []
        keep(lambda: (wi, in_out), outs)
        keep(lambda: (wo, out_out), outs)
        for m in range(micro_count):
            token_copies[m].wait_recv()
            project_other(m)
            keep(lambda m=m: (token_other.at[m], token_out.at[m]), late)
            keep(lambda m=m: (query.at[m], query_out.at[m]), outs)
            keep(lambda m=m: (pair.at[m], pair_out.at[m]), outs)

            def store_bias(half, block):
                bias[half] = block

            bias_stage(lengths_ref, m, rows, store_bias)
            for copy in local:
                copy().wait()
            attend_stage(query.at[m], pair.at[m], bias, attended, stats_out.at[m])
            summed = tokens_ref[m].astype(F32) + mm(attended[...], wo[...])
            residual[...] = summed
            moe_input = (normalise(summed)[0] * gain(2) + gain(3)).astype(BF16)
            moe[...] = moe_input
            gates = gates_of(mm_nt(moe_input, pack_out[...]), routes_ref[m])
            gates_out[m] = jnp.where(lane_two == 0, gates[0], gates[1])

            def gate_rows(expert, block):
                slots, gates = slots_out[m], gates_out[m]
                place = iota((rows, 128), 1)
                row = sum(
                    jnp.where(
                        slots[:, k : k + 1] - expert * padded == place, gates[:, k : k + 1], 0.0
                    )
                    for k in range(2)
                )
                return with_rows(block, capacity, pieces(jnp.sum(row, axis=0, keepdims=True), 2))

            spread_stage(moe, slots_out.at[m], row_send.at[m], gate_rows)
            rowses[m].start()
            if m == 0:
                cots[1].start()
            local = []
            keep(lambda m=m: (residual, residual_out.at[m]), local)
            keep(lambda m=m: (moe, moe_out.at[m]), local)
            keep(lambda m=m: (attended, attended_out.at[m]), local)
        for copy in outs + local:
            copy().wait()

    pl.run_scoped(
        attention_phase,
        pltpu.VMEM((micro_count, width // 128, rows, 128), BF16),
        pltpu.VMEM((micro_count, 2, width // 64, rows, 128), BF16),
        pltpu.VMEM((2, rows, rows), F32),
        pltpu.VMEM((rows, width), F32),
        pltpu.VMEM((rows, width), BF16),
        pltpu.VMEM((rows, width), BF16),
        pltpu.VMEM((width, 3 * width), BF16),
        pltpu.VMEM((width, width), BF16),
    )
    have(3)
    have(4)
    chunks, _, chunk = up_old.shape
    half_chunks = chunks // 2
    half_rows = width // 2

    def span(i):
        return pl.ds(pl.multiple_of(i * chunk, chunk), chunk)

    def own_columns():
        return pl.ds(pl.multiple_of(core * half_rows, 128), half_rows)

    def other_columns():
        return pl.ds(pl.multiple_of((1 - core) * half_rows, 128), half_rows)

    def mine(i):
        return lax.div(i, half_chunks) == core

    def cross(i):
        return remote(
            up_sum.at[:, span(i)],
            up_arrived.at[:, span(i)],
            cross_sems.at[i, 0],
            cross_sems.at[i, 1],
            across,
        )

    early = half_chunks

    def cross_down(i):
        return remote(
            down_sum.at[span(i)],
            down_arrived.at[span(i)],
            cross_sems.at[chunks + i, 0],
            cross_sems.at[chunks + i, 1],
            across,
        )

    def expert_phase(x, g, y, dx):
        def start_expert(m):
            cots[m].arrived()
            rowses[m].arrived()
            flatten_stage(row_got.at[m], cot_got.at[m], x, g, capacity)
            y[...] = jnp.zeros_like(y)
            dx[...] = jnp.zeros_like(dx)

        def end_expert(m):
            cots[m].sent()
            rowses[m].sent()
            finish_stage(cot_got.at[m], y, dx, row_send.at[m], cot_send.at[m], capacity)
            gradses[m].start()
            if m == 0:
                return
            for item in backs:
                item.start()

        def first_weights(up_buf, down_buf):
            def chunk_out(slot, i):
                return (
                    pltpu.make_async_copy(up_buf.at[slot], up_old.at[i], chunk_sems.at[slot, 0]),
                    pltpu.make_async_copy(down_buf.at[slot], down_old.at[i], chunk_sems.at[slot, 1]),
                )

            def step(i, _):
                slot = lax.rem(i, 2)
                active, hidden = expert_step(x, g, y, dx, up[:, span(i)], down[span(i), :])

                @pl.when(i >= 2)
                def _():
                    for copy in chunk_out(slot, i - 2):
                        copy.wait()

                up_buf[slot] = mm_tn(x[...], hidden)
                down_buf[slot] = mm_tn(active, g[...])
                for copy in chunk_out(slot, i):
                    copy.start()
                return 0

            lax.fori_loop(0, chunks, step, 0)
            end_expert(0)
            for i in range(chunks - 2, chunks):
                for copy in chunk_out(i % 2, i):
                    copy.wait()

        def second_weights(
            up_past, down_past, up_ring, down_ring, up_low, down_low, up_total, down_total
        ):
            def past(slot, i):
                return (
                    pltpu.make_async_copy(up_old.at[i], up_past.at[slot], past_sems.at[slot, 0]),
                    pltpu.make_async_copy(down_old.at[i], down_past.at[slot], past_sems.at[slot, 1]),
                )

            def up_given(i):
                slot = lax.rem(i, 2)
                return remote(
                    up_low.at[slot], up_got.at[i], low_sems.at[slot, 0], got_sems.at[0, i], partner
                )

            def down_given(i):
                slot, place = lax.rem(i, 2), lax.rem(i, half_chunks)
                return remote(
                    down_low.at[slot],
                    down_got.at[place],
                    low_sems.at[slot, 1],
                    got_sems.at[1, place],
                    partner,
                )

            def up_store(i):
                slot = lax.rem(i, 2)
                return pltpu.make_async_copy(
                    up_total.at[slot], up_sum.at[:, span(i)], chunk_sems.at[slot, 0]
                )

            def down_store(i):
                slot = lax.rem(i, 2)
                return pltpu.make_async_copy(
                    down_total.at[slot],
                    down_sum.at[span(lax.rem(i, half_chunks))],
                    chunk_sems.at[slot, 1],
                )

            def crossing(i):
                @pl.when(i >= 3)
                def _():
                    up_store(i - 3).wait()
                    cross(i - 3).start()

                    @pl.when(mine(i - 3))
                    def _():
                        down_store(i - 3).wait()

                        @pl.when(lax.rem(i - 3, half_chunks) < early)
                        def _():
                            cross_down(lax.rem(i - 3, half_chunks)).start()

            def compute(i):
                slot, ring = lax.rem(i, 2), lax.rem(i, 3)

                @pl.when(i + 1 < chunks)
                def _():
                    for copy in past(1 - slot, i + 1):
                        copy.start()

                active, hidden = expert_step(x, g, y, dx, up[:, span(i)], down[span(i), :])

                @pl.when(i >= 2)
                def _():
                    up_given(i - 2).wait_send()

                    @pl.when(jnp.logical_not(mine(i - 2)))
                    def _():
                        down_given(i - 2).wait_send()

                for copy in past(slot, i):
                    copy.wait()
                up_past[slot] = mm_tn(x[...], hidden) + up_past[slot]
                up_low[slot] = up_past[slot, other_columns(), :].astype(BF16)
                up_given(i).start()
                up_ring[ring] = up_past[slot, own_columns(), :]
                down_grad = mm_tn(active, g[...]) + down_past[slot]

                @pl.when(mine(i))
                def _():
                    down_ring[ring] = down_grad

                @pl.when(jnp.logical_not(mine(i)))
                def _():
                    down_low[slot] = down_grad.astype(BF16)
                    down_given(i).start()

            def summing(i):
                slot = lax.rem(i, 2)

                @pl.when((i >= 2) & (i < chunks + 2))
                def _():
                    last = i - 2
                    up_given(last).wait_recv()
                    total = up_ring[lax.rem(last, 3)] + up_got[last].astype(F32)
                    up_total[slot] = total.astype(BF16)
                    up_store(last).start()

                    @pl.when(mine(last))
                    def _():
                        down_given(last).wait_recv()
                        total = down_ring[lax.rem(last, 3)] + down_got[
                            lax.rem(last, half_chunks)
                        ].astype(F32)
                        down_total[slot] = total.astype(BF16)
                        down_store(last).start()

            for copy in past(0, 0):
                copy.start()

            def step(i, _):
                crossing(i)
                compute(i)
                summing(i)
                return 0

            def rest(i, _):
                crossing(i)
                summing(i)
                return 0

            lax.fori_loop(0, chunks, step, 0)
            end_expert(1)
            lax.fori_loop(chunks, chunks + 3, rest, 0)
            for i in range(chunks - 2, chunks):
                up_given(i).wait_send()

                @pl.when(jnp.logical_not(mine(i)))
                def _():
                    down_given(i).wait_send()

        start_expert(0)
        pl.run_scoped(
            first_weights,
            pltpu.VMEM((2, width, chunk), F32),
            pltpu.VMEM((2, chunk, width), F32),
        )
        start_expert(1)
        pl.run_scoped(
            second_weights,
            pltpu.VMEM((2, width, chunk), F32),
            pltpu.VMEM((2, chunk, width), F32),
            pltpu.VMEM((3, half_rows, chunk), F32),
            pltpu.VMEM((3, chunk, width), F32),
            pltpu.VMEM((2, half_rows, chunk), BF16),
            pltpu.VMEM((2, chunk, width), BF16),
            pltpu.VMEM((2, half_rows, chunk), BF16),
            pltpu.VMEM((2, chunk, width), BF16),
        )

    pl.run_scoped(
        expert_phase,
        pltpu.VMEM((flat, width), BF16),
        pltpu.VMEM((flat, width), BF16),
        pltpu.VMEM((flat, width), F32),
        pltpu.VMEM((flat, width), F32),
    )

    def other_copy():
        return remote(
            other_grad_out.at[0], other_got_out, token_sems.at[2, 0], token_sems.at[2, 1], across
        )

    def back_phase(
        grads,
        moe,
        attended,
        query,
        pair,
        residual,
        bias,
        attended_grad,
        packed,
        low,
        residual_grad,
        first_grad,
        other_grad,
        stage,
        low_stage,
        wi,
        wo,
    ):
        def load(index, m):
            source, target = (
                (grads_out, grads),
                (moe_out, moe),
                (attended_out, attended),
                (residual_out, residual),
                (query_out, query),
                (pair_out, pair),
                (in_out, wi),
                (out_out, wo),
            )[index]
            return pltpu.make_async_copy(
                source.at[m] if index < 6 else source, target, load_sems.at[index]
            )

        def saves(m):
            return [
                pltpu.make_async_copy(source, target.at[m], out_sems.at[24 + index])
                for index, (source, target) in enumerate(
                    (
                        (residual_grad, residual_grad_out),
                        (first_grad, first_grad_out),
                        (other_grad, other_grad_out),
                    )
                )
            ]

        def item(m):
            return Backward(
                m,
                m == 0,
                capacity,
                padded,
                pack=pack_out,
                dense=dense_out,
                kept=kept_out,
                got=core_got_out,
                stage=stage,
                low_stage=low_stage,
                save_sems=save_sems,
                give_sems=give_sems,
                grads=grads,
                tokens=tokens_ref.at[m],
                token_other=token_other.at[m],
                query=query,
                pair=pair,
                bias=bias,
                lengths=lengths_ref,
                slots=slots_out.at[m],
                gates=gates_out.at[m],
                moe=moe,
                residual=residual,
                small=small_out,
                cot=cot_ref.at[m],
                residual_grad=residual_grad,
                attended=attended,
                attended_grad=attended_grad,
                wo=wo,
                wi=wi,
                low=low,
                packed=packed,
                stats=stats_out.at[m],
                first_grad=first_grad,
                other_grad=other_grad,
            )

        for index in range(1, 8):
            load(index, 0).start()
        for m in range(micro_count):
            work = item(m)
            gradses[m].arrived()
            load(0, m).start()
            if m > 0:
                for copy in saves(m - 1):
                    copy.wait()
                other_copy().start()
                work.past(0).start()
            for index in range(8 if m == 0 else 6):
                load(index, m).wait()
            work.before()
            if m + 1 < micro_count:
                for index in range(1, 4):
                    load(index, m + 1).start()
            work.heads(0, query.shape[0])
            if m + 1 < micro_count:
                for index in range(4, 6):
                    load(index, m + 1).start()
            work.project_grads(0)
            work.project_grads(1)
            work.firsts()
            for copy in saves(m):
                copy.start()
            work.drain()
        for copy in saves(micro_count - 1):
            copy.wait()
        for index in range(8):
            item(1).give(index).wait_recv()

    pl.run_scoped(
        back_phase,
        pltpu.VMEM((experts, padded, width), BF16),
        pltpu.VMEM((rows, width), BF16),
        pltpu.VMEM((rows, width), BF16),
        pltpu.VMEM((width // 128, rows, 128), BF16),
        pltpu.VMEM((2, width // 64, rows, 128), BF16),
        pltpu.VMEM((rows, width), F32),
        pltpu.VMEM((2, rows, rows), F32),
        pltpu.VMEM((width // 128, rows, 128), BF16),
        pltpu.VMEM((2 * rows, 3 * width), BF16),
        pltpu.VMEM((2 * rows, width), BF16),
        pltpu.VMEM((rows, width), F32),
        pltpu.VMEM((rows, width), F32),
        pltpu.VMEM((rows, width), BF16),
        pltpu.VMEM((2, 2, 16, width // 32, width // 2), F32),
        pltpu.VMEM((2, 16, width // 32, width // 2), BF16),
        pltpu.VMEM((width, 3 * width), BF16),
        pltpu.VMEM((width, width), BF16),
    )
    other_copy().wait()
    for m in range(micro_count):
        backs[m].arrived()
        backs[m].sent()
        token_copies[m].wait_send()
        gradses[m].sent()
    for index in range(5):
        weights[index][0].wait_send()
    for copy in late:
        copy().wait()

    def crossed(i, _):
        cross(i).wait()
        return 0

    lax.fori_loop(0, chunks, crossed, 0)

    def crossed_down(i, _):
        cross_down(i).wait()
        return 0

    lax.fori_loop(0, early, crossed_down, 0)


class Reduction:
    def __init__(self, index, columns, seq_first, refs):
        self.acc, self.give, self.land, self.give2, self.land2, self.give3, self.land3 = refs[:7]
        self.more_give, self.more_land, self.final, self.sems = refs[7:]
        self.index, self.cols = index, columns
        size, me = lax.axis_size("exp"), lax.axis_index("exp")
        self.size, self.me = size, me
        seq, low = lax.axis_index("seq"), lax.rem(me, 2)
        flip = {"exp": me + 1 - 2 * low}
        across = {"seq": 1 - seq}
        self.first, self.second = (seq, low) if seq_first else (low, seq)
        self.to_first, self.to_second = (across, flip) if seq_first else (flip, across)
        self.turn = lax.rem(lax.div(me, 2), 4)
        self.quad = self.first * 8 + self.second * 4

    def peer(self, step):
        turn = lax.rem(self.turn + step, 4)
        return turn, {"exp": self.me + 2 * (turn - self.turn)}

    def copy(self, step, source, target, device):
        return remote(
            source, target, self.sems.at[self.index, step, 0], self.sems.at[self.index, step, 1], device
        )

    def one(self):
        return self.copy(0, self.give.at[:, :, self.cols], self.land.at[:, :, self.cols], self.to_first)

    def two(self):
        return self.copy(1, self.give2.at[:, :, self.cols], self.land2.at[:, :, self.cols], self.to_second)

    def three(self, step):
        turn, device = self.peer(step)
        return self.copy(
            1 + step, self.give3.at[turn, :, self.cols], self.land3.at[self.turn, :, self.cols], device
        )

    def more(self, step):
        block = 8 << step
        device = {"exp": self.me + block * (1 - 2 * lax.rem(lax.div(self.me, block), 2))}
        return self.copy(
            10 + step, self.more_give.at[step, :, self.cols], self.more_land.at[step, :, self.cols], device
        )

    def four(self, step):
        place = self.final.at[self.quad + self.turn, :, self.cols]
        return self.copy(4 + step, place, place, self.peer(step)[1])

    def five(self):
        place = self.final.at[pl.ds(self.quad, 4), :, self.cols]
        return self.copy(8, place, place, self.to_second)

    def six(self):
        place = self.final.at[pl.ds(self.first * 8, 8), :, self.cols]
        return self.copy(9, place, place, self.to_first)

    def start_one(self):
        self.give[:, :, self.cols] = self.acc[pl.ds((1 - self.first) * 8, 8), :, self.cols].astype(BF16)
        self.one().start()

    def start_two(self):
        self.one().wait_recv()
        mine = pl.ds(self.first * 8, 8)
        self.acc[mine, :, self.cols] = self.acc[mine, :, self.cols] + self.land[
            :, :, self.cols
        ].astype(F32)
        self.give2[:, :, self.cols] = self.acc[
            pl.ds(self.first * 8 + (1 - self.second) * 4, 4), :, self.cols
        ].astype(BF16)
        self.two().start()

    def start_three(self):
        self.two().wait_recv()
        total = self.acc[pl.ds(self.quad, 4), :, self.cols] + self.land2[:, :, self.cols].astype(F32)
        self.acc[pl.ds(self.quad, 4), :, self.cols] = total
        self.give3[:, :, self.cols] = total.astype(BF16)
        for step in range(1, 4):
            self.three(step).start()

    def start_four(self):
        total = self.acc[self.quad + self.turn, :, self.cols]
        for step in range(1, 4):
            self.three(step).wait_recv()
        for step in range(1, 4):
            total = total + self.land3[self.peer(step)[0], :, self.cols].astype(F32)
        steps = (self.size // 8).bit_length() - 1
        for step in range(steps):
            low = total.astype(BF16)
            self.more_give[step, :, self.cols] = low
            copy = self.more(step)
            copy.start()
            copy.wait_recv()
            total = low.astype(F32) + self.more_land[step, :, self.cols].astype(F32)
            copy.wait_send()
        self.final[self.quad + self.turn, :, self.cols] = total.astype(BF16)
        for step in range(1, 4):
            self.four(step).start()

    def start_five(self):
        for step in range(1, 4):
            turn, device = self.peer(step)
            place = self.final.at[self.quad + turn, :, self.cols]
            self.copy(4 + 4 - step, place, place, device).wait_recv()
        self.five().start()

    def start_six(self):
        self.five().wait_recv()
        self.six().start()

    def finish(self):
        self.six().wait_recv()
        self.one().wait_send()
        self.two().wait_send()
        for step in range(1, 4):
            self.three(step).wait_send()
            self.four(step).wait_send()
        self.five().wait_send()
        self.six().wait_send()


def sum_kernel(
    slots_ref,
    gates_ref,
    residual_ref,
    pack_ref,
    tokens_ref,
    small,
    residual_grad,
    first_grad,
    other_first,
    other_grad,
    kept_in,
    core_got_in,
    back_in,
    mixed_out,
    tokens_out,
    small_out,
    final_out,
    grads,
    other_got,
    acc,
    core_got,
    land,
    land2,
    land3,
    more_give,
    more_land,
    final,
    small_give,
    small_got,
    load_sems,
    other_sems,
    sum_sems,
    small_sems,
):
    micro_count, rows, width = tokens_ref.shape
    padded = grads.shape[1]
    core, half_seq = lax.axis_index("dp"), lax.axis_index("seq")
    partner, across = {"dp": 1 - core}, {"seq": 1 - half_seq}
    third = width // 2
    one = micro_count - 1
    group_width = 3 * third
    edges = [(0, width), (width, width + group_width), (width + group_width, 4 * width)]

    def load(group):
        here = slice(*edges[group])
        return (
            pltpu.make_async_copy(kept_in.at[:, :, here], acc.at[:, :, here], load_sems.at[group, 0]),
            pltpu.make_async_copy(
                core_got_in.at[:, :, here], core_got.at[:, :, here], load_sems.at[group, 1]
            ),
        )

    for group in range(3):
        for copy in load(group):
            copy.start()
    greet(("seq", "exp", "dp"))

    def other_copy():
        return remote(
            other_grad.at[one], other_got, other_sems.at[0], other_sems.at[1], across
        )

    def lasts(m):
        if m == one:
            other_copy().wait()
        total = first_grad[m] + (other_first if m == 0 else other_got)[...].astype(F32)
        xhat, scale = normalise(tokens_ref[m].astype(F32))
        back = norm_backward(total, pack_ref[0:1].astype(F32), xhat, scale)
        tokens_out[m] = (residual_grad[m] + back).astype(BF16)

    def mix(m):
        copy = pltpu.make_async_copy(back_in.at[m], grads, load_sems.at[0, 0])
        copy.start()
        copy.wait()
        gates = gates_ref[m]
        rows_one, rows_two = gather_stage(grads, slots_ref[m], ((0,), (1,)), padded)
        chosen = gates[:, 0:1] * rows_one + gates[:, 1:2] * rows_two
        mixed_out[m] = (residual_ref[m] + chosen).astype(BF16)

    sums = []
    for index, (begin, end) in enumerate(edges):
        middle = begin + ((end - begin) // 128 + 1) // 2 * 128
        for part, (start, stop) in enumerate(((begin, middle), (middle, end))):
            sums.append(
                Reduction(
                    2 * index + part,
                    slice(start, stop),
                    part == 0,
                    (
                        acc,
                        core_got.at[pl.ds(0, 8)],
                        land,
                        core_got.at[pl.ds(8, 4)],
                        land2,
                        core_got.at[pl.ds(12, 4)],
                        land3,
                        more_give,
                        more_land,
                        final,
                        sum_sems,
                    ),
                )
            )

    def advance(group, name):
        if name == "one":
            here = slice(*edges[group])
            for copy in load(group):
                copy.wait()
            acc[:, :, here] = acc[:, :, here] + core_got[:, :, here].astype(F32)
        for item in sums[2 * group : 2 * group + 2]:
            getattr(item, "finish" if name == "finish" else "start_" + name)()

    half_width = width // 2

    def small_copy(step):
        size, me = lax.axis_size("exp"), lax.axis_index("exp")
        if step == 0:
            device = partner
        elif step == 1:
            device = across
        else:
            block = 1 << (step - 2)
            device = {"exp": me + block * (1 - 2 * lax.rem(lax.div(me, block), 2))}
        return remote(
            small_give.at[step],
            small_got.at[step],
            small_sems.at[step, 0],
            small_sems.at[step, 1],
            device,
        )

    small_steps = small_give.shape[0]

    def start_small(step):
        if step == 0:
            place = pl.ds(pl.multiple_of((1 - core) * half_width, 128), half_width)
            small_give[0] = small[:, place]
            small_out[...] = small[:, pl.ds(pl.multiple_of(core * half_width, 128), half_width)]
        else:
            small_copy(step - 1).wait_recv()
            small_out[...] = small_out[...] + small_got[step - 1]
            if step == small_steps:
                return
            small_give[step] = small_out[...]
        small_copy(step).start()

    advance(0, "one")
    advance(1, "one")
    start_small(0)
    advance(2, "one")
    advance(0, "two")
    advance(1, "two")
    start_small(1)
    advance(2, "two")
    advance(0, "three")
    other_copy().start()
    lasts(0)
    advance(1, "three")
    start_small(2)
    advance(2, "three")
    advance(0, "four")
    mix(0)
    advance(1, "four")
    start_small(3)
    advance(0, "five")
    advance(2, "four")
    advance(1, "five")
    advance(0, "six")
    lasts(1)
    for step in range(4, small_steps + 1):
        start_small(step)
    advance(2, "five")
    advance(1, "six")
    advance(0, "finish")
    mix(1)
    advance(2, "six")
    advance(1, "finish")
    advance(2, "finish")
    result = pltpu.make_async_copy(final, final_out, load_sems.at[0, 0])
    result.start()
    for step in range(small_steps):
        small_copy(step).wait_send()
    result.wait()


def shape(dims, dtype):
    return jax.ShapeDtypeStruct(dims, dtype)


def body(
    tokens,
    first_gain,
    first_shift,
    attention_in,
    attention_out,
    second_gain,
    second_shift,
    router_weight,
    up_weight,
    down_weight,
    routes,
    priority,
    lengths,
    out_cotangent,
):
    micro_count, _, rows, width = tokens.shape
    experts = lax.axis_size("exp") * up_weight.shape[0]
    hidden = up_weight.shape[2]
    capacity = (210 * rows + 100 * experts - 1) // (100 * experts)
    padded = (capacity + 3 + 7) // 8 * 8
    flat = experts * padded
    core = lax.axis_index("dp")
    chunk = 384 if flat <= 896 else 128
    chunks = hidden // chunk
    couples = width // 128

    pack_rows = (ROUTER_ROW + experts + 15) // 16 * 16
    norms = jnp.stack([first_gain, first_shift, second_gain, second_shift])
    pack = jnp.concatenate(
        [
            norms,
            jnp.zeros((ROUTER_ROW - 4, norms.shape[1]), BF16),
            router_weight.T,
            jnp.zeros((pack_rows - ROUTER_ROW - experts, norms.shape[1]), BF16),
        ]
    )
    blocks = (micro_count, experts, padded, width)
    token_dims = (micro_count, rows, width)
    dma = pltpu.SemaphoreType.DMA
    tokens, cot = tokens[:, 0], out_cotangent[:, 0]
    routes, lengths = routes[:, 0], lengths[:, 0]
    query_dims = (micro_count, couples, rows, 128)
    pair_dims = (micro_count, 2, 2 * couples, rows, 128)
    outs = (
        (VMEM, (pack_rows, width), BF16),
        (ANY, (width, 3 * width), BF16),
        (ANY, (width, width), BF16),
        (ANY, (width // 2, 3 * width), BF16),
        (ANY, (width // 2, width), BF16),
        (ANY, token_dims, BF16),
        (ANY, query_dims, BF16),
        (ANY, pair_dims, BF16),
        (ANY, token_dims, F32),
        (ANY, token_dims, BF16),
        (ANY, token_dims, BF16),
        (VMEM, (micro_count, 16, rows), F32),
        (VMEM, (micro_count, rows, 2), F32),
        (VMEM, (micro_count, rows, 4), jnp.int32),
        (ANY, blocks, BF16),
        (ANY, blocks, BF16),
        (ANY, (chunks, width, chunk), F32),
        (ANY, (chunks, chunk, width), F32),
        (ANY, (width // 2, hidden), BF16),
        (ANY, (hidden // 2, width), BF16),
        (ANY, (width // 2, hidden), BF16),
        (ANY, (hidden // 2, width), BF16),
        (VMEM, (pack_rows, width), F32),
        (ANY, token_dims, F32),
        (ANY, token_dims, F32),
        (ANY, token_dims, BF16),
        (ANY, (rows, width), BF16),
        (ANY, (2, 16, width // 32, 4 * width), F32),
        (ANY, (16, width // 32, 4 * width), F32),
        (ANY, (16, width // 32, 4 * width), BF16),
    )
    size = lax.axis_size("exp")
    (
        pack,
        wi,
        wo,
        _,
        _,
        token_other,
        query,
        pair,
        residual,
        moe,
        attended,
        stats,
        gates,
        slots,
        back,
        grads,
        _,
        _,
        up_sum,
        down_sum,
        up_arrived,
        down_arrived,
        small,
        residual_grad,
        first_grad,
        other_grad,
        other_got,
        _,
        kept,
        core_got,
    ) = pl.pallas_call(
        partial(forward_kernel, capacity),
        out_shape=tuple(shape(dims, dtype) for _, dims, dtype in outs),
        in_specs=[VMEM] * 4 + [SMEM] + [ANY] * 5,
        out_specs=tuple(spec for spec, _, _ in outs),
        scratch_shapes=[
            pltpu.VMEM((2, pack_rows, width // 2), BF16),
            pltpu.VMEM((width, hidden), BF16),
            pltpu.VMEM((hidden, width), BF16),
            pltpu.VMEM(token_dims, BF16),
            pltpu.VMEM(blocks, BF16),
            pltpu.VMEM(blocks, BF16),
            pltpu.VMEM(blocks, BF16),
            pltpu.VMEM(blocks, BF16),
            pltpu.VMEM((chunks, width // 2, chunk), BF16),
            pltpu.VMEM((chunks // 2, chunk, width), BF16),
            dma((8, 2, size)),
            dma((5, 3)),
            dma((micro_count + 1, 2)),
            dma((27,)),
            dma((2, 2)),
            dma((2, 2)),
            dma((2, 2)),
            dma((2, chunks)),
            dma((chunks + chunks // 2, 2)),
            dma((8,)),
            dma((4,)),
            dma((8, 2)),
        ],
        compiler_params=pltpu.CompilerParams(
            collective_id=0, has_side_effects=True, vmem_limit_bytes=61 * 2**20
        ),
        cost_estimate=pl.CostEstimate(
            flops=5 * 10**10, bytes_accessed=10**8, transcendentals=10**7
        ),
        name="forward_and_experts",
    )(tokens, cot, routes, priority, lengths, pack, attention_in, attention_out, up_weight[0], down_weight[0])
    reds = (16, width // 32, 4 * width)
    extra = max((size // 8).bit_length() - 1, 1)
    steps = 2 + size.bit_length() - 1

    def reduced(count):
        return pltpu.VMEM((count,) + reds[1:], BF16)

    outs = (
        (VMEM, token_dims, BF16),
        (VMEM, token_dims, BF16),
        (VMEM, (pack_rows, width // 2), F32),
        (ANY, reds, BF16),
    )
    mixed, tokens_grad, small, final = pl.pallas_call(
        sum_kernel,
        out_shape=tuple(shape(dims, dtype) for _, dims, dtype in outs),
        in_specs=[VMEM] * 9 + [ANY] * 4,
        out_specs=tuple(spec for spec, _, _ in outs),
        scratch_shapes=[
            pltpu.VMEM(blocks[1:], BF16),
            pltpu.VMEM((rows, width), BF16),
            pltpu.VMEM(reds, F32),
            reduced(16),
            reduced(8),
            reduced(4),
            reduced(4),
            reduced(extra),
            reduced(extra),
            reduced(16),
            pltpu.VMEM((steps, pack_rows, width // 2), F32),
            pltpu.VMEM((steps, pack_rows, width // 2), F32),
            dma((3, 2)),
            dma((2,)),
            dma((6, 12, 2)),
            dma((steps, 2)),
        ],
        compiler_params=pltpu.CompilerParams(
            collective_id=1, has_side_effects=True, vmem_limit_bytes=58 * 2**20
        ),
        cost_estimate=pl.CostEstimate(
            flops=2 * 10**9, bytes_accessed=3 * 10**7, transcendentals=10**6
        ),
        name="mix_and_sums",
    )(
        slots,
        gates,
        residual,
        pack,
        tokens,
        small,
        residual_grad,
        first_grad,
        other_got,
        other_grad,
        kept,
        core_got,
        back,
    )
    final = final.reshape(width // 2, 4 * width).astype(F32)
    third = width // 2
    in_grad = jnp.concatenate(
        [
            final[:, width + (3 * group + part) * third : width + (3 * group + part + 1) * third]
            for part in range(3)
            for group in range(2)
        ],
        axis=1,
    )
    return (
        mixed[:, None],
        tokens_grad[:, None],
        small[0],
        small[1],
        in_grad,
        final[:, :width],
        small[2],
        small[3],
        small[ROUTER_ROW : ROUTER_ROW + experts].T,
        (up_sum.astype(F32) + up_arrived.astype(F32))[None],
        (down_sum.astype(F32) + down_arrived.astype(F32))[None],
    )


def solution(mesh):
    placed = (
        P(None, ("exp", "dp"), "seq", None),
        P("dp"),
        P("dp"),
        P("dp", None),
        P("dp", None),
        P("dp"),
        P("dp"),
        P("dp", None),
        P("exp", "dp", None),
        P("exp", "dp", None),
        P(None, ("exp", "dp"), "seq", None),
        P(None, ("exp", "dp"), "seq"),
        P(None, ("exp", "dp"), None),
        P(None, ("exp", "dp"), "seq", None),
    )
    return jax.shard_map(
        body,
        mesh=mesh,
        in_specs=placed,
        out_specs=(
            P(None, ("exp", "dp"), "seq", None),
            P(None, ("exp", "dp"), "seq", None),
            P("dp"),
            P("dp"),
            P("dp", None),
            P("dp", None),
            P("dp"),
            P("dp"),
            P("dp", None),
            P("exp", "dp", None),
            P("exp", "dp", None),
        ),
        check_vma=False,
    )
```

```python
from functools import partial

import jax
import jax.numpy as jnp
from jax import lax
from jax.experimental import pallas as pl
from jax.experimental.pallas import tpu as pltpu
from jax.sharding import PartitionSpec as P

HEADS = 12
EPSILON = 1e-06
F32 = jnp.float32
BF16 = jnp.bfloat16
VMEM = pl.BlockSpec(memory_space=pltpu.VMEM)
SMEM = pl.BlockSpec(memory_space=pltpu.SMEM)
ROUTER_ROW = 8


def mm(a, b):
    return lax.dot_general(a, b, (((1,), (0,)), ((), ())), preferred_element_type=F32)


def mm_nt(a, b):
    return lax.dot_general(a, b, (((1,), (1,)), ((), ())), preferred_element_type=F32)


def mm_tn(a, b):
    return lax.dot_general(a, b, (((0,), (0,)), ((), ())), preferred_element_type=F32)


def iota(shape, dim):
    return lax.broadcasted_iota(jnp.int32, shape, dim)


def row_of(column, size):
    return jnp.sum(jnp.where(iota((size, size), 0) == iota((size, size), 1), column, 0.0), axis=0, keepdims=True)


def column_of(row, size):
    return jnp.sum(jnp.where(iota((size, size), 0) == iota((size, size), 1), row, 0.0), axis=1, keepdims=True)


def normalise(values):
    centre = values - jnp.mean(values, axis=-1, keepdims=True)
    spread = jnp.mean(centre * centre, axis=-1, keepdims=True)
    scale = lax.rsqrt(spread + EPSILON)
    return centre * scale, scale


def norm_backward(grad, gain, xhat, scale):
    scaled = grad * gain
    along = jnp.mean(scaled * xhat, axis=-1, keepdims=True)
    return scale * (scaled - jnp.mean(scaled, axis=-1, keepdims=True) - xhat * along)


def assign_stage(routes, level, capacity, padded):
    rows = routes.shape[0]
    level_row = level.astype(F32)
    level_column = column_of(level_row, rows)
    me, other = iota((rows, rows), 0), iota((rows, rows), 1)
    ahead = (level_row > level_column) | ((level_row == level_column) & (other < me))
    lane = iota((rows, 128), 1)
    first, second = routes[:, 0:1], routes[:, 1:2]
    wants = jnp.where((lane == first) | (lane == second + 64), 1.0, 0.0)
    count = mm(jnp.where(ahead, 1.0, 0.0).astype(BF16), wants.astype(BF16))
    total = jnp.sum(wants, axis=0, keepdims=True)
    rank_one = jnp.sum(jnp.where(lane == first, count, 0.0), axis=1, keepdims=True)
    rank_two = jnp.sum(
        jnp.where(lane == second + 64, count, 0.0) + jnp.where(lane == second, total, 0.0),
        axis=1,
        keepdims=True,
    )
    slot_one = jnp.where(rank_one < capacity, first.astype(F32) * padded + rank_one, -1.0)
    slot_two = jnp.where(rank_two < capacity, second.astype(F32) * padded + rank_two, -1.0)
    return slot_one, slot_two


def batch_of(experts, padded):
    best = 1
    for count in range(1, experts + 1):
        if experts % count == 0 and count * padded <= 256 and (count * padded) % 16 == 0:
            best = count
    return best


def spread_stage(values_ref, slots_ref, target_ref, extra=None):
    rows, width = values_ref.shape
    experts, padded = target_ref.shape[0], target_ref.shape[1]
    batch = batch_of(experts, padded)

    def step(index, _):
        slots = slots_ref[...].astype(F32)
        one, two = [row_of(slots[:, k : k + 1], rows).astype(jnp.int32) for k in range(2)]
        start = index * batch
        here = iota((batch * padded, rows), 0) + start * padded
        pick = jnp.where((here == one) | (here == two), 1.0, 0.0).astype(BF16)
        block = mm(pick, values_ref[...]).reshape(batch, padded, width)
        if extra is not None:
            block = jnp.stack([extra(start + inner, block[inner]) for inner in range(batch)])
        target_ref[pl.ds(start, batch)] = block.astype(BF16)
        return 0

    lax.fori_loop(0, experts // batch, step, 0)


def with_rows(block, first_row, rows):
    place = iota(block.shape, 0)
    for step, row in enumerate(rows):
        wide = jnp.concatenate([row, jnp.zeros((1, block.shape[1] - row.shape[1]), F32)], axis=1)
        block = jnp.where(place == first_row + step, wide, block)
    return block


def pieces(value, count):
    parts = []
    for _ in range(count):
        part = value.astype(BF16).astype(F32)
        parts.append(part)
        value = value - part
    return parts


def bias_stage(lengths_ref, m, rows, store):
    own_start = lax.axis_index("seq") * rows
    span = lax.axis_size("seq") * rows
    ends = []
    total = 0
    for step in range(lengths_ref.shape[1]):
        total = total + lengths_ref[m, step]
        ends.append(total)

    def documents(place):
        found = jnp.zeros(place.shape, jnp.int32)
        for end in ends:
            found = found + jnp.where(place >= end, 1, 0)
        return found

    asked = documents(iota((1, rows), 1) + own_start)
    for half in range(2):
        start = own_start if half == 0 else span - rows - own_start
        held = documents(iota((rows, 1), 0) + start)
        store(half, jnp.where(held == asked, 0.0, -1e30))


def gates_of(logits, routes):
    lane = iota(logits.shape, 1)
    chosen = [
        jnp.sum(jnp.where(lane == routes[:, k : k + 1] + ROUTER_ROW, logits, 0.0), axis=1, keepdims=True)
        for k in range(2)
    ]
    peak = jnp.maximum(*chosen)
    raised = [jnp.exp(part - peak) for part in chosen]
    total = raised[0] + raised[1]
    return raised[0] / total, raised[1] / total


def phi_terms(hidden):
    size = jnp.abs(hidden)
    bell = jnp.exp(hidden * hidden * -0.5)
    t = 1.0 / (1.0 + 0.23164188828 * size)
    tail = t * (
        0.127414796
        + t * (-0.142248368 + t * (0.7107068705 + t * (-0.7265760135 + t * 0.5307027145)))
    )
    tail = tail * bell
    return jnp.where(hidden >= 0, 1.0 - tail, tail), bell


def gather_stage(blocks_ref, slots, weights, padded):
    experts, _, width = blocks_ref.shape
    rows = slots.shape[0]
    batch = batch_of(experts, padded)
    place = iota((rows, batch * padded), 1)
    totals = [jnp.zeros((rows, width), F32) for _ in weights]
    for start in range(0, experts, batch):
        block = (
            blocks_ref[start : start + batch].astype(F32).reshape(batch * padded, width).astype(BF16)
        )
        here = place + start * padded
        for index, chosen in enumerate(weights):
            hit = slots[:, chosen[0] : chosen[0] + 1] == here
            for k in chosen[1:]:
                hit = hit | (slots[:, k : k + 1] == here)
            totals[index] = totals[index] + mm(jnp.where(hit, 1.0, 0.0).astype(BF16), block)
    return totals


MESH = pl.DeviceIdType.MESH
ANY = pl.BlockSpec(memory_space=pl.ANY)

def remote(source, target, sends, arrives, device):
    return pltpu.make_async_remote_copy(
        src_ref=source,
        dst_ref=target,
        send_sem=sends,
        recv_sem=arrives,
        device_id=device,
        device_id_type=MESH,
    )


def greet(axes):
    barrier = pltpu.get_barrier_semaphore()
    count = 0
    for axis in axes:
        size, me = lax.axis_size(axis), lax.axis_index(axis)
        for step in range(1, size):
            pl.semaphore_signal(
                barrier, inc=1, device_id={axis: lax.rem(me + step, size)}, device_id_type=MESH
            )
            count += 1
    pl.semaphore_wait(barrier, count)


class Exchange:
    def __init__(self, source, target, sems, index):
        self.refs, self.index = (source, target, sems), index

    def copies(self):
        source, target, sems = self.refs
        size, me = lax.axis_size("exp"), lax.axis_index("exp")
        found = []
        for step in range(1, size):
            peer = lax.rem(me + step, size)
            found.append(
                remote(
                    source.at[peer],
                    target.at[me],
                    sems.at[self.index, 0, step],
                    sems.at[self.index, 1, step],
                    {"exp": peer},
                )
            )
        return found

    def own(self):
        source, target, sems = self.refs
        me = lax.axis_index("exp")
        return pltpu.make_async_copy(source.at[me], target.at[me], sems.at[self.index, 0, 0])

    def start(self):
        for copy in self.copies():
            copy.start()
        self.own().start()

    def arrived(self):
        for copy in self.copies():
            copy.wait_recv()
        self.own().wait()

    def sent(self):
        for copy in self.copies():
            copy.wait_send()


def project(low, weight_ref, parts, store):
    width = low.shape[1]
    for part in parts:
        block = mm(low, weight_ref[:, part * width : (part + 1) * width]).astype(BF16)
        for index in range(width // 128):
            store(part, index, block[:, index * 128 : (index + 1) * 128])


def attend_stage(query_ref, pair_ref, bias_ref, attended_ref, stats_ref):
    couples, rows, couple = query_ref.shape
    head_dim = couple // 2
    low_lane = iota((1, couple), 1) < head_dim

    def step(index, _):
        query = query_ref[index].astype(F32) * head_dim**-0.5
        keys = [pair_ref[half, 2 * index] for half in range(2)]
        values = [pair_ref[half, 2 * index + 1].astype(F32).T.astype(BF16) for half in range(2)]
        outs = []
        for head in range(2):
            mine = jnp.where(low_lane == (head == 0), query, 0.0).astype(BF16)
            scores = [mm_nt(keys[half], mine) + bias_ref[half] for half in range(2)]
            peak = jnp.maximum(*[jnp.max(part, axis=0, keepdims=True) for part in scores])
            raised = [jnp.exp(part - peak) for part in scores]
            total = sum(jnp.sum(part, axis=0, keepdims=True) for part in raised)
            here = slice(head * head_dim, (head + 1) * head_dim)
            summed = sum(mm(values[half][here], raised[half].astype(BF16)) for half in range(2))
            outs.append(summed / total)
            stats_ref[pl.ds(index * 2 + head, 1), :] = peak + jnp.log(total)
        lanes = pl.ds(pl.multiple_of(index * couple, couple), couple)
        attended_ref[:, lanes] = jnp.concatenate(outs, axis=0).T.astype(BF16)
        return 0

    lax.fori_loop(0, couples, step, 0)


def flatten_stage(rows_ref, cot_ref, x, g, capacity):
    experts, padded, width = rows_ref.shape
    batch = batch_of(experts, padded)
    flat = batch * padded

    def step(index, _):
        place, lane = iota((padded, 128), 0), iota((padded, 128), 1)
        inside = (place == capacity) | (place == capacity + 1)
        block = rows_ref[pl.ds(index * batch, batch)].astype(F32)
        cot = cot_ref[pl.ds(index * batch, batch)].astype(F32)
        here = pl.ds(pl.multiple_of(index * flat, 16), flat)
        x[here, :] = block.reshape(flat, width).astype(BF16)
        scaled = []
        for inner in range(batch):
            gate_row = jnp.sum(jnp.where(inside, block[inner][:, 0:128], 0.0), axis=0, keepdims=True)
            gate = jnp.sum(jnp.where(place == lane, gate_row, 0.0), axis=1, keepdims=True)
            scaled.append(cot[inner] * gate)
        g[here, :] = jnp.stack(scaled).reshape(flat, width).astype(BF16)
        return 0

    lax.fori_loop(0, experts // batch, step, 0)


def expert_step(x, g, y, dx, up, down):
    hidden = mm(x[...], up)
    active_grad = mm_nt(g[...], down)
    phi, bell = phi_terms(hidden)
    active = (hidden * phi).astype(BF16)
    hidden_grad = (active_grad * (phi + hidden * bell * 0.3989422804)).astype(BF16)
    y[...] += mm(active, down)
    dx[...] += mm_nt(hidden_grad, up)
    return active, hidden_grad


def finish_stage(cot_ref, y, dx, back_ref, grads_ref, capacity):
    experts, padded, width = cot_ref.shape
    batch = batch_of(experts, padded)
    flat = batch * padded

    def step(index, _):
        place, lane = iota((padded, 128), 0), iota((padded, 128), 1)
        here = pl.ds(pl.multiple_of(index * flat, 16), flat)
        there = pl.ds(index * batch, batch)
        produced = y[here, :].reshape(batch, padded, width).astype(BF16)
        back_ref[there] = produced
        cot = cot_ref[there].astype(F32)
        along = jnp.sum(cot * produced.astype(F32), axis=-1, keepdims=True)
        grads = dx[here, :].reshape(batch, padded, width)
        parts = []
        for inner in range(batch):
            row = jnp.sum(jnp.where(place == lane, along[inner], 0.0), axis=0, keepdims=True)
            parts.append(with_rows(grads[inner], capacity, pieces(row, 3)))
        grads_ref[there] = jnp.stack(parts).astype(BF16)
        return 0

    lax.fori_loop(0, experts // batch, step, 0)


class Backward:
    def __init__(self, m, fresh, capacity, padded, **refs):
        self.m, self.fresh, self.capacity, self.padded = m, fresh, capacity, padded
        self.__dict__.update(refs)

    def gain(self, row):
        return self.pack[row : row + 1].astype(F32)

    def place(self, index):
        third = self.tokens.shape[1] // 2
        return slice(index * third, (index + 1) * third)

    def past(self, index):
        return pltpu.make_async_copy(
            self.dense.at[:, :, :, self.place(index)], self.stage.at[index % 2], self.save_sems.at[index % 2]
        )

    def save(self, index):
        return pltpu.make_async_copy(
            self.stage.at[index % 2], self.dense.at[:, :, :, self.place(index)], self.save_sems.at[index % 2]
        )

    def keep(self, index):
        return pltpu.make_async_copy(
            self.stage.at[index % 2, lax.axis_index("dp")],
            self.kept.at[:, :, self.place(index)],
            self.save_sems.at[2 + index % 2],
        )

    def give(self, index):
        return remote(
            self.low_stage.at[index % 2],
            self.got.at[:, :, self.place(index)],
            self.give_sems.at[index, 0],
            self.give_sems.at[index, 1],
            {"dp": 1 - lax.axis_index("dp")},
        )

    def store(self, start, value):
        third = self.tokens.shape[1] // 2
        for index in range(value.shape[1] // third):
            self.store_piece(start // third + index, value[:, index * third : (index + 1) * third])

    def store_piece(self, index, value):
        slot = index % 2
        value = value.reshape(2, 16, value.shape[0] // 32, value.shape[1])
        if self.fresh:
            if index >= 2:
                self.save(index - 2).wait()
            self.stage[slot] = value
            self.save(index).start()
            return
        self.past(index).wait()
        self.stage[slot] = self.stage[slot] + value
        self.keep(index).start()
        if index >= 2:
            self.give(index - 2).wait_send()
        self.low_stage[slot] = self.stage[slot, 1 - lax.axis_index("dp")].astype(BF16)
        self.give(index).start()
        if index + 1 < 8:
            if index >= 1:
                self.keep(index - 1).wait()
            self.past(index + 1).start()

    def drain(self):
        for index in (6, 7):
            if self.fresh:
                self.save(index).wait()
            else:
                self.keep(index).wait()
                self.give(index).wait_send()

    def before(self):
        grads, capacity, padded = self.grads, self.capacity, self.padded
        rows = self.tokens.shape[0]
        couples, _, couple = self.query.shape

        def store_bias(half, block):
            self.bias[half] = block

        bias_stage(self.lengths, self.m, rows, store_bias)
        slots, gates = self.slots[...], self.gates[...]
        routes = slots[:, 2:4]
        pack = self.pack[...]
        batch = batch_of(grads.shape[0], padded)
        flat = batch * padded
        place, lane = iota((padded, 128), 0), iota((padded, 128), 1)
        inside = (place >= capacity) & (place < capacity + 3)
        wide_lane, here = iota((flat, 128), 1), iota((rows, flat), 1)
        moe_grad = 0.0
        found = [0.0, 0.0]
        for start in range(0, grads.shape[0], batch):
            block = grads[start : start + batch].astype(F32)
            columns = []
            for inner in range(batch):
                row = jnp.sum(
                    jnp.where(inside, block[inner][:, 0:128], 0.0), axis=0, keepdims=True
                )
                columns.append(
                    jnp.sum(jnp.where(place == lane, row, 0.0), axis=1, keepdims=True)
                )
            column = jnp.stack(columns).reshape(flat, 1)
            spread = 0.0
            for index, piece in enumerate(pieces(column, 3)):
                spread = spread + jnp.where(wide_lane == index, piece, 0.0)
            spread = spread.astype(BF16)
            hits = [slots[:, k : k + 1] - start * padded == here for k in range(2)]
            for k in range(2):
                found[k] = found[k] + mm(jnp.where(hits[k], 1.0, 0.0).astype(BF16), spread)
            pick = jnp.where(hits[0] | hits[1], 1.0, 0.0).astype(BF16)
            moe_grad = moe_grad + mm(pick, block.reshape(flat, block.shape[2]).astype(BF16))
        gate_grad = [jnp.sum(part, axis=1, keepdims=True) for part in found]
        gate = [gates[:, k : k + 1] for k in range(2)]
        inner = gate[0] * gate_grad[0] + gate[1] * gate_grad[1]
        pack_lane = iota((rows, pack.shape[0]), 1)
        logit_grad = sum(
            jnp.where(
                pack_lane == routes[:, k : k + 1] + ROUTER_ROW,
                gate[k] * (gate_grad[k] - inner),
                0.0,
            )
            for k in range(2)
        )
        parts = [part.astype(BF16) for part in pieces(logit_grad, 3)]
        moe_grad = moe_grad + sum(mm(part, pack) for part in parts)
        router_grad = sum(mm_tn(part, self.moe[...]) for part in parts)
        xhat, scale = normalise(self.residual[...])
        small_row = iota(router_grad.shape, 0)
        terms = jnp.where(
            small_row == 2,
            jnp.sum(moe_grad * xhat, axis=0, keepdims=True),
            jnp.where(small_row == 3, jnp.sum(moe_grad, axis=0, keepdims=True), router_grad),
        )
        self.small[...] = terms if self.fresh else self.small[...] + terms
        total = self.cot[...].astype(F32) + norm_backward(moe_grad, self.gain(2), xhat, scale)
        self.residual_grad[...] = total
        branch = total.astype(BF16)
        self.store(0, mm_tn(self.attended[...], branch))
        turned = mm_nt(branch, self.wo[...]).astype(BF16)
        for index in range(couples):
            self.attended_grad[index] = turned[:, index * couple : (index + 1) * couple]
        for half, ref in enumerate((self.tokens, self.token_other)):
            self.low[half * rows : (half + 1) * rows] = (
                normalise(ref[...].astype(F32))[0] * self.gain(0) + self.gain(1)
            ).astype(BF16)

    def heads(self, begin, end):
        rows, width = self.tokens.shape
        couple = self.query.shape[2]
        head_dim = couple // 2
        low_lane = iota((1, couple), 1) < head_dim
        query, pair, bias, packed = self.query, self.pair, self.bias, self.packed

        def step(index, _):
            asked = query[index].astype(F32) * head_dim**-0.5
            grad_low = self.attended_grad[index]
            grad = grad_low.astype(F32)
            asked_low = asked.astype(BF16)
            keys = [pair[half, 2 * index] for half in range(2)]
            values = [pair[half, 2 * index + 1] for half in range(2)]
            keys_turned = [part.astype(F32).T.astype(BF16) for part in keys]
            key_grads, value_grads, query_grads = [[], []], [[], []], []
            for head in range(2):
                chosen = low_lane == (head == 0)
                mine = jnp.where(chosen, asked, 0.0).astype(BF16)
                mine_grad = jnp.where(chosen, grad, 0.0).astype(BF16)
                stats = self.stats[pl.ds(index * 2 + head, 1), :]
                weighting = [
                    jnp.exp(mm_nt(keys[half], mine) + bias[half] - stats) for half in range(2)
                ]
                weighting_grad = [mm_nt(values[half], mine_grad) for half in range(2)]
                delta = sum(
                    jnp.sum(weighting[half] * weighting_grad[half], axis=0, keepdims=True)
                    for half in range(2)
                )
                here = slice(head * head_dim, (head + 1) * head_dim)
                query_total = 0.0
                for half in range(2):
                    scores_grad = (weighting[half] * (weighting_grad[half] - delta)).astype(BF16)
                    value_grads[half].append(mm(weighting[half].astype(BF16), grad_low))
                    key_grads[half].append(mm(scores_grad, asked_low))
                    query_total = query_total + mm(keys_turned[half][here], scores_grad)
                query_grads.append(query_total * head_dim**-0.5)

            def lanes(part):
                return pl.ds(pl.multiple_of(part * width + index * couple, couple), couple)

            packed[0:rows, lanes(0)] = jnp.concatenate(query_grads, axis=0).T.astype(BF16)
            for half in range(2):
                here = slice(half * rows, (half + 1) * rows)
                packed[here, lanes(1)] = jnp.where(low_lane, *key_grads[half]).astype(BF16)
                packed[here, lanes(2)] = jnp.where(low_lane, *value_grads[half]).astype(BF16)
            return 0

        lax.fori_loop(begin, end, step, 0)

    def project_grads(self, group):
        rows, width = self.tokens.shape
        third = width // 2
        for part in range(3):
            tall = rows if part == 0 else 2 * rows
            source = slice(part * width + group * third, part * width + (group + 1) * third)
            value = mm_tn(self.low[0:tall], self.packed[0:tall, source])
            self.store(width + (3 * group + part) * third, value)

    def firsts(self):
        rows, width = self.tokens.shape
        packed, wi = self.packed, self.wi
        own = mm_nt(packed[0:rows, 0:width], wi[:, 0:width])
        other = 0.0
        for part in range(1, 3):
            here = slice(part * width, (part + 1) * width)
            own = own + mm_nt(packed[0:rows, here], wi[:, here])
            other = other + mm_nt(packed[rows:, here], wi[:, here])
        self.other_grad[...] = other.astype(BF16)
        self.first_grad[...] = own
        own_hat = normalise(self.tokens[...].astype(F32))[0]
        other_hat = normalise(self.token_other[...].astype(F32))[0]
        gain_grad = jnp.sum(own * own_hat + other * other_hat, axis=0, keepdims=True)
        shift_grad = jnp.sum(own + other, axis=0, keepdims=True)
        row = iota(self.small.shape, 0)
        self.small[...] = self.small[...] + jnp.where(
            row == 0, gain_grad, jnp.where(row == 1, shift_grad, 0.0)
        )


def forward_kernel(
    capacity,
    tokens_ref,
    cot_ref,
    routes_ref,
    priority_ref,
    norms_ref,
    router_ref,
    lengths_ref,
    in_own,
    out_own,
    up_own,
    down_own,
    pack_out,
    in_out,
    out_out,
    in_half,
    out_half,
    token_out,
    query_out,
    pair_out,
    residual_out,
    moe_out,
    attended_out,
    stats_out,
    gates_out,
    slots_out,
    back_got,
    grads_out,
    up_old,
    down_old,
    up_sum,
    down_sum,
    up_arrived,
    down_arrived,
    small_out,
    residual_grad_out,
    first_grad_out,
    other_grad_out,
    other_got_out,
    dense_out,
    kept_out,
    core_got_out,
    pk,
    up,
    down,
    token_other,
    cot_send,
    row_send,
    cot_got,
    row_got,
    up_got,
    down_got,
    all_sems,
    weight_sems,
    token_sems,
    out_sems,
    chunk_sems,
    past_sems,
    low_sems,
    got_sems,
    cross_sems,
    load_sems,
    save_sems,
    give_sems,
):
    micro_count, rows, width = tokens_ref.shape
    experts, padded = cot_send.shape[1], cot_send.shape[2]
    flat = experts * padded
    core, half_seq = lax.axis_index("dp"), lax.axis_index("seq")
    partner = {"dp": 1 - core}
    across = {"seq": 1 - half_seq}
    half_width = width // 2
    rest_rows = pk.shape[1] - ROUTER_ROW - experts
    pk[core] = jnp.concatenate(
        [
            norms_ref[...].astype(F32),
            jnp.zeros((ROUTER_ROW - 4, half_width), F32),
            router_ref[...].astype(F32),
        ]
        + ([jnp.zeros((rest_rows, half_width), F32)] if rest_rows else []),
        axis=0,
    ).astype(BF16)
    greet(("seq", "exp", "dp"))

    token_copies = [
        remote(
            tokens_ref.at[m], token_other.at[m], token_sems.at[m, 0], token_sems.at[m, 1], across
        )
        for m in range(micro_count)
    ]
    weights = []
    for index, (own, full) in enumerate(
        ((pk.at[core], pk), (in_own, in_half), (out_own, out_half), (up_own, up), (down_own, down))
    ):
        size = own.shape[0]
        whole_there = index in (1, 2)
        place = full.at[core] if index == 0 else full.at[pl.ds(core * size, size)]
        weights.append(
            (
                remote(
                    own,
                    full if whole_there else place,
                    weight_sems.at[index, 0],
                    weight_sems.at[index, 1],
                    partner,
                ),
                None if index < 3 else pltpu.make_async_copy(own, place, weight_sems.at[index, 2]),
            )
        )
    token_copies[0].start()
    for index in range(3):
        weights[index][0].start()
    token_copies[1].start()
    for index in range(3, 5):
        weights[index][0].start()
        weights[index][1].start()

    def have(index):
        weights[index][0].wait_recv()
        if weights[index][1] is not None:
            weights[index][1].wait()

    cots = [Exchange(cot_send.at[m], cot_got.at[m], all_sems, m) for m in range(micro_count)]
    rowses = [Exchange(row_send.at[m], row_got.at[m], all_sems, 2 + m) for m in range(micro_count)]
    gradses = [Exchange(cot_send.at[m], grads_out.at[m], all_sems, 4 + m) for m in range(micro_count)]
    backs = [Exchange(row_send.at[m], back_got.at[m], all_sems, 6 + m) for m in range(micro_count)]
    lane_two, lane_four = iota((rows, 2), 1), iota((rows, 4), 1)

    def claim(m):
        one, two = assign_stage(routes_ref[m], priority_ref[m], capacity, padded)
        routes = routes_ref[m]
        found = jnp.where(lane_four == 0, one, two).astype(jnp.int32)
        chosen = jnp.where(lane_four == 2, routes[:, 0:1], routes[:, 1:2])
        slots_out[m] = jnp.where(lane_four < 2, found, chosen)
        spread_stage(cot_ref.at[m], slots_out.at[m], cot_send.at[m])

    used = [0]

    def keep(refs, later):
        index = used[0]
        used[0] += 1

        def copy():
            source, target = refs()
            return pltpu.make_async_copy(source, target, out_sems.at[index])

        copy().start()
        later.append(copy)

    late = []
    claim(0)
    cots[0].start()
    have(0)
    pack_out[...] = jnp.concatenate([pk[0], pk[1]], axis=1)

    def gain(row):
        return pack_out[row : row + 1].astype(F32)

    def first_norm(values):
        return (normalise(values.astype(F32))[0] * gain(0) + gain(1)).astype(BF16)

    def attention_phase(query, pair, bias, residual, moe, attended, wi, wo):
        half = width // 2
        weight_loads = []
        for index, (own, got, full) in enumerate(((in_own, in_half, wi), (out_own, out_half, wo))):
            mine, theirs = [full.at[pl.ds(place * half, half)] for place in (core, 1 - core)]
            weight_loads.append(
                (
                    pltpu.make_async_copy(own, mine, load_sems.at[2 * index]),
                    pltpu.make_async_copy(got, theirs, load_sems.at[2 * index + 1]),
                )
            )
            weight_loads[index][0].start()

        def project_own(m):
            def store(part, index, block):
                if part == 0:
                    query[m, index] = block
                else:
                    pair[m, 0, 2 * index + part - 1] = block

            project(first_norm(tokens_ref[m]), wi, range(3), store)

        def project_other(m):
            def store(part, index, block):
                pair[m, 1, 2 * index + part - 1] = block

            project(first_norm(token_other[m]), wi, range(1, 3), store)

        have(1)
        weight_loads[0][1].start()
        weight_loads[0][1].wait()
        weight_loads[0][0].wait()
        for m in range(micro_count):
            project_own(m)
        claim(1)
        have(2)
        weight_loads[1][1].start()
        weight_loads[1][1].wait()
        weight_loads[1][0].wait()
        outs, local = [], []
        keep(lambda: (wi, in_out), outs)
        keep(lambda: (wo, out_out), outs)
        for m in range(micro_count):
            token_copies[m].wait_recv()
            project_other(m)
            keep(lambda m=m: (token_other.at[m], token_out.at[m]), late)
            keep(lambda m=m: (query.at[m], query_out.at[m]), outs)
            keep(lambda m=m: (pair.at[m], pair_out.at[m]), outs)

            def store_bias(half, block):
                bias[half] = block

            bias_stage(lengths_ref, m, rows, store_bias)
            for copy in local:
                copy().wait()
            attend_stage(query.at[m], pair.at[m], bias, attended, stats_out.at[m])
            summed = tokens_ref[m].astype(F32) + mm(attended[...], wo[...])
            residual[...] = summed
            moe_input = (normalise(summed)[0] * gain(2) + gain(3)).astype(BF16)
            moe[...] = moe_input
            gates = gates_of(mm_nt(moe_input, pack_out[...]), routes_ref[m])
            gates_out[m] = jnp.where(lane_two == 0, gates[0], gates[1])

            def gate_rows(expert, block):
                slots, gates = slots_out[m], gates_out[m]
                place = iota((rows, 128), 1)
                row = sum(
                    jnp.where(
                        slots[:, k : k + 1] - expert * padded == place, gates[:, k : k + 1], 0.0
                    )
                    for k in range(2)
                )
                return with_rows(block, capacity, pieces(jnp.sum(row, axis=0, keepdims=True), 2))

            spread_stage(moe, slots_out.at[m], row_send.at[m], gate_rows)
            rowses[m].start()
            if m == 0:
                cots[1].start()
            local = []
            keep(lambda m=m: (residual, residual_out.at[m]), local)
            keep(lambda m=m: (moe, moe_out.at[m]), local)
            keep(lambda m=m: (attended, attended_out.at[m]), local)
        for copy in outs + local:
            copy().wait()

    pl.run_scoped(
        attention_phase,
        pltpu.VMEM((micro_count, width // 128, rows, 128), BF16),
        pltpu.VMEM((micro_count, 2, width // 64, rows, 128), BF16),
        pltpu.VMEM((2, rows, rows), F32),
        pltpu.VMEM((rows, width), F32),
        pltpu.VMEM((rows, width), BF16),
        pltpu.VMEM((rows, width), BF16),
        pltpu.VMEM((width, 3 * width), BF16),
        pltpu.VMEM((width, width), BF16),
    )
    have(3)
    have(4)
    chunks, _, chunk = up_old.shape
    half_chunks = chunks // 2
    half_rows = width // 2

    def span(i):
        return pl.ds(pl.multiple_of(i * chunk, chunk), chunk)

    def own_columns():
        return pl.ds(pl.multiple_of(core * half_rows, 128), half_rows)

    def other_columns():
        return pl.ds(pl.multiple_of((1 - core) * half_rows, 128), half_rows)

    def mine(i):
        return lax.div(i, half_chunks) == core

    def cross(i):
        return remote(
            up_sum.at[:, span(i)],
            up_arrived.at[:, span(i)],
            cross_sems.at[i, 0],
            cross_sems.at[i, 1],
            across,
        )

    early = half_chunks

    def cross_down(i):
        return remote(
            down_sum.at[span(i)],
            down_arrived.at[span(i)],
            cross_sems.at[chunks + i, 0],
            cross_sems.at[chunks + i, 1],
            across,
        )

    def expert_phase(x, g, y, dx):
        def start_expert(m):
            cots[m].arrived()
            rowses[m].arrived()
            flatten_stage(row_got.at[m], cot_got.at[m], x, g, capacity)
            y[...] = jnp.zeros_like(y)
            dx[...] = jnp.zeros_like(dx)

        def end_expert(m):
            cots[m].sent()
            rowses[m].sent()
            finish_stage(cot_got.at[m], y, dx, row_send.at[m], cot_send.at[m], capacity)
            gradses[m].start()
            if m == 0:
                return
            backs[1].start()

        def first_weights(up_buf, down_buf):
            def chunk_out(slot, i):
                return (
                    pltpu.make_async_copy(up_buf.at[slot], up_old.at[i], chunk_sems.at[slot, 0]),
                    pltpu.make_async_copy(down_buf.at[slot], down_old.at[i], chunk_sems.at[slot, 1]),
                )

            def step(i, _):
                slot = lax.rem(i, 2)
                active, hidden = expert_step(x, g, y, dx, up[:, span(i)], down[span(i), :])

                @pl.when(i >= 2)
                def _():
                    for copy in chunk_out(slot, i - 2):
                        copy.wait()

                up_buf[slot] = mm_tn(x[...], hidden)
                down_buf[slot] = mm_tn(active, g[...])
                for copy in chunk_out(slot, i):
                    copy.start()
                return 0

            lax.fori_loop(0, chunks, step, 0)
            end_expert(0)
            for i in range(chunks - 2, chunks):
                for copy in chunk_out(i % 2, i):
                    copy.wait()

        def second_weights(
            up_past, down_past, up_ring, down_ring, up_low, down_low, up_total, down_total
        ):
            def past(slot, i):
                return (
                    pltpu.make_async_copy(up_old.at[i], up_past.at[slot], past_sems.at[slot, 0]),
                    pltpu.make_async_copy(down_old.at[i], down_past.at[slot], past_sems.at[slot, 1]),
                )

            def up_given(i):
                slot = lax.rem(i, 2)
                return remote(
                    up_low.at[slot], up_got.at[i], low_sems.at[slot, 0], got_sems.at[0, i], partner
                )

            def down_given(i):
                slot, place = lax.rem(i, 2), lax.rem(i, half_chunks)
                return remote(
                    down_low.at[slot],
                    down_got.at[place],
                    low_sems.at[slot, 1],
                    got_sems.at[1, place],
                    partner,
                )

            def up_store(i):
                slot = lax.rem(i, 2)
                return pltpu.make_async_copy(
                    up_total.at[slot], up_sum.at[:, span(i)], chunk_sems.at[slot, 0]
                )

            def down_store(i):
                slot = lax.rem(i, 2)
                return pltpu.make_async_copy(
                    down_total.at[slot],
                    down_sum.at[span(lax.rem(i, half_chunks))],
                    chunk_sems.at[slot, 1],
                )

            def crossing(i):
                @pl.when(i >= 3)
                def _():
                    up_store(i - 3).wait()
                    cross(i - 3).start()

                    @pl.when(mine(i - 3))
                    def _():
                        down_store(i - 3).wait()

                        @pl.when(lax.rem(i - 3, half_chunks) < early)
                        def _():
                            cross_down(lax.rem(i - 3, half_chunks)).start()

            def compute(i):
                slot, ring = lax.rem(i, 2), lax.rem(i, 3)

                @pl.when(i + 1 < chunks)
                def _():
                    for copy in past(1 - slot, i + 1):
                        copy.start()

                active, hidden = expert_step(x, g, y, dx, up[:, span(i)], down[span(i), :])

                @pl.when(i >= 2)
                def _():
                    up_given(i - 2).wait_send()

                    @pl.when(jnp.logical_not(mine(i - 2)))
                    def _():
                        down_given(i - 2).wait_send()

                for copy in past(slot, i):
                    copy.wait()
                up_past[slot] = mm_tn(x[...], hidden) + up_past[slot]
                up_low[slot] = up_past[slot, other_columns(), :].astype(BF16)
                up_given(i).start()
                up_ring[ring] = up_past[slot, own_columns(), :]
                down_grad = mm_tn(active, g[...]) + down_past[slot]

                @pl.when(mine(i))
                def _():
                    down_ring[ring] = down_grad

                @pl.when(jnp.logical_not(mine(i)))
                def _():
                    down_low[slot] = down_grad.astype(BF16)
                    down_given(i).start()

            def summing(i):
                slot = lax.rem(i, 2)

                @pl.when((i >= 2) & (i < chunks + 2))
                def _():
                    last = i - 2
                    up_given(last).wait_recv()
                    total = up_ring[lax.rem(last, 3)] + up_got[last].astype(F32)
                    up_total[slot] = total.astype(BF16)
                    up_store(last).start()

                    @pl.when(mine(last))
                    def _():
                        down_given(last).wait_recv()
                        total = down_ring[lax.rem(last, 3)] + down_got[
                            lax.rem(last, half_chunks)
                        ].astype(F32)
                        down_total[slot] = total.astype(BF16)
                        down_store(last).start()

            for copy in past(0, 0):
                copy.start()

            def step(i, _):
                @pl.when(i == half_chunks)
                def _():
                    backs[0].start()

                crossing(i)
                compute(i)
                summing(i)
                return 0

            def rest(i, _):
                crossing(i)
                summing(i)
                return 0

            lax.fori_loop(0, chunks, step, 0)
            end_expert(1)
            lax.fori_loop(chunks, chunks + 3, rest, 0)
            for i in range(chunks - 2, chunks):
                up_given(i).wait_send()

                @pl.when(jnp.logical_not(mine(i)))
                def _():
                    down_given(i).wait_send()

        start_expert(0)
        pl.run_scoped(
            first_weights,
            pltpu.VMEM((2, width, chunk), F32),
            pltpu.VMEM((2, chunk, width), F32),
        )
        start_expert(1)
        pl.run_scoped(
            second_weights,
            pltpu.VMEM((2, width, chunk), F32),
            pltpu.VMEM((2, chunk, width), F32),
            pltpu.VMEM((3, half_rows, chunk), F32),
            pltpu.VMEM((3, chunk, width), F32),
            pltpu.VMEM((2, half_rows, chunk), BF16),
            pltpu.VMEM((2, chunk, width), BF16),
            pltpu.VMEM((2, half_rows, chunk), BF16),
            pltpu.VMEM((2, chunk, width), BF16),
        )

    pl.run_scoped(
        expert_phase,
        pltpu.VMEM((flat, width), BF16),
        pltpu.VMEM((flat, width), BF16),
        pltpu.VMEM((flat, width), F32),
        pltpu.VMEM((flat, width), F32),
    )

    def other_copy():
        return remote(
            other_grad_out.at[0], other_got_out, token_sems.at[2, 0], token_sems.at[2, 1], across
        )

    def back_phase(
        grads,
        moe,
        attended,
        query,
        pair,
        residual,
        bias,
        attended_grad,
        packed,
        low,
        residual_grad,
        first_grad,
        other_grad,
        stage,
        low_stage,
        wi,
        wo,
    ):
        def load(index, m):
            source, target = (
                (grads_out, grads),
                (moe_out, moe),
                (attended_out, attended),
                (residual_out, residual),
                (query_out, query),
                (pair_out, pair),
                (in_out, wi),
                (out_out, wo),
            )[index]
            return pltpu.make_async_copy(
                source.at[m] if index < 6 else source, target, load_sems.at[index]
            )

        def saves(m):
            return [
                pltpu.make_async_copy(source, target.at[m], out_sems.at[24 + index])
                for index, (source, target) in enumerate(
                    (
                        (residual_grad, residual_grad_out),
                        (first_grad, first_grad_out),
                        (other_grad, other_grad_out),
                    )
                )
            ]

        def item(m):
            return Backward(
                m,
                m == 0,
                capacity,
                padded,
                pack=pack_out,
                dense=dense_out,
                kept=kept_out,
                got=core_got_out,
                stage=stage,
                low_stage=low_stage,
                save_sems=save_sems,
                give_sems=give_sems,
                grads=grads,
                tokens=tokens_ref.at[m],
                token_other=token_other.at[m],
                query=query,
                pair=pair,
                bias=bias,
                lengths=lengths_ref,
                slots=slots_out.at[m],
                gates=gates_out.at[m],
                moe=moe,
                residual=residual,
                small=small_out,
                cot=cot_ref.at[m],
                residual_grad=residual_grad,
                attended=attended,
                attended_grad=attended_grad,
                wo=wo,
                wi=wi,
                low=low,
                packed=packed,
                stats=stats_out.at[m],
                first_grad=first_grad,
                other_grad=other_grad,
            )

        for index in range(1, 8):
            load(index, 0).start()
        for m in range(micro_count):
            work = item(m)
            gradses[m].arrived()
            load(0, m).start()
            if m > 0:
                for copy in saves(m - 1):
                    copy.wait()
                other_copy().start()
                work.past(0).start()
            for index in range(8 if m == 0 else 6):
                load(index, m).wait()
            work.before()
            if m + 1 < micro_count:
                for index in range(1, 4):
                    load(index, m + 1).start()
            work.heads(0, query.shape[0])
            if m + 1 < micro_count:
                for index in range(4, 6):
                    load(index, m + 1).start()
            work.project_grads(0)
            work.project_grads(1)
            work.firsts()
            for copy in saves(m):
                copy.start()
            work.drain()
        for copy in saves(micro_count - 1):
            copy.wait()
        for index in range(8):
            item(1).give(index).wait_recv()

    pl.run_scoped(
        back_phase,
        pltpu.VMEM((experts, padded, width), BF16),
        pltpu.VMEM((rows, width), BF16),
        pltpu.VMEM((rows, width), BF16),
        pltpu.VMEM((width // 128, rows, 128), BF16),
        pltpu.VMEM((2, width // 64, rows, 128), BF16),
        pltpu.VMEM((rows, width), F32),
        pltpu.VMEM((2, rows, rows), F32),
        pltpu.VMEM((width // 128, rows, 128), BF16),
        pltpu.VMEM((2 * rows, 3 * width), BF16),
        pltpu.VMEM((2 * rows, width), BF16),
        pltpu.VMEM((rows, width), F32),
        pltpu.VMEM((rows, width), F32),
        pltpu.VMEM((rows, width), BF16),
        pltpu.VMEM((2, 2, 16, width // 32, width // 2), F32),
        pltpu.VMEM((2, 16, width // 32, width // 2), BF16),
        pltpu.VMEM((width, 3 * width), BF16),
        pltpu.VMEM((width, width), BF16),
    )
    other_copy().wait()
    for m in range(micro_count):
        backs[m].arrived()
        backs[m].sent()
        token_copies[m].wait_send()
        gradses[m].sent()
    for index in range(5):
        weights[index][0].wait_send()
    for copy in late:
        copy().wait()

    def crossed(i, _):
        cross(i).wait()
        return 0

    lax.fori_loop(0, chunks, crossed, 0)

    def crossed_down(i, _):
        cross_down(i).wait()
        return 0

    lax.fori_loop(0, early, crossed_down, 0)


class Reduction:
    def __init__(self, index, columns, seq_first, refs):
        self.acc, self.give, self.land, self.give2, self.land2, self.give3, self.land3 = refs[:7]
        self.more_give, self.more_land, self.final, self.sems = refs[7:]
        self.index, self.cols = index, columns
        size, me = lax.axis_size("exp"), lax.axis_index("exp")
        self.size, self.me = size, me
        seq, low = lax.axis_index("seq"), lax.rem(me, 2)
        flip = {"exp": me + 1 - 2 * low}
        across = {"seq": 1 - seq}
        self.first, self.second = (seq, low) if seq_first else (low, seq)
        self.to_first, self.to_second = (across, flip) if seq_first else (flip, across)
        self.turn = lax.rem(lax.div(me, 2), 4)
        self.quad = self.first * 8 + self.second * 4

    def peer(self, step):
        turn = lax.rem(self.turn + step, 4)
        return turn, {"exp": self.me + 2 * (turn - self.turn)}

    def copy(self, step, source, target, device):
        return remote(
            source, target, self.sems.at[self.index, step, 0], self.sems.at[self.index, step, 1], device
        )

    def one(self):
        return self.copy(0, self.give.at[:, :, self.cols], self.land.at[:, :, self.cols], self.to_first)

    def two(self):
        return self.copy(1, self.give2.at[:, :, self.cols], self.land2.at[:, :, self.cols], self.to_second)

    def three(self, step):
        turn, device = self.peer(step)
        return self.copy(
            1 + step, self.give3.at[turn, :, self.cols], self.land3.at[self.turn, :, self.cols], device
        )

    def more(self, step):
        block = 8 << step
        device = {"exp": self.me + block * (1 - 2 * lax.rem(lax.div(self.me, block), 2))}
        return self.copy(
            10 + step, self.more_give.at[step, :, self.cols], self.more_land.at[step, :, self.cols], device
        )

    def four(self, step):
        place = self.final.at[self.quad + self.turn, :, self.cols]
        return self.copy(4 + step, place, place, self.peer(step)[1])

    def five(self):
        place = self.final.at[pl.ds(self.quad, 4), :, self.cols]
        return self.copy(8, place, place, self.to_second)

    def six(self):
        place = self.final.at[pl.ds(self.first * 8, 8), :, self.cols]
        return self.copy(9, place, place, self.to_first)

    def start_one(self):
        self.give[:, :, self.cols] = self.acc[pl.ds((1 - self.first) * 8, 8), :, self.cols].astype(BF16)
        self.one().start()

    def start_two(self):
        self.one().wait_recv()
        mine = pl.ds(self.first * 8, 8)
        self.acc[mine, :, self.cols] = self.acc[mine, :, self.cols] + self.land[
            :, :, self.cols
        ].astype(F32)
        self.give2[:, :, self.cols] = self.acc[
            pl.ds(self.first * 8 + (1 - self.second) * 4, 4), :, self.cols
        ].astype(BF16)
        self.two().start()

    def start_three(self):
        self.two().wait_recv()
        total = self.acc[pl.ds(self.quad, 4), :, self.cols] + self.land2[:, :, self.cols].astype(F32)
        self.acc[pl.ds(self.quad, 4), :, self.cols] = total
        self.give3[:, :, self.cols] = total.astype(BF16)
        for step in range(1, 4):
            self.three(step).start()

    def start_four(self):
        total = self.acc[self.quad + self.turn, :, self.cols]
        for step in range(1, 4):
            self.three(step).wait_recv()
        for step in range(1, 4):
            total = total + self.land3[self.peer(step)[0], :, self.cols].astype(F32)
        steps = (self.size // 8).bit_length() - 1
        for step in range(steps):
            low = total.astype(BF16)
            self.more_give[step, :, self.cols] = low
            copy = self.more(step)
            copy.start()
            copy.wait_recv()
            total = low.astype(F32) + self.more_land[step, :, self.cols].astype(F32)
            copy.wait_send()
        self.final[self.quad + self.turn, :, self.cols] = total.astype(BF16)
        for step in range(1, 4):
            self.four(step).start()

    def start_five(self):
        for step in range(1, 4):
            turn, device = self.peer(step)
            place = self.final.at[self.quad + turn, :, self.cols]
            self.copy(4 + 4 - step, place, place, device).wait_recv()
        self.five().start()

    def start_six(self):
        self.five().wait_recv()
        self.six().start()

    def finish(self):
        self.six().wait_recv()
        self.one().wait_send()
        self.two().wait_send()
        for step in range(1, 4):
            self.three(step).wait_send()
            self.four(step).wait_send()
        self.five().wait_send()
        self.six().wait_send()


def sum_kernel(
    slots_ref,
    gates_ref,
    pack_ref,
    small,
    residual_in,
    tokens_in,
    residual_grad_in,
    first_grad_in,
    other_first_in,
    other_grad,
    kept_in,
    core_got_in,
    back_in,
    mixed_out,
    tokens_out,
    small_out,
    final_out,
    grads,
    other_got,
    acc,
    core_got,
    land,
    land2,
    land3,
    more_give,
    more_land,
    final,
    small_give,
    small_got,
    residual_ref,
    tokens_ref,
    residual_grad,
    first_grad,
    other_first,
    load_sems,
    late_sems,
    other_sems,
    sum_sems,
    small_sems,
):
    micro_count, rows, width = mixed_out.shape
    padded = grads.shape[2]
    core, half_seq = lax.axis_index("dp"), lax.axis_index("seq")
    partner, across = {"dp": 1 - core}, {"seq": 1 - half_seq}
    third = width // 2
    one = micro_count - 1
    group_width = 3 * third
    edges = [(0, width), (width, width + group_width), (width + group_width, 4 * width)]

    def load(group):
        here = slice(*edges[group])
        return (
            pltpu.make_async_copy(kept_in.at[:, :, here], acc.at[:, :, here], load_sems.at[group, 0]),
            pltpu.make_async_copy(
                core_got_in.at[:, :, here], core_got.at[:, :, here], load_sems.at[group, 1]
            ),
        )

    for group in range(3):
        for copy in load(group):
            copy.start()
    late = [
        pltpu.make_async_copy(source, target, late_sems.at[index])
        for index, (source, target) in enumerate(
            (
                (residual_in, residual_ref),
                (tokens_in, tokens_ref),
                (residual_grad_in, residual_grad),
                (first_grad_in, first_grad),
                (other_first_in, other_first),
                (back_in.at[0], grads.at[0]),
                (back_in.at[1], grads.at[1]),
            )
        )
    ]
    for copy in late:
        copy.start()
    greet(("seq", "exp", "dp"))

    def other_copy():
        return remote(
            other_grad.at[one], other_got, other_sems.at[0], other_sems.at[1], across
        )

    def lasts(m):
        if m == one:
            other_copy().wait()
        total = first_grad[m] + (other_first if m == 0 else other_got)[...].astype(F32)
        xhat, scale = normalise(tokens_ref[m].astype(F32))
        back = norm_backward(total, pack_ref[0:1].astype(F32), xhat, scale)
        tokens_out[m] = (residual_grad[m] + back).astype(BF16)

    def mix(m):
        gates = gates_ref[m]
        rows_one, rows_two = gather_stage(grads.at[m], slots_ref[m], ((0,), (1,)), padded)
        chosen = gates[:, 0:1] * rows_one + gates[:, 1:2] * rows_two
        mixed_out[m] = (residual_ref[m] + chosen).astype(BF16)

    sums = []
    for index, (begin, end) in enumerate(edges):
        middle = begin + ((end - begin) // 128 + 1) // 2 * 128
        for part, (start, stop) in enumerate(((begin, middle), (middle, end))):
            sums.append(
                Reduction(
                    2 * index + part,
                    slice(start, stop),
                    part == 0,
                    (
                        acc,
                        core_got.at[pl.ds(0, 8)],
                        land,
                        core_got.at[pl.ds(8, 4)],
                        land2,
                        core_got.at[pl.ds(12, 4)],
                        land3,
                        more_give,
                        more_land,
                        final,
                        sum_sems,
                    ),
                )
            )

    def advance(group, name):
        if name == "one":
            here = slice(*edges[group])
            for copy in load(group):
                copy.wait()
            acc[:, :, here] = acc[:, :, here] + core_got[:, :, here].astype(F32)
        for item in sums[2 * group : 2 * group + 2]:
            getattr(item, "finish" if name == "finish" else "start_" + name)()

    half_width = width // 2

    def small_copy(step):
        size, me = lax.axis_size("exp"), lax.axis_index("exp")
        if step == 0:
            device = partner
        elif step == 1:
            device = across
        else:
            block = 1 << (step - 2)
            device = {"exp": me + block * (1 - 2 * lax.rem(lax.div(me, block), 2))}
        return remote(
            small_give.at[step],
            small_got.at[step],
            small_sems.at[step, 0],
            small_sems.at[step, 1],
            device,
        )

    small_steps = small_give.shape[0]

    def start_small(step):
        if step == 0:
            place = pl.ds(pl.multiple_of((1 - core) * half_width, 128), half_width)
            small_give[0] = small[:, place]
            small_out[...] = small[:, pl.ds(pl.multiple_of(core * half_width, 128), half_width)]
        else:
            small_copy(step - 1).wait_recv()
            small_out[...] = small_out[...] + small_got[step - 1]
            if step == small_steps:
                return
            small_give[step] = small_out[...]
        small_copy(step).start()

    advance(0, "one")
    advance(1, "one")
    start_small(0)
    advance(2, "one")
    advance(0, "two")
    advance(1, "two")
    start_small(1)
    advance(2, "two")
    advance(0, "three")
    other_copy().start()
    for copy in late:
        copy.wait()
    lasts(0)
    advance(1, "three")
    start_small(2)
    advance(2, "three")
    advance(0, "four")
    mix(0)
    advance(1, "four")
    start_small(3)
    advance(0, "five")
    advance(2, "four")
    advance(1, "five")
    advance(0, "six")
    lasts(1)
    for step in range(4, small_steps + 1):
        start_small(step)
    advance(2, "five")
    advance(1, "six")
    advance(0, "finish")
    mix(1)
    advance(2, "six")
    advance(1, "finish")
    advance(2, "finish")
    result = pltpu.make_async_copy(final, final_out, load_sems.at[0, 0])
    result.start()
    for step in range(small_steps):
        small_copy(step).wait_send()
    result.wait()


def shape(dims, dtype):
    return jax.ShapeDtypeStruct(dims, dtype)


def body(
    tokens,
    first_gain,
    first_shift,
    attention_in,
    attention_out,
    second_gain,
    second_shift,
    router_weight,
    up_weight,
    down_weight,
    routes,
    priority,
    lengths,
    out_cotangent,
):
    micro_count, _, rows, width = tokens.shape
    experts = lax.axis_size("exp") * up_weight.shape[0]
    hidden = up_weight.shape[2]
    capacity = (210 * rows + 100 * experts - 1) // (100 * experts)
    padded = (capacity + 3 + 7) // 8 * 8
    flat = experts * padded
    core = lax.axis_index("dp")
    chunk = 384 if flat <= 896 else 128
    chunks = hidden // chunk
    couples = width // 128

    pack_rows = (ROUTER_ROW + experts + 15) // 16 * 16
    norms = jnp.concatenate([first_gain, first_shift, second_gain, second_shift])
    norms = norms.reshape(4, width // 2)
    blocks = (micro_count, experts, padded, width)
    token_dims = (micro_count, rows, width)
    dma = pltpu.SemaphoreType.DMA
    tokens, cot = tokens[:, 0], out_cotangent[:, 0]
    routes, lengths = routes[:, 0], lengths[:, 0]
    query_dims = (micro_count, couples, rows, 128)
    pair_dims = (micro_count, 2, 2 * couples, rows, 128)
    outs = (
        (VMEM, (pack_rows, width), BF16),
        (ANY, (width, 3 * width), BF16),
        (ANY, (width, width), BF16),
        (ANY, (width // 2, 3 * width), BF16),
        (ANY, (width // 2, width), BF16),
        (ANY, token_dims, BF16),
        (ANY, query_dims, BF16),
        (ANY, pair_dims, BF16),
        (ANY, token_dims, F32),
        (ANY, token_dims, BF16),
        (ANY, token_dims, BF16),
        (VMEM, (micro_count, 16, rows), F32),
        (VMEM, (micro_count, rows, 2), F32),
        (VMEM, (micro_count, rows, 4), jnp.int32),
        (ANY, blocks, BF16),
        (ANY, blocks, BF16),
        (ANY, (chunks, width, chunk), F32),
        (ANY, (chunks, chunk, width), F32),
        (ANY, (width // 2, hidden), BF16),
        (ANY, (hidden // 2, width), BF16),
        (ANY, (width // 2, hidden), BF16),
        (ANY, (hidden // 2, width), BF16),
        (VMEM, (pack_rows, width), F32),
        (ANY, token_dims, F32),
        (ANY, token_dims, F32),
        (ANY, token_dims, BF16),
        (ANY, (rows, width), BF16),
        (ANY, (2, 16, width // 32, 4 * width), F32),
        (ANY, (16, width // 32, 4 * width), F32),
        (ANY, (16, width // 32, 4 * width), BF16),
    )
    size = lax.axis_size("exp")
    (
        pack,
        wi,
        wo,
        _,
        _,
        token_other,
        query,
        pair,
        residual,
        moe,
        attended,
        stats,
        gates,
        slots,
        back,
        grads,
        _,
        _,
        up_sum,
        down_sum,
        up_arrived,
        down_arrived,
        small,
        residual_grad,
        first_grad,
        other_grad,
        other_got,
        _,
        kept,
        core_got,
    ) = pl.pallas_call(
        partial(forward_kernel, capacity),
        out_shape=tuple(shape(dims, dtype) for _, dims, dtype in outs),
        in_specs=[VMEM] * 6 + [SMEM] + [ANY] * 4,
        out_specs=tuple(spec for spec, _, _ in outs),
        scratch_shapes=[
            pltpu.VMEM((2, pack_rows, width // 2), BF16),
            pltpu.VMEM((width, hidden), BF16),
            pltpu.VMEM((hidden, width), BF16),
            pltpu.VMEM(token_dims, BF16),
            pltpu.VMEM(blocks, BF16),
            pltpu.VMEM(blocks, BF16),
            pltpu.VMEM(blocks, BF16),
            pltpu.VMEM(blocks, BF16),
            pltpu.VMEM((chunks, width // 2, chunk), BF16),
            pltpu.VMEM((chunks // 2, chunk, width), BF16),
            dma((8, 2, size)),
            dma((5, 3)),
            dma((micro_count + 1, 2)),
            dma((27,)),
            dma((2, 2)),
            dma((2, 2)),
            dma((2, 2)),
            dma((2, chunks)),
            dma((chunks + chunks // 2, 2)),
            dma((8,)),
            dma((4,)),
            dma((8, 2)),
        ],
        compiler_params=pltpu.CompilerParams(
            collective_id=0, has_side_effects=True, vmem_limit_bytes=61 * 2**20
        ),
        cost_estimate=pl.CostEstimate(
            flops=5 * 10**10, bytes_accessed=10**8, transcendentals=10**7
        ),
        name="forward_and_experts",
    )(tokens, cot, routes, priority, norms, router_weight.T, lengths, attention_in, attention_out, up_weight[0], down_weight[0])
    reds = (16, width // 32, 4 * width)
    extra = max((size // 8).bit_length() - 1, 1)
    steps = 2 + size.bit_length() - 1

    def reduced(count):
        return pltpu.VMEM((count,) + reds[1:], BF16)

    outs = (
        (VMEM, token_dims, BF16),
        (VMEM, token_dims, BF16),
        (VMEM, (pack_rows, width // 2), F32),
        (ANY, reds, BF16),
    )
    mixed, tokens_grad, small, final = pl.pallas_call(
        sum_kernel,
        out_shape=tuple(shape(dims, dtype) for _, dims, dtype in outs),
        in_specs=[VMEM] * 4 + [ANY] * 9,
        out_specs=tuple(spec for spec, _, _ in outs),
        scratch_shapes=[
            pltpu.VMEM(blocks, BF16),
            pltpu.VMEM((rows, width), BF16),
            pltpu.VMEM(reds, F32),
            reduced(16),
            reduced(8),
            reduced(4),
            reduced(4),
            reduced(extra),
            reduced(extra),
            reduced(16),
            pltpu.VMEM((steps, pack_rows, width // 2), F32),
            pltpu.VMEM((steps, pack_rows, width // 2), F32),
            pltpu.VMEM(token_dims, F32),
            pltpu.VMEM(token_dims, BF16),
            pltpu.VMEM(token_dims, F32),
            pltpu.VMEM(token_dims, F32),
            pltpu.VMEM((rows, width), BF16),
            dma((3, 2)),
            dma((7,)),
            dma((2,)),
            dma((6, 12, 2)),
            dma((steps, 2)),
        ],
        compiler_params=pltpu.CompilerParams(
            collective_id=1, has_side_effects=True, vmem_limit_bytes=58 * 2**20
        ),
        cost_estimate=pl.CostEstimate(
            flops=2 * 10**9, bytes_accessed=3 * 10**7, transcendentals=10**6
        ),
        name="mix_and_sums",
    )(
        slots,
        gates,
        pack,
        small,
        residual,
        tokens,
        residual_grad,
        first_grad,
        other_got,
        other_grad,
        kept,
        core_got,
        back,
    )
    final = final.reshape(width // 2, 4 * width).astype(F32)
    third = width // 2
    in_grad = jnp.concatenate(
        [
            final[:, width + (3 * group + part) * third : width + (3 * group + part + 1) * third]
            for part in range(3)
            for group in range(2)
        ],
        axis=1,
    )
    return (
        mixed[:, None],
        tokens_grad[:, None],
        small[0],
        small[1],
        in_grad,
        final[:, :width],
        small[2],
        small[3],
        small[ROUTER_ROW : ROUTER_ROW + experts].T,
        (up_sum.astype(F32) + up_arrived.astype(F32))[None],
        (down_sum.astype(F32) + down_arrived.astype(F32))[None],
    )


def solution(mesh):
    placed = (
        P(None, ("exp", "dp"), "seq", None),
        P("dp"),
        P("dp"),
        P("dp", None),
        P("dp", None),
        P("dp"),
        P("dp"),
        P("dp", None),
        P("exp", "dp", None),
        P("exp", "dp", None),
        P(None, ("exp", "dp"), "seq", None),
        P(None, ("exp", "dp"), "seq"),
        P(None, ("exp", "dp"), None),
        P(None, ("exp", "dp"), "seq", None),
    )
    return jax.shard_map(
        body,
        mesh=mesh,
        in_specs=placed,
        out_specs=(
            P(None, ("exp", "dp"), "seq", None),
            P(None, ("exp", "dp"), "seq", None),
            P("dp"),
            P("dp"),
            P("dp", None),
            P("dp", None),
            P("dp"),
            P("dp"),
            P("dp", None),
            P("exp", "dp", None),
            P("exp", "dp", None),
        ),
        check_vma=False,
    )
```

```python
from functools import partial

import jax
import jax.numpy as jnp
from jax import lax
from jax.experimental import pallas as pl
from jax.experimental.pallas import tpu as pltpu
from jax.sharding import PartitionSpec as P

HEADS = 12
EPSILON = 1e-06
F32 = jnp.float32
BF16 = jnp.bfloat16
VMEM = pl.BlockSpec(memory_space=pltpu.VMEM)
SMEM = pl.BlockSpec(memory_space=pltpu.SMEM)
ROUTER_ROW = 8


def mm(a, b):
    return lax.dot_general(a, b, (((1,), (0,)), ((), ())), preferred_element_type=F32)


def mm_nt(a, b):
    return lax.dot_general(a, b, (((1,), (1,)), ((), ())), preferred_element_type=F32)


def mm_tn(a, b):
    return lax.dot_general(a, b, (((0,), (0,)), ((), ())), preferred_element_type=F32)


def iota(shape, dim):
    return lax.broadcasted_iota(jnp.int32, shape, dim)


def row_of(column, size):
    return jnp.sum(jnp.where(iota((size, size), 0) == iota((size, size), 1), column, 0.0), axis=0, keepdims=True)


def column_of(row, size):
    return jnp.sum(jnp.where(iota((size, size), 0) == iota((size, size), 1), row, 0.0), axis=1, keepdims=True)


def normalise(values):
    centre = values - jnp.mean(values, axis=-1, keepdims=True)
    spread = jnp.mean(centre * centre, axis=-1, keepdims=True)
    scale = lax.rsqrt(spread + EPSILON)
    return centre * scale, scale


def norm_backward(grad, gain, xhat, scale):
    scaled = grad * gain
    along = jnp.mean(scaled * xhat, axis=-1, keepdims=True)
    return scale * (scaled - jnp.mean(scaled, axis=-1, keepdims=True) - xhat * along)


def assign_stage(routes, level, capacity, padded):
    rows = routes.shape[0]
    level_row = level.astype(F32)
    level_column = column_of(level_row, rows)
    me, other = iota((rows, rows), 0), iota((rows, rows), 1)
    ahead = (level_row > level_column) | ((level_row == level_column) & (other < me))
    lane = iota((rows, 128), 1)
    first, second = routes[:, 0:1], routes[:, 1:2]
    wants = jnp.where((lane == first) | (lane == second + 64), 1.0, 0.0)
    count = mm(jnp.where(ahead, 1.0, 0.0).astype(BF16), wants.astype(BF16))
    total = jnp.sum(wants, axis=0, keepdims=True)
    rank_one = jnp.sum(jnp.where(lane == first, count, 0.0), axis=1, keepdims=True)
    rank_two = jnp.sum(
        jnp.where(lane == second + 64, count, 0.0) + jnp.where(lane == second, total, 0.0),
        axis=1,
        keepdims=True,
    )
    slot_one = jnp.where(rank_one < capacity, first.astype(F32) * padded + rank_one, -1.0)
    slot_two = jnp.where(rank_two < capacity, second.astype(F32) * padded + rank_two, -1.0)
    return slot_one, slot_two


def batch_of(experts, padded):
    best = 1
    for count in range(1, experts + 1):
        if experts % count == 0 and count * padded <= 256 and (count * padded) % 16 == 0:
            best = count
    return best


def spread_stage(values_ref, slots_ref, target_ref, extra=None):
    rows, width = values_ref.shape
    experts, padded = target_ref.shape[0], target_ref.shape[1]
    batch = batch_of(experts, padded)

    def step(index, _):
        slots = slots_ref[...].astype(F32)
        one, two = [row_of(slots[:, k : k + 1], rows).astype(jnp.int32) for k in range(2)]
        start = index * batch
        here = iota((batch * padded, rows), 0) + start * padded
        pick = jnp.where((here == one) | (here == two), 1.0, 0.0).astype(BF16)
        block = mm(pick, values_ref[...]).reshape(batch, padded, width)
        if extra is not None:
            block = jnp.stack([extra(start + inner, block[inner]) for inner in range(batch)])
        target_ref[pl.ds(start, batch)] = block.astype(BF16)
        return 0

    lax.fori_loop(0, experts // batch, step, 0)


def with_rows(block, first_row, rows):
    place = iota(block.shape, 0)
    for step, row in enumerate(rows):
        wide = jnp.concatenate([row, jnp.zeros((1, block.shape[1] - row.shape[1]), F32)], axis=1)
        block = jnp.where(place == first_row + step, wide, block)
    return block


def pieces(value, count):
    parts = []
    for _ in range(count):
        part = value.astype(BF16).astype(F32)
        parts.append(part)
        value = value - part
    return parts


def bias_stage(lengths_ref, m, rows, store):
    own_start = lax.axis_index("seq") * rows
    span = lax.axis_size("seq") * rows
    ends = []
    total = 0
    for step in range(lengths_ref.shape[1]):
        total = total + lengths_ref[m, step]
        ends.append(total)

    def documents(place):
        found = jnp.zeros(place.shape, jnp.int32)
        for end in ends:
            found = found + jnp.where(place >= end, 1, 0)
        return found

    asked = documents(iota((1, rows), 1) + own_start)
    for half in range(2):
        start = own_start if half == 0 else span - rows - own_start
        held = documents(iota((rows, 1), 0) + start)
        store(half, jnp.where(held == asked, 0.0, -1e30))


def gates_of(logits, routes):
    lane = iota(logits.shape, 1)
    chosen = [
        jnp.sum(jnp.where(lane == routes[:, k : k + 1] + ROUTER_ROW, logits, 0.0), axis=1, keepdims=True)
        for k in range(2)
    ]
    peak = jnp.maximum(*chosen)
    raised = [jnp.exp(part - peak) for part in chosen]
    total = raised[0] + raised[1]
    return raised[0] / total, raised[1] / total


def phi_terms(hidden):
    size = jnp.abs(hidden)
    bell = jnp.exp(hidden * hidden * -0.5)
    t = 1.0 / (1.0 + 0.23164188828 * size)
    tail = t * (
        0.127414796
        + t * (-0.142248368 + t * (0.7107068705 + t * (-0.7265760135 + t * 0.5307027145)))
    )
    tail = tail * bell
    return jnp.where(hidden >= 0, 1.0 - tail, tail), bell


def gather_stage(blocks_ref, slots, weights, padded):
    experts, _, width = blocks_ref.shape
    rows = slots.shape[0]
    batch = batch_of(experts, padded)
    place = iota((rows, batch * padded), 1)
    totals = [jnp.zeros((rows, width), F32) for _ in weights]
    for start in range(0, experts, batch):
        block = (
            blocks_ref[start : start + batch].astype(F32).reshape(batch * padded, width).astype(BF16)
        )
        here = place + start * padded
        for index, chosen in enumerate(weights):
            hit = slots[:, chosen[0] : chosen[0] + 1] == here
            for k in chosen[1:]:
                hit = hit | (slots[:, k : k + 1] == here)
            totals[index] = totals[index] + mm(jnp.where(hit, 1.0, 0.0).astype(BF16), block)
    return totals


MESH = pl.DeviceIdType.MESH
ANY = pl.BlockSpec(memory_space=pl.ANY)

def remote(source, target, sends, arrives, device):
    return pltpu.make_async_remote_copy(
        src_ref=source,
        dst_ref=target,
        send_sem=sends,
        recv_sem=arrives,
        device_id=device,
        device_id_type=MESH,
    )


def greet(axes):
    barrier = pltpu.get_barrier_semaphore()
    count = 0
    for axis in axes:
        size, me = lax.axis_size(axis), lax.axis_index(axis)
        for step in range(1, size):
            pl.semaphore_signal(
                barrier, inc=1, device_id={axis: lax.rem(me + step, size)}, device_id_type=MESH
            )
            count += 1
    pl.semaphore_wait(barrier, count)


class Exchange:
    def __init__(self, source, target, sems, index):
        self.refs, self.index = (source, target, sems), index

    def copies(self):
        source, target, sems = self.refs
        size, me = lax.axis_size("exp"), lax.axis_index("exp")
        found = []
        for step in range(1, size):
            peer = lax.rem(me + step, size)
            found.append(
                remote(
                    source.at[peer],
                    target.at[me],
                    sems.at[self.index, 0, step],
                    sems.at[self.index, 1, step],
                    {"exp": peer},
                )
            )
        return found

    def own(self):
        source, target, sems = self.refs
        me = lax.axis_index("exp")
        return pltpu.make_async_copy(source.at[me], target.at[me], sems.at[self.index, 0, 0])

    def start(self):
        for copy in self.copies():
            copy.start()
        self.own().start()

    def arrived(self):
        for copy in self.copies():
            copy.wait_recv()
        self.own().wait()

    def sent(self):
        for copy in self.copies():
            copy.wait_send()


def project(low, weight_ref, parts, store):
    width = low.shape[1]
    for part in parts:
        block = mm(low, weight_ref[:, part * width : (part + 1) * width]).astype(BF16)
        for index in range(width // 128):
            store(part, index, block[:, index * 128 : (index + 1) * 128])


def attend_stage(query_ref, pair_ref, bias_ref, attended_ref, stats_ref):
    couples, rows, couple = query_ref.shape
    head_dim = couple // 2
    low_lane = iota((1, couple), 1) < head_dim

    def step(index, _):
        query = query_ref[index].astype(F32) * head_dim**-0.5
        keys = [pair_ref[half, 2 * index] for half in range(2)]
        values = [pair_ref[half, 2 * index + 1].astype(F32).T.astype(BF16) for half in range(2)]
        outs = []
        for head in range(2):
            mine = jnp.where(low_lane == (head == 0), query, 0.0).astype(BF16)
            scores = [mm_nt(keys[half], mine) + bias_ref[half] for half in range(2)]
            peak = jnp.maximum(*[jnp.max(part, axis=0, keepdims=True) for part in scores])
            raised = [jnp.exp(part - peak) for part in scores]
            total = sum(jnp.sum(part, axis=0, keepdims=True) for part in raised)
            here = slice(head * head_dim, (head + 1) * head_dim)
            summed = sum(mm(values[half][here], raised[half].astype(BF16)) for half in range(2))
            outs.append(summed / total)
            stats_ref[pl.ds(index * 2 + head, 1), :] = peak + jnp.log(total)
        lanes = pl.ds(pl.multiple_of(index * couple, couple), couple)
        attended_ref[:, lanes] = jnp.concatenate(outs, axis=0).T.astype(BF16)
        return 0

    lax.fori_loop(0, couples, step, 0)


def flatten_stage(rows_ref, cot_ref, x, g, capacity):
    experts, padded, width = rows_ref.shape
    batch = batch_of(experts, padded)
    flat = batch * padded

    def step(index, _):
        place, lane = iota((padded, 128), 0), iota((padded, 128), 1)
        inside = (place == capacity) | (place == capacity + 1)
        block = rows_ref[pl.ds(index * batch, batch)].astype(F32)
        cot = cot_ref[pl.ds(index * batch, batch)].astype(F32)
        here = pl.ds(pl.multiple_of(index * flat, 16), flat)
        x[here, :] = block.reshape(flat, width).astype(BF16)
        scaled = []
        for inner in range(batch):
            gate_row = jnp.sum(jnp.where(inside, block[inner][:, 0:128], 0.0), axis=0, keepdims=True)
            gate = jnp.sum(jnp.where(place == lane, gate_row, 0.0), axis=1, keepdims=True)
            scaled.append(cot[inner] * gate)
        g[here, :] = jnp.stack(scaled).reshape(flat, width).astype(BF16)
        return 0

    lax.fori_loop(0, experts // batch, step, 0)


def expert_step(x, g, y, dx, up, down):
    hidden = mm(x[...], up)
    active_grad = mm_nt(g[...], down)
    phi, bell = phi_terms(hidden)
    active = (hidden * phi).astype(BF16)
    hidden_grad = (active_grad * (phi + hidden * bell * 0.3989422804)).astype(BF16)
    y[...] += mm(active, down)
    dx[...] += mm_nt(hidden_grad, up)
    return active, hidden_grad


def finish_stage(cot_ref, y, dx, back_ref, grads_ref, capacity):
    experts, padded, width = cot_ref.shape
    batch = batch_of(experts, padded)
    flat = batch * padded

    def step(index, _):
        place, lane = iota((padded, 128), 0), iota((padded, 128), 1)
        here = pl.ds(pl.multiple_of(index * flat, 16), flat)
        there = pl.ds(index * batch, batch)
        produced = y[here, :].reshape(batch, padded, width).astype(BF16)
        back_ref[there] = produced
        cot = cot_ref[there].astype(F32)
        along = jnp.sum(cot * produced.astype(F32), axis=-1, keepdims=True)
        grads = dx[here, :].reshape(batch, padded, width)
        parts = []
        for inner in range(batch):
            row = jnp.sum(jnp.where(place == lane, along[inner], 0.0), axis=0, keepdims=True)
            parts.append(with_rows(grads[inner], capacity, pieces(row, 3)))
        grads_ref[there] = jnp.stack(parts).astype(BF16)
        return 0

    lax.fori_loop(0, experts // batch, step, 0)


class Backward:
    def __init__(self, m, fresh, capacity, padded, **refs):
        self.m, self.fresh, self.capacity, self.padded = m, fresh, capacity, padded
        self.__dict__.update(refs)

    def gain(self, row):
        return self.pack[row : row + 1].astype(F32)

    def place(self, index):
        third = self.tokens.shape[1] // 2
        return slice(index * third, (index + 1) * third)

    def past(self, index):
        return pltpu.make_async_copy(
            self.dense.at[:, :, :, self.place(index)], self.stage.at[index % 2], self.save_sems.at[index % 2]
        )

    def save(self, index):
        return pltpu.make_async_copy(
            self.stage.at[index % 2], self.dense.at[:, :, :, self.place(index)], self.save_sems.at[index % 2]
        )

    def keep(self, index):
        return pltpu.make_async_copy(
            self.stage.at[index % 2, lax.axis_index("dp")],
            self.kept.at[:, :, self.place(index)],
            self.save_sems.at[2 + index % 2],
        )

    def give(self, index):
        return remote(
            self.low_stage.at[index % 2],
            self.got.at[:, :, self.place(index)],
            self.give_sems.at[index, 0],
            self.give_sems.at[index, 1],
            {"dp": 1 - lax.axis_index("dp")},
        )

    def store(self, start, value):
        third = self.tokens.shape[1] // 2
        for index in range(value.shape[1] // third):
            self.store_piece(start // third + index, value[:, index * third : (index + 1) * third])

    def store_piece(self, index, value):
        slot = index % 2
        value = value.reshape(2, 16, value.shape[0] // 32, value.shape[1])
        if self.fresh:
            if index >= 2:
                self.save(index - 2).wait()
            self.stage[slot] = value
            self.save(index).start()
            return
        self.past(index).wait()
        self.stage[slot] = self.stage[slot] + value
        self.keep(index).start()
        if index >= 2:
            self.give(index - 2).wait_send()
        self.low_stage[slot] = self.stage[slot, 1 - lax.axis_index("dp")].astype(BF16)
        self.give(index).start()
        if index + 1 < 8:
            if index >= 1:
                self.keep(index - 1).wait()
            self.past(index + 1).start()

    def drain(self):
        for index in (6, 7):
            if self.fresh:
                self.save(index).wait()
            else:
                self.keep(index).wait()
                self.give(index).wait_send()

    def before(self):
        grads, capacity, padded = self.grads, self.capacity, self.padded
        rows = self.tokens.shape[0]
        couples, _, couple = self.query.shape

        def store_bias(half, block):
            self.bias[half] = block

        bias_stage(self.lengths, self.m, rows, store_bias)
        slots, gates = self.slots[...], self.gates[...]
        routes = slots[:, 2:4]
        pack = self.pack[...]
        batch = batch_of(grads.shape[0], padded)
        flat = batch * padded
        place, lane = iota((padded, 128), 0), iota((padded, 128), 1)
        inside = (place >= capacity) & (place < capacity + 3)
        wide_lane, here = iota((flat, 128), 1), iota((rows, flat), 1)
        moe_grad = 0.0
        found = [0.0, 0.0]
        for start in range(0, grads.shape[0], batch):
            block = grads[start : start + batch].astype(F32)
            columns = []
            for inner in range(batch):
                row = jnp.sum(
                    jnp.where(inside, block[inner][:, 0:128], 0.0), axis=0, keepdims=True
                )
                columns.append(
                    jnp.sum(jnp.where(place == lane, row, 0.0), axis=1, keepdims=True)
                )
            column = jnp.stack(columns).reshape(flat, 1)
            spread = 0.0
            for index, piece in enumerate(pieces(column, 3)):
                spread = spread + jnp.where(wide_lane == index, piece, 0.0)
            spread = spread.astype(BF16)
            hits = [slots[:, k : k + 1] - start * padded == here for k in range(2)]
            for k in range(2):
                found[k] = found[k] + mm(jnp.where(hits[k], 1.0, 0.0).astype(BF16), spread)
            pick = jnp.where(hits[0] | hits[1], 1.0, 0.0).astype(BF16)
            moe_grad = moe_grad + mm(pick, block.reshape(flat, block.shape[2]).astype(BF16))
        gate_grad = [jnp.sum(part, axis=1, keepdims=True) for part in found]
        gate = [gates[:, k : k + 1] for k in range(2)]
        inner = gate[0] * gate_grad[0] + gate[1] * gate_grad[1]
        pack_lane = iota((rows, pack.shape[0]), 1)
        logit_grad = sum(
            jnp.where(
                pack_lane == routes[:, k : k + 1] + ROUTER_ROW,
                gate[k] * (gate_grad[k] - inner),
                0.0,
            )
            for k in range(2)
        )
        parts = [part.astype(BF16) for part in pieces(logit_grad, 3)]
        moe_grad = moe_grad + sum(mm(part, pack) for part in parts)
        router_grad = sum(mm_tn(part, self.moe[...]) for part in parts)
        xhat, scale = normalise(self.residual[...])
        small_row = iota(router_grad.shape, 0)
        terms = jnp.where(
            small_row == 2,
            jnp.sum(moe_grad * xhat, axis=0, keepdims=True),
            jnp.where(small_row == 3, jnp.sum(moe_grad, axis=0, keepdims=True), router_grad),
        )
        self.small[...] = terms if self.fresh else self.small[...] + terms
        total = self.cot[...].astype(F32) + norm_backward(moe_grad, self.gain(2), xhat, scale)
        self.residual_grad[...] = total
        branch = total.astype(BF16)
        self.store(0, mm_tn(self.attended[...], branch))
        turned = mm_nt(branch, self.wo[...]).astype(BF16)
        for index in range(couples):
            self.attended_grad[index] = turned[:, index * couple : (index + 1) * couple]
        for half, ref in enumerate((self.tokens, self.token_other)):
            self.low[half * rows : (half + 1) * rows] = (
                normalise(ref[...].astype(F32))[0] * self.gain(0) + self.gain(1)
            ).astype(BF16)

    def heads(self, begin, end):
        rows, width = self.tokens.shape
        couple = self.query.shape[2]
        head_dim = couple // 2
        low_lane = iota((1, couple), 1) < head_dim
        query, pair, bias, packed = self.query, self.pair, self.bias, self.packed

        def step(index, _):
            asked = query[index].astype(F32) * head_dim**-0.5
            grad_low = self.attended_grad[index]
            grad = grad_low.astype(F32)
            asked_low = asked.astype(BF16)
            keys = [pair[half, 2 * index] for half in range(2)]
            values = [pair[half, 2 * index + 1] for half in range(2)]
            keys_turned = [part.astype(F32).T.astype(BF16) for part in keys]
            key_grads, value_grads, query_grads = [[], []], [[], []], []
            for head in range(2):
                chosen = low_lane == (head == 0)
                mine = jnp.where(chosen, asked, 0.0).astype(BF16)
                mine_grad = jnp.where(chosen, grad, 0.0).astype(BF16)
                stats = self.stats[pl.ds(index * 2 + head, 1), :]
                weighting = [
                    jnp.exp(mm_nt(keys[half], mine) + bias[half] - stats) for half in range(2)
                ]
                weighting_grad = [mm_nt(values[half], mine_grad) for half in range(2)]
                delta = sum(
                    jnp.sum(weighting[half] * weighting_grad[half], axis=0, keepdims=True)
                    for half in range(2)
                )
                here = slice(head * head_dim, (head + 1) * head_dim)
                query_total = 0.0
                for half in range(2):
                    scores_grad = (weighting[half] * (weighting_grad[half] - delta)).astype(BF16)
                    value_grads[half].append(mm(weighting[half].astype(BF16), grad_low))
                    key_grads[half].append(mm(scores_grad, asked_low))
                    query_total = query_total + mm(keys_turned[half][here], scores_grad)
                query_grads.append(query_total * head_dim**-0.5)

            def lanes(part):
                return pl.ds(pl.multiple_of(part * width + index * couple, couple), couple)

            packed[0:rows, lanes(0)] = jnp.concatenate(query_grads, axis=0).T.astype(BF16)
            for half in range(2):
                here = slice(half * rows, (half + 1) * rows)
                packed[here, lanes(1)] = jnp.where(low_lane, *key_grads[half]).astype(BF16)
                packed[here, lanes(2)] = jnp.where(low_lane, *value_grads[half]).astype(BF16)
            return 0

        lax.fori_loop(begin, end, step, 0)

    def project_grads(self, group):
        rows, width = self.tokens.shape
        third = width // 2
        for part in range(3):
            tall = rows if part == 0 else 2 * rows
            source = slice(part * width + group * third, part * width + (group + 1) * third)
            value = mm_tn(self.low[0:tall], self.packed[0:tall, source])
            self.store(width + (3 * group + part) * third, value)

    def firsts(self):
        rows, width = self.tokens.shape
        packed, wi = self.packed, self.wi
        own = mm_nt(packed[0:rows, 0:width], wi[:, 0:width])
        other = 0.0
        for part in range(1, 3):
            here = slice(part * width, (part + 1) * width)
            own = own + mm_nt(packed[0:rows, here], wi[:, here])
            other = other + mm_nt(packed[rows:, here], wi[:, here])
        self.other_grad[...] = other.astype(BF16)
        self.first_grad[...] = own
        own_hat = normalise(self.tokens[...].astype(F32))[0]
        other_hat = normalise(self.token_other[...].astype(F32))[0]
        gain_grad = jnp.sum(own * own_hat + other * other_hat, axis=0, keepdims=True)
        shift_grad = jnp.sum(own + other, axis=0, keepdims=True)
        row = iota(self.small.shape, 0)
        self.small[...] = self.small[...] + jnp.where(
            row == 0, gain_grad, jnp.where(row == 1, shift_grad, 0.0)
        )


def forward_kernel(
    capacity,
    tokens_ref,
    cot_ref,
    routes_ref,
    priority_ref,
    norms_ref,
    router_ref,
    lengths_ref,
    in_own,
    out_own,
    up_own,
    down_own,
    pack_out,
    in_out,
    out_out,
    in_half,
    out_half,
    token_out,
    query_out,
    pair_out,
    residual_out,
    moe_out,
    attended_out,
    stats_out,
    gates_out,
    slots_out,
    back_got,
    grads_out,
    up_old,
    down_old,
    up_sum,
    down_sum,
    up_arrived,
    down_arrived,
    small_out,
    residual_grad_out,
    first_grad_out,
    other_grad_out,
    dense_out,
    kept_out,
    core_got_out,
    pk,
    up,
    down,
    token_other,
    cot_send,
    row_send,
    cot_got,
    row_got,
    up_got,
    down_got,
    all_sems,
    weight_sems,
    token_sems,
    out_sems,
    chunk_sems,
    past_sems,
    low_sems,
    got_sems,
    cross_sems,
    load_sems,
    save_sems,
    give_sems,
):
    micro_count, rows, width = tokens_ref.shape
    experts, padded = cot_send.shape[1], cot_send.shape[2]
    flat = experts * padded
    core, half_seq = lax.axis_index("dp"), lax.axis_index("seq")
    partner = {"dp": 1 - core}
    across = {"seq": 1 - half_seq}
    half_width = width // 2
    rest_rows = pk.shape[1] - ROUTER_ROW - experts
    pk[core] = jnp.concatenate(
        [
            norms_ref[...].astype(F32),
            jnp.zeros((ROUTER_ROW - 4, half_width), F32),
            router_ref[...].astype(F32),
        ]
        + ([jnp.zeros((rest_rows, half_width), F32)] if rest_rows else []),
        axis=0,
    ).astype(BF16)
    greet(("seq", "exp", "dp"))

    token_copies = [
        remote(
            tokens_ref.at[m], token_other.at[m], token_sems.at[m, 0], token_sems.at[m, 1], across
        )
        for m in range(micro_count)
    ]
    weights = []
    for index, (own, full) in enumerate(
        ((pk.at[core], pk), (in_own, in_half), (out_own, out_half), (up_own, up), (down_own, down))
    ):
        size = own.shape[0]
        whole_there = index in (1, 2)
        place = full.at[core] if index == 0 else full.at[pl.ds(core * size, size)]
        weights.append(
            (
                remote(
                    own,
                    full if whole_there else place,
                    weight_sems.at[index, 0],
                    weight_sems.at[index, 1],
                    partner,
                ),
                None if index < 3 else pltpu.make_async_copy(own, place, weight_sems.at[index, 2]),
            )
        )
    token_copies[0].start()
    for index in range(3):
        weights[index][0].start()
    token_copies[1].start()
    for index in range(3, 5):
        weights[index][0].start()
        weights[index][1].start()

    def have(index):
        weights[index][0].wait_recv()
        if weights[index][1] is not None:
            weights[index][1].wait()

    cots = [Exchange(cot_send.at[m], cot_got.at[m], all_sems, m) for m in range(micro_count)]
    rowses = [Exchange(row_send.at[m], row_got.at[m], all_sems, 2 + m) for m in range(micro_count)]
    gradses = [Exchange(cot_send.at[m], grads_out.at[m], all_sems, 4 + m) for m in range(micro_count)]
    backs = [Exchange(row_send.at[m], back_got.at[m], all_sems, 6 + m) for m in range(micro_count)]
    lane_two, lane_four = iota((rows, 2), 1), iota((rows, 4), 1)

    def claim(m):
        one, two = assign_stage(routes_ref[m], priority_ref[m], capacity, padded)
        routes = routes_ref[m]
        found = jnp.where(lane_four == 0, one, two).astype(jnp.int32)
        chosen = jnp.where(lane_four == 2, routes[:, 0:1], routes[:, 1:2])
        slots_out[m] = jnp.where(lane_four < 2, found, chosen)
        spread_stage(cot_ref.at[m], slots_out.at[m], cot_send.at[m])

    used = [0]

    def keep(refs, later):
        index = used[0]
        used[0] += 1

        def copy():
            source, target = refs()
            return pltpu.make_async_copy(source, target, out_sems.at[index])

        copy().start()
        later.append(copy)

    late = []
    claim(0)
    cots[0].start()
    have(0)
    pack_out[...] = jnp.concatenate([pk[0], pk[1]], axis=1)

    def gain(row):
        return pack_out[row : row + 1].astype(F32)

    def first_norm(values):
        return (normalise(values.astype(F32))[0] * gain(0) + gain(1)).astype(BF16)

    def attention_phase(query, pair, bias, residual, moe, attended, wi, wo):
        half = width // 2
        weight_loads = []
        for index, (own, got, full) in enumerate(((in_own, in_half, wi), (out_own, out_half, wo))):
            mine, theirs = [full.at[pl.ds(place * half, half)] for place in (core, 1 - core)]
            weight_loads.append(
                (
                    pltpu.make_async_copy(own, mine, load_sems.at[2 * index]),
                    pltpu.make_async_copy(got, theirs, load_sems.at[2 * index + 1]),
                )
            )
            weight_loads[index][0].start()

        def project_own(m):
            def store(part, index, block):
                if part == 0:
                    query[m, index] = block
                else:
                    pair[m, 0, 2 * index + part - 1] = block

            project(first_norm(tokens_ref[m]), wi, range(3), store)

        def project_other(m):
            def store(part, index, block):
                pair[m, 1, 2 * index + part - 1] = block

            project(first_norm(token_other[m]), wi, range(1, 3), store)

        have(1)
        weight_loads[0][1].start()
        weight_loads[0][1].wait()
        weight_loads[0][0].wait()
        for m in range(micro_count):
            project_own(m)
        claim(1)
        have(2)
        weight_loads[1][1].start()
        weight_loads[1][1].wait()
        weight_loads[1][0].wait()
        outs, local = [], []
        keep(lambda: (wi, in_out), outs)
        keep(lambda: (wo, out_out), outs)
        for m in range(micro_count):
            token_copies[m].wait_recv()
            project_other(m)
            keep(lambda m=m: (token_other.at[m], token_out.at[m]), late)
            keep(lambda m=m: (query.at[m], query_out.at[m]), outs)
            keep(lambda m=m: (pair.at[m], pair_out.at[m]), outs)

            def store_bias(half, block):
                bias[half] = block

            bias_stage(lengths_ref, m, rows, store_bias)
            for copy in local:
                copy().wait()
            attend_stage(query.at[m], pair.at[m], bias, attended, stats_out.at[m])
            summed = tokens_ref[m].astype(F32) + mm(attended[...], wo[...])
            residual[...] = summed
            moe_input = (normalise(summed)[0] * gain(2) + gain(3)).astype(BF16)
            moe[...] = moe_input
            gates = gates_of(mm_nt(moe_input, pack_out[...]), routes_ref[m])
            gates_out[m] = jnp.where(lane_two == 0, gates[0], gates[1])

            def gate_rows(expert, block):
                slots, gates = slots_out[m], gates_out[m]
                place = iota((rows, 128), 1)
                row = sum(
                    jnp.where(
                        slots[:, k : k + 1] - expert * padded == place, gates[:, k : k + 1], 0.0
                    )
                    for k in range(2)
                )
                return with_rows(block, capacity, pieces(jnp.sum(row, axis=0, keepdims=True), 2))

            spread_stage(moe, slots_out.at[m], row_send.at[m], gate_rows)
            rowses[m].start()
            if m == 0:
                cots[1].start()
            local = []
            keep(lambda m=m: (residual, residual_out.at[m]), local)
            keep(lambda m=m: (moe, moe_out.at[m]), local)
            keep(lambda m=m: (attended, attended_out.at[m]), local)
        for copy in outs + local:
            copy().wait()

    pl.run_scoped(
        attention_phase,
        pltpu.VMEM((micro_count, width // 128, rows, 128), BF16),
        pltpu.VMEM((micro_count, 2, width // 64, rows, 128), BF16),
        pltpu.VMEM((2, rows, rows), F32),
        pltpu.VMEM((rows, width), F32),
        pltpu.VMEM((rows, width), BF16),
        pltpu.VMEM((rows, width), BF16),
        pltpu.VMEM((width, 3 * width), BF16),
        pltpu.VMEM((width, width), BF16),
    )
    have(3)
    have(4)
    chunks, _, chunk = up_old.shape
    half_chunks = chunks // 2
    half_rows = width // 2

    def span(i):
        return pl.ds(pl.multiple_of(i * chunk, chunk), chunk)

    def own_columns():
        return pl.ds(pl.multiple_of(core * half_rows, 128), half_rows)

    def other_columns():
        return pl.ds(pl.multiple_of((1 - core) * half_rows, 128), half_rows)

    def mine(i):
        return lax.div(i, half_chunks) == core

    def cross(i):
        return remote(
            up_sum.at[:, span(i)],
            up_arrived.at[:, span(i)],
            cross_sems.at[i, 0],
            cross_sems.at[i, 1],
            across,
        )

    early = half_chunks

    def cross_down(i):
        return remote(
            down_sum.at[span(i)],
            down_arrived.at[span(i)],
            cross_sems.at[chunks + i, 0],
            cross_sems.at[chunks + i, 1],
            across,
        )

    def expert_phase(x, g, y, dx):
        def start_expert(m):
            cots[m].arrived()
            rowses[m].arrived()
            flatten_stage(row_got.at[m], cot_got.at[m], x, g, capacity)
            y[...] = jnp.zeros_like(y)
            dx[...] = jnp.zeros_like(dx)

        def end_expert(m):
            cots[m].sent()
            rowses[m].sent()
            finish_stage(cot_got.at[m], y, dx, row_send.at[m], cot_send.at[m], capacity)
            gradses[m].start()
            if m == 0:
                return
            backs[1].start()

        def first_weights(up_buf, down_buf):
            def chunk_out(slot, i):
                return (
                    pltpu.make_async_copy(up_buf.at[slot], up_old.at[i], chunk_sems.at[slot, 0]),
                    pltpu.make_async_copy(down_buf.at[slot], down_old.at[i], chunk_sems.at[slot, 1]),
                )

            def step(i, _):
                slot = lax.rem(i, 2)
                active, hidden = expert_step(x, g, y, dx, up[:, span(i)], down[span(i), :])

                @pl.when(i >= 2)
                def _():
                    for copy in chunk_out(slot, i - 2):
                        copy.wait()

                up_buf[slot] = mm_tn(x[...], hidden)
                down_buf[slot] = mm_tn(active, g[...])
                for copy in chunk_out(slot, i):
                    copy.start()
                return 0

            lax.fori_loop(0, chunks, step, 0)
            end_expert(0)
            for i in range(chunks - 2, chunks):
                for copy in chunk_out(i % 2, i):
                    copy.wait()

        def second_weights(
            up_past, down_past, up_ring, down_ring, up_low, down_low, up_total, down_total
        ):
            def past(slot, i):
                return (
                    pltpu.make_async_copy(up_old.at[i], up_past.at[slot], past_sems.at[slot, 0]),
                    pltpu.make_async_copy(down_old.at[i], down_past.at[slot], past_sems.at[slot, 1]),
                )

            def up_given(i):
                slot = lax.rem(i, 2)
                return remote(
                    up_low.at[slot], up_got.at[i], low_sems.at[slot, 0], got_sems.at[0, i], partner
                )

            def down_given(i):
                slot, place = lax.rem(i, 2), lax.rem(i, half_chunks)
                return remote(
                    down_low.at[slot],
                    down_got.at[place],
                    low_sems.at[slot, 1],
                    got_sems.at[1, place],
                    partner,
                )

            def up_store(i):
                slot = lax.rem(i, 2)
                return pltpu.make_async_copy(
                    up_total.at[slot], up_sum.at[:, span(i)], chunk_sems.at[slot, 0]
                )

            def down_store(i):
                slot = lax.rem(i, 2)
                return pltpu.make_async_copy(
                    down_total.at[slot],
                    down_sum.at[span(lax.rem(i, half_chunks))],
                    chunk_sems.at[slot, 1],
                )

            def crossing(i):
                @pl.when(i >= 3)
                def _():
                    up_store(i - 3).wait()
                    cross(i - 3).start()

                    @pl.when(mine(i - 3))
                    def _():
                        down_store(i - 3).wait()

                        @pl.when(lax.rem(i - 3, half_chunks) < early)
                        def _():
                            cross_down(lax.rem(i - 3, half_chunks)).start()

            def compute(i):
                slot, ring = lax.rem(i, 2), lax.rem(i, 3)

                @pl.when(i + 1 < chunks)
                def _():
                    for copy in past(1 - slot, i + 1):
                        copy.start()

                active, hidden = expert_step(x, g, y, dx, up[:, span(i)], down[span(i), :])

                @pl.when(i >= 2)
                def _():
                    up_given(i - 2).wait_send()

                    @pl.when(jnp.logical_not(mine(i - 2)))
                    def _():
                        down_given(i - 2).wait_send()

                for copy in past(slot, i):
                    copy.wait()
                up_past[slot] = mm_tn(x[...], hidden) + up_past[slot]
                up_low[slot] = up_past[slot, other_columns(), :].astype(BF16)
                up_given(i).start()
                up_ring[ring] = up_past[slot, own_columns(), :]
                down_grad = mm_tn(active, g[...]) + down_past[slot]

                @pl.when(mine(i))
                def _():
                    down_ring[ring] = down_grad

                @pl.when(jnp.logical_not(mine(i)))
                def _():
                    down_low[slot] = down_grad.astype(BF16)
                    down_given(i).start()

            def summing(i):
                slot = lax.rem(i, 2)

                @pl.when((i >= 2) & (i < chunks + 2))
                def _():
                    last = i - 2
                    up_given(last).wait_recv()
                    total = up_ring[lax.rem(last, 3)] + up_got[last].astype(F32)
                    up_total[slot] = total.astype(BF16)
                    up_store(last).start()

                    @pl.when(mine(last))
                    def _():
                        down_given(last).wait_recv()
                        total = down_ring[lax.rem(last, 3)] + down_got[
                            lax.rem(last, half_chunks)
                        ].astype(F32)
                        down_total[slot] = total.astype(BF16)
                        down_store(last).start()

            for copy in past(0, 0):
                copy.start()

            def step(i, _):
                @pl.when(i == half_chunks)
                def _():
                    backs[0].start()

                crossing(i)
                compute(i)
                summing(i)
                return 0

            def rest(i, _):
                crossing(i)
                summing(i)
                return 0

            lax.fori_loop(0, chunks, step, 0)
            end_expert(1)
            lax.fori_loop(chunks, chunks + 3, rest, 0)
            for i in range(chunks - 2, chunks):
                up_given(i).wait_send()

                @pl.when(jnp.logical_not(mine(i)))
                def _():
                    down_given(i).wait_send()

        start_expert(0)
        pl.run_scoped(
            first_weights,
            pltpu.VMEM((2, width, chunk), F32),
            pltpu.VMEM((2, chunk, width), F32),
        )
        start_expert(1)
        pl.run_scoped(
            second_weights,
            pltpu.VMEM((2, width, chunk), F32),
            pltpu.VMEM((2, chunk, width), F32),
            pltpu.VMEM((3, half_rows, chunk), F32),
            pltpu.VMEM((3, chunk, width), F32),
            pltpu.VMEM((2, half_rows, chunk), BF16),
            pltpu.VMEM((2, chunk, width), BF16),
            pltpu.VMEM((2, half_rows, chunk), BF16),
            pltpu.VMEM((2, chunk, width), BF16),
        )

    pl.run_scoped(
        expert_phase,
        pltpu.VMEM((flat, width), BF16),
        pltpu.VMEM((flat, width), BF16),
        pltpu.VMEM((flat, width), F32),
        pltpu.VMEM((flat, width), F32),
    )

    def back_phase(
        grads,
        moe,
        attended,
        query,
        pair,
        residual,
        bias,
        attended_grad,
        packed,
        low,
        residual_grad,
        first_grad,
        other_grad,
        stage,
        low_stage,
        wi,
        wo,
    ):
        def load(index, m):
            source, target = (
                (grads_out, grads),
                (moe_out, moe),
                (attended_out, attended),
                (residual_out, residual),
                (query_out, query),
                (pair_out, pair),
                (in_out, wi),
                (out_out, wo),
            )[index]
            return pltpu.make_async_copy(
                source.at[m] if index < 6 else source, target, load_sems.at[index]
            )

        def saves(m):
            return [
                pltpu.make_async_copy(source, target.at[m], out_sems.at[24 + index])
                for index, (source, target) in enumerate(
                    (
                        (residual_grad, residual_grad_out),
                        (first_grad, first_grad_out),
                        (other_grad, other_grad_out),
                    )
                )
            ]

        def item(m):
            return Backward(
                m,
                m == 0,
                capacity,
                padded,
                pack=pack_out,
                dense=dense_out,
                kept=kept_out,
                got=core_got_out,
                stage=stage,
                low_stage=low_stage,
                save_sems=save_sems,
                give_sems=give_sems,
                grads=grads,
                tokens=tokens_ref.at[m],
                token_other=token_other.at[m],
                query=query,
                pair=pair,
                bias=bias,
                lengths=lengths_ref,
                slots=slots_out.at[m],
                gates=gates_out.at[m],
                moe=moe,
                residual=residual,
                small=small_out,
                cot=cot_ref.at[m],
                residual_grad=residual_grad,
                attended=attended,
                attended_grad=attended_grad,
                wo=wo,
                wi=wi,
                low=low,
                packed=packed,
                stats=stats_out.at[m],
                first_grad=first_grad,
                other_grad=other_grad,
            )

        for index in range(1, 8):
            load(index, 0).start()
        for m in range(micro_count):
            work = item(m)
            gradses[m].arrived()
            load(0, m).start()
            if m > 0:
                for copy in saves(m - 1):
                    copy.wait()
                work.past(0).start()
            for index in range(8 if m == 0 else 6):
                load(index, m).wait()
            work.before()
            if m + 1 < micro_count:
                for index in range(1, 4):
                    load(index, m + 1).start()
            work.heads(0, query.shape[0])
            if m + 1 < micro_count:
                for index in range(4, 6):
                    load(index, m + 1).start()
            work.project_grads(0)
            work.project_grads(1)
            work.firsts()
            for copy in saves(m):
                copy.start()
            work.drain()
        for copy in saves(micro_count - 1):
            copy.wait()
        for index in range(8):
            item(1).give(index).wait_recv()

    pl.run_scoped(
        back_phase,
        pltpu.VMEM((experts, padded, width), BF16),
        pltpu.VMEM((rows, width), BF16),
        pltpu.VMEM((rows, width), BF16),
        pltpu.VMEM((width // 128, rows, 128), BF16),
        pltpu.VMEM((2, width // 64, rows, 128), BF16),
        pltpu.VMEM((rows, width), F32),
        pltpu.VMEM((2, rows, rows), F32),
        pltpu.VMEM((width // 128, rows, 128), BF16),
        pltpu.VMEM((2 * rows, 3 * width), BF16),
        pltpu.VMEM((2 * rows, width), BF16),
        pltpu.VMEM((rows, width), F32),
        pltpu.VMEM((rows, width), F32),
        pltpu.VMEM((rows, width), BF16),
        pltpu.VMEM((2, 2, 16, width // 32, width // 2), F32),
        pltpu.VMEM((2, 16, width // 32, width // 2), BF16),
        pltpu.VMEM((width, 3 * width), BF16),
        pltpu.VMEM((width, width), BF16),
    )
    for m in range(micro_count):
        backs[m].arrived()
        backs[m].sent()
        token_copies[m].wait_send()
        gradses[m].sent()
    for index in range(5):
        weights[index][0].wait_send()
    for copy in late:
        copy().wait()

    def crossed(i, _):
        cross(i).wait()
        return 0

    lax.fori_loop(0, chunks, crossed, 0)

    def crossed_down(i, _):
        cross_down(i).wait()
        return 0

    lax.fori_loop(0, early, crossed_down, 0)


class Reduction:
    def __init__(self, index, columns, seq_first, refs):
        self.acc, self.give, self.land, self.give2, self.land2, self.give3, self.land3 = refs[:7]
        self.more_give, self.more_land, self.final, self.sems = refs[7:]
        self.index, self.cols = index, columns
        size, me = lax.axis_size("exp"), lax.axis_index("exp")
        self.size, self.me = size, me
        seq, low = lax.axis_index("seq"), lax.rem(me, 2)
        flip = {"exp": me + 1 - 2 * low}
        across = {"seq": 1 - seq}
        self.first, self.second = (seq, low) if seq_first else (low, seq)
        self.to_first, self.to_second = (across, flip) if seq_first else (flip, across)
        self.turn = lax.rem(lax.div(me, 2), 4)
        self.quad = self.first * 8 + self.second * 4

    def peer(self, step):
        turn = lax.rem(self.turn + step, 4)
        return turn, {"exp": self.me + 2 * (turn - self.turn)}

    def copy(self, step, source, target, device):
        return remote(
            source, target, self.sems.at[self.index, step, 0], self.sems.at[self.index, step, 1], device
        )

    def one(self):
        return self.copy(0, self.give.at[:, :, self.cols], self.land.at[:, :, self.cols], self.to_first)

    def two(self):
        return self.copy(1, self.give2.at[:, :, self.cols], self.land2.at[:, :, self.cols], self.to_second)

    def three(self, step):
        turn, device = self.peer(step)
        return self.copy(
            1 + step, self.give3.at[turn, :, self.cols], self.land3.at[self.turn, :, self.cols], device
        )

    def more(self, step):
        block = 8 << step
        device = {"exp": self.me + block * (1 - 2 * lax.rem(lax.div(self.me, block), 2))}
        return self.copy(
            10 + step, self.more_give.at[step, :, self.cols], self.more_land.at[step, :, self.cols], device
        )

    def four(self, step):
        place = self.final.at[self.quad + self.turn, :, self.cols]
        return self.copy(4 + step, place, place, self.peer(step)[1])

    def five(self):
        place = self.final.at[pl.ds(self.quad, 4), :, self.cols]
        return self.copy(8, place, place, self.to_second)

    def six(self):
        place = self.final.at[pl.ds(self.first * 8, 8), :, self.cols]
        return self.copy(9, place, place, self.to_first)

    def start_one(self):
        self.give[:, :, self.cols] = self.acc[pl.ds((1 - self.first) * 8, 8), :, self.cols].astype(BF16)
        self.one().start()

    def start_two(self):
        self.one().wait_recv()
        mine = pl.ds(self.first * 8, 8)
        self.acc[mine, :, self.cols] = self.acc[mine, :, self.cols] + self.land[
            :, :, self.cols
        ].astype(F32)
        self.give2[:, :, self.cols] = self.acc[
            pl.ds(self.first * 8 + (1 - self.second) * 4, 4), :, self.cols
        ].astype(BF16)
        self.two().start()

    def start_three(self):
        self.two().wait_recv()
        total = self.acc[pl.ds(self.quad, 4), :, self.cols] + self.land2[:, :, self.cols].astype(F32)
        self.acc[pl.ds(self.quad, 4), :, self.cols] = total
        self.give3[:, :, self.cols] = total.astype(BF16)
        for step in range(1, 4):
            self.three(step).start()

    def start_four(self):
        total = self.acc[self.quad + self.turn, :, self.cols]
        for step in range(1, 4):
            self.three(step).wait_recv()
        for step in range(1, 4):
            total = total + self.land3[self.peer(step)[0], :, self.cols].astype(F32)
        steps = (self.size // 8).bit_length() - 1
        for step in range(steps):
            low = total.astype(BF16)
            self.more_give[step, :, self.cols] = low
            copy = self.more(step)
            copy.start()
            copy.wait_recv()
            total = low.astype(F32) + self.more_land[step, :, self.cols].astype(F32)
            copy.wait_send()
        self.final[self.quad + self.turn, :, self.cols] = total.astype(BF16)
        for step in range(1, 4):
            self.four(step).start()

    def start_five(self):
        for step in range(1, 4):
            turn, device = self.peer(step)
            place = self.final.at[self.quad + turn, :, self.cols]
            self.copy(4 + 4 - step, place, place, device).wait_recv()
        self.five().start()

    def start_six(self):
        self.five().wait_recv()
        self.six().start()

    def finish(self):
        self.six().wait_recv()
        self.one().wait_send()
        self.two().wait_send()
        for step in range(1, 4):
            self.three(step).wait_send()
            self.four(step).wait_send()
        self.five().wait_send()
        self.six().wait_send()


def sum_kernel(
    slots_ref,
    gates_ref,
    pack_ref,
    small,
    residual_in,
    tokens_in,
    residual_grad_in,
    first_grad_in,
    other_grad,
    kept_in,
    core_got_in,
    back_in,
    mixed_out,
    tokens_out,
    small_out,
    final_out,
    grads,
    other_got,
    acc,
    core_got,
    land,
    land2,
    land3,
    more_give,
    more_land,
    final,
    small_give,
    small_got,
    residual_ref,
    tokens_ref,
    residual_grad,
    first_grad,
    other_first,
    load_sems,
    late_sems,
    other_sems,
    sum_sems,
    small_sems,
):
    micro_count, rows, width = mixed_out.shape
    padded = grads.shape[2]
    core, half_seq = lax.axis_index("dp"), lax.axis_index("seq")
    partner, across = {"dp": 1 - core}, {"seq": 1 - half_seq}
    third = width // 2
    one = micro_count - 1
    group_width = 3 * third
    edges = [(0, width), (width, width + group_width), (width + group_width, 4 * width)]

    def load(group):
        here = slice(*edges[group])
        return (
            pltpu.make_async_copy(kept_in.at[:, :, here], acc.at[:, :, here], load_sems.at[group, 0]),
            pltpu.make_async_copy(
                core_got_in.at[:, :, here], core_got.at[:, :, here], load_sems.at[group, 1]
            ),
        )

    for group in range(3):
        for copy in load(group):
            copy.start()
    late = [
        pltpu.make_async_copy(source, target, late_sems.at[index])
        for index, (source, target) in enumerate(
            (
                (residual_in, residual_ref),
                (tokens_in, tokens_ref),
                (residual_grad_in, residual_grad),
                (first_grad_in, first_grad),
                (back_in.at[0], grads.at[0]),
                (back_in.at[1], grads.at[1]),
            )
        )
    ]
    for copy in late:
        copy.start()
    greet(("seq", "exp", "dp"))

    def other_copy(m):
        return remote(
            other_grad.at[m],
            other_first if m == 0 else other_got,
            other_sems.at[m, 0],
            other_sems.at[m, 1],
            across,
        )

    def lasts(m):
        other_copy(m).wait()
        total = first_grad[m] + (other_first if m == 0 else other_got)[...].astype(F32)
        xhat, scale = normalise(tokens_ref[m].astype(F32))
        back = norm_backward(total, pack_ref[0:1].astype(F32), xhat, scale)
        tokens_out[m] = (residual_grad[m] + back).astype(BF16)

    def mix(m):
        gates = gates_ref[m]
        rows_one, rows_two = gather_stage(grads.at[m], slots_ref[m], ((0,), (1,)), padded)
        chosen = gates[:, 0:1] * rows_one + gates[:, 1:2] * rows_two
        mixed_out[m] = (residual_ref[m] + chosen).astype(BF16)

    sums = []
    for index, (begin, end) in enumerate(edges):
        middle = begin + ((end - begin) // 128 + 1) // 2 * 128
        for part, (start, stop) in enumerate(((begin, middle), (middle, end))):
            sums.append(
                Reduction(
                    2 * index + part,
                    slice(start, stop),
                    part == 0,
                    (
                        acc,
                        core_got.at[pl.ds(0, 8)],
                        land,
                        core_got.at[pl.ds(8, 4)],
                        land2,
                        core_got.at[pl.ds(12, 4)],
                        land3,
                        more_give,
                        more_land,
                        final,
                        sum_sems,
                    ),
                )
            )

    def advance(group, name):
        if name == "one":
            here = slice(*edges[group])
            for copy in load(group):
                copy.wait()
            acc[:, :, here] = acc[:, :, here] + core_got[:, :, here].astype(F32)
        for item in sums[2 * group : 2 * group + 2]:
            getattr(item, "finish" if name == "finish" else "start_" + name)()

    half_width = width // 2

    def small_copy(step):
        size, me = lax.axis_size("exp"), lax.axis_index("exp")
        if step == 0:
            device = partner
        elif step == 1:
            device = across
        else:
            block = 1 << (step - 2)
            device = {"exp": me + block * (1 - 2 * lax.rem(lax.div(me, block), 2))}
        return remote(
            small_give.at[step],
            small_got.at[step],
            small_sems.at[step, 0],
            small_sems.at[step, 1],
            device,
        )

    small_steps = small_give.shape[0]

    def start_small(step):
        if step == 0:
            place = pl.ds(pl.multiple_of((1 - core) * half_width, 128), half_width)
            small_give[0] = small[:, place]
            small_out[...] = small[:, pl.ds(pl.multiple_of(core * half_width, 128), half_width)]
        else:
            small_copy(step - 1).wait_recv()
            small_out[...] = small_out[...] + small_got[step - 1]
            if step == small_steps:
                return
            small_give[step] = small_out[...]
        small_copy(step).start()

    advance(0, "one")
    advance(1, "one")
    start_small(0)
    advance(2, "one")
    advance(0, "two")
    advance(1, "two")
    start_small(1)
    advance(2, "two")
    advance(0, "three")
    for m in range(micro_count):
        other_copy(m).start()
    for copy in late:
        copy.wait()
    mix(0)
    advance(1, "three")
    start_small(2)
    advance(2, "three")
    advance(0, "four")
    lasts(0)
    advance(1, "four")
    start_small(3)
    advance(0, "five")
    advance(2, "four")
    advance(1, "five")
    advance(0, "six")
    lasts(1)
    for step in range(4, small_steps + 1):
        start_small(step)
    advance(2, "five")
    advance(1, "six")
    advance(0, "finish")
    mix(1)
    advance(2, "six")
    advance(1, "finish")
    advance(2, "finish")
    result = pltpu.make_async_copy(final, final_out, load_sems.at[0, 0])
    result.start()
    for step in range(small_steps):
        small_copy(step).wait_send()
    result.wait()


def shape(dims, dtype):
    return jax.ShapeDtypeStruct(dims, dtype)


def body(
    tokens,
    first_gain,
    first_shift,
    attention_in,
    attention_out,
    second_gain,
    second_shift,
    router_weight,
    up_weight,
    down_weight,
    routes,
    priority,
    lengths,
    out_cotangent,
):
    micro_count, _, rows, width = tokens.shape
    experts = lax.axis_size("exp") * up_weight.shape[0]
    hidden = up_weight.shape[2]
    capacity = (210 * rows + 100 * experts - 1) // (100 * experts)
    padded = (capacity + 3 + 7) // 8 * 8
    flat = experts * padded
    core = lax.axis_index("dp")
    chunk = 384 if flat <= 896 else 128
    chunks = hidden // chunk
    couples = width // 128

    pack_rows = (ROUTER_ROW + experts + 15) // 16 * 16
    norms = jnp.concatenate([first_gain, first_shift, second_gain, second_shift])
    norms = norms.reshape(4, width // 2)
    blocks = (micro_count, experts, padded, width)
    token_dims = (micro_count, rows, width)
    dma = pltpu.SemaphoreType.DMA
    tokens, cot = tokens[:, 0], out_cotangent[:, 0]
    routes, lengths = routes[:, 0], lengths[:, 0]
    query_dims = (micro_count, couples, rows, 128)
    pair_dims = (micro_count, 2, 2 * couples, rows, 128)
    outs = (
        (VMEM, (pack_rows, width), BF16),
        (ANY, (width, 3 * width), BF16),
        (ANY, (width, width), BF16),
        (ANY, (width // 2, 3 * width), BF16),
        (ANY, (width // 2, width), BF16),
        (ANY, token_dims, BF16),
        (ANY, query_dims, BF16),
        (ANY, pair_dims, BF16),
        (ANY, token_dims, F32),
        (ANY, token_dims, BF16),
        (ANY, token_dims, BF16),
        (VMEM, (micro_count, 16, rows), F32),
        (VMEM, (micro_count, rows, 2), F32),
        (VMEM, (micro_count, rows, 4), jnp.int32),
        (ANY, blocks, BF16),
        (ANY, blocks, BF16),
        (ANY, (chunks, width, chunk), F32),
        (ANY, (chunks, chunk, width), F32),
        (ANY, (width // 2, hidden), BF16),
        (ANY, (hidden // 2, width), BF16),
        (ANY, (width // 2, hidden), BF16),
        (ANY, (hidden // 2, width), BF16),
        (VMEM, (pack_rows, width), F32),
        (ANY, token_dims, F32),
        (ANY, token_dims, F32),
        (ANY, token_dims, BF16),
        (ANY, (2, 16, width // 32, 4 * width), F32),
        (ANY, (16, width // 32, 4 * width), F32),
        (ANY, (16, width // 32, 4 * width), BF16),
    )
    size = lax.axis_size("exp")
    (
        pack,
        wi,
        wo,
        _,
        _,
        token_other,
        query,
        pair,
        residual,
        moe,
        attended,
        stats,
        gates,
        slots,
        back,
        grads,
        _,
        _,
        up_sum,
        down_sum,
        up_arrived,
        down_arrived,
        small,
        residual_grad,
        first_grad,
        other_grad,
        _,
        kept,
        core_got,
    ) = pl.pallas_call(
        partial(forward_kernel, capacity),
        out_shape=tuple(shape(dims, dtype) for _, dims, dtype in outs),
        in_specs=[VMEM] * 6 + [SMEM] + [ANY] * 4,
        out_specs=tuple(spec for spec, _, _ in outs),
        scratch_shapes=[
            pltpu.VMEM((2, pack_rows, width // 2), BF16),
            pltpu.VMEM((width, hidden), BF16),
            pltpu.VMEM((hidden, width), BF16),
            pltpu.VMEM(token_dims, BF16),
            pltpu.VMEM(blocks, BF16),
            pltpu.VMEM(blocks, BF16),
            pltpu.VMEM(blocks, BF16),
            pltpu.VMEM(blocks, BF16),
            pltpu.VMEM((chunks, width // 2, chunk), BF16),
            pltpu.VMEM((chunks // 2, chunk, width), BF16),
            dma((8, 2, size)),
            dma((5, 3)),
            dma((micro_count, 2)),
            dma((27,)),
            dma((2, 2)),
            dma((2, 2)),
            dma((2, 2)),
            dma((2, chunks)),
            dma((chunks + chunks // 2, 2)),
            dma((8,)),
            dma((4,)),
            dma((8, 2)),
        ],
        compiler_params=pltpu.CompilerParams(
            collective_id=0, has_side_effects=True, vmem_limit_bytes=61 * 2**20
        ),
        cost_estimate=pl.CostEstimate(
            flops=5 * 10**10, bytes_accessed=10**8, transcendentals=10**7
        ),
        name="forward_and_experts",
    )(tokens, cot, routes, priority, norms, router_weight.T, lengths, attention_in, attention_out, up_weight[0], down_weight[0])
    reds = (16, width // 32, 4 * width)
    extra = max((size // 8).bit_length() - 1, 1)
    steps = 2 + size.bit_length() - 1

    def reduced(count):
        return pltpu.VMEM((count,) + reds[1:], BF16)

    outs = (
        (VMEM, token_dims, BF16),
        (VMEM, token_dims, BF16),
        (VMEM, (pack_rows, width // 2), F32),
        (ANY, reds, BF16),
    )
    mixed, tokens_grad, small, final = pl.pallas_call(
        sum_kernel,
        out_shape=tuple(shape(dims, dtype) for _, dims, dtype in outs),
        in_specs=[VMEM] * 4 + [ANY] * 8,
        out_specs=tuple(spec for spec, _, _ in outs),
        scratch_shapes=[
            pltpu.VMEM(blocks, BF16),
            pltpu.VMEM((rows, width), BF16),
            pltpu.VMEM(reds, F32),
            reduced(16),
            reduced(8),
            reduced(4),
            reduced(4),
            reduced(extra),
            reduced(extra),
            reduced(16),
            pltpu.VMEM((steps, pack_rows, width // 2), F32),
            pltpu.VMEM((steps, pack_rows, width // 2), F32),
            pltpu.VMEM(token_dims, F32),
            pltpu.VMEM(token_dims, BF16),
            pltpu.VMEM(token_dims, F32),
            pltpu.VMEM(token_dims, F32),
            pltpu.VMEM((rows, width), BF16),
            dma((3, 2)),
            dma((6,)),
            dma((2, 2)),
            dma((6, 12, 2)),
            dma((steps, 2)),
        ],
        compiler_params=pltpu.CompilerParams(
            collective_id=1, has_side_effects=True, vmem_limit_bytes=58 * 2**20
        ),
        cost_estimate=pl.CostEstimate(
            flops=2 * 10**9, bytes_accessed=3 * 10**7, transcendentals=10**6
        ),
        name="mix_and_sums",
    )(
        slots,
        gates,
        pack,
        small,
        residual,
        tokens,
        residual_grad,
        first_grad,
        other_grad,
        kept,
        core_got,
        back,
    )
    final = final.reshape(width // 2, 4 * width).astype(F32)
    third = width // 2
    in_grad = jnp.concatenate(
        [
            final[:, width + (3 * group + part) * third : width + (3 * group + part + 1) * third]
            for part in range(3)
            for group in range(2)
        ],
        axis=1,
    )
    return (
        mixed[:, None],
        tokens_grad[:, None],
        small[0],
        small[1],
        in_grad,
        final[:, :width],
        small[2],
        small[3],
        small[ROUTER_ROW : ROUTER_ROW + experts].T,
        (up_sum.astype(F32) + up_arrived.astype(F32))[None],
        (down_sum.astype(F32) + down_arrived.astype(F32))[None],
    )


def solution(mesh):
    placed = (
        P(None, ("exp", "dp"), "seq", None),
        P("dp"),
        P("dp"),
        P("dp", None),
        P("dp", None),
        P("dp"),
        P("dp"),
        P("dp", None),
        P("exp", "dp", None),
        P("exp", "dp", None),
        P(None, ("exp", "dp"), "seq", None),
        P(None, ("exp", "dp"), "seq"),
        P(None, ("exp", "dp"), None),
        P(None, ("exp", "dp"), "seq", None),
    )
    return jax.shard_map(
        body,
        mesh=mesh,
        in_specs=placed,
        out_specs=(
            P(None, ("exp", "dp"), "seq", None),
            P(None, ("exp", "dp"), "seq", None),
            P("dp"),
            P("dp"),
            P("dp", None),
            P("dp", None),
            P("dp"),
            P("dp"),
            P("dp", None),
            P("exp", "dp", None),
            P("exp", "dp", None),
        ),
        check_vma=False,
    )
```
